32 devices in a mesh: energy: 8 (over z, x), mom: 4 (over y, core).
Axes of the slice: x: 2, y: 2, z: 4, core: 2. Of those that a mesh axis runs over, the one named last changes fastest.
Arguments:
- green: bfloat16 [4, 16, 16, 2048], P('mom', 'energy'), may hold values from -6 to 6
- coupling: float32 [4, 6, 9, 5, 16], P('mom'), may hold values from -0.12 to 0.12
- gradient: bfloat16 [5, 3, 16, 1024], replicated, may hold values from -1 to 1
- neighbours: int32 [16, 5], replicated, may hold values from 0 to 15, as said below
- offsets: int32 [3], replicated, may hold values from 1 to 4, as said below
Outputs:
- sigma: float32 [16, 16, 2048], P('energy', 'mom')
The draws below stay inside these ranges and needn't reach their ends.
Inputs may be any that keep to these rules, and one draw needn't show every extreme that they name: `neighbours`: each row names 5 different atoms, none of them the row's own atom. `offsets`: one offset is at most 2 and one equals 4.
All inputs are finite; a program needn't handle non-finite values.
Results may differ from the reference program's by a relative error of at most 0.012.
Values may be sent and summed in bfloat16 or wider, within the bound.
No kernel may reach another device: no remote copies, remote signals or barrier semaphores. Data moves between devices by JAX's collectives and lax.ppermute only.
A program may use at most 64 MiB of HBM per device.

```python
import jax
import jax.numpy as jnp
from jax import lax

NO = 32
NB = 5
NW = 3
NA = 16
E_DEV = 2
NE = 16
NK = 4


def draw_neighbours(key, part):
    keys = jax.random.split(jax.random.fold_in(key, 11), NA)
    others = jnp.arange(NA - 1, dtype=jnp.int32)
    orders = jax.vmap(lambda single: jax.random.permutation(single, others))(keys)
    atoms = jnp.arange(NA, dtype=jnp.int32)[:, None]
    return ((atoms + 1 + orders[:, :NB]) % NA).astype(jnp.int32)


def draw_offsets(key, part):
    first, second, third = jax.random.split(jax.random.fold_in(key, 23), 3)
    lower = jax.random.randint(first, (1,), 1, E_DEV + 1, dtype=jnp.int32)
    upper = jnp.full((1,), 2 * E_DEV, jnp.int32)
    others = jax.random.randint(second, (NW - 2,), 1, 2 * E_DEV + 1, dtype=jnp.int32)
    values = jnp.concatenate([lower, upper, others], 0)
    return jax.random.permutation(third, values).astype(jnp.int32)


def levels(rng, extent, cuts, low, high):
    def one(axis_at, blocks):
        steps = jax.random.uniform(jax.random.fold_in(jax.random.fold_in(rng, 6), axis_at), (blocks,), jnp.float32, low / len(cuts), high / len(cuts))
        return jnp.repeat(jnp.exp(steps), extent[axis_at] // blocks).reshape((-1,) + (1,) * (len(extent) - axis_at - 1))

    loudness = one(*cuts[0])
    for cut in cuts[1:]:
        loudness = loudness * one(*cut)
    return loudness


def normal_values(rng, dims, width, most, cuts=(), kind=jnp.bfloat16):
    level = levels(rng, dims, cuts, -0.22, 0.18) if cuts else 1.0
    array = jax.random.normal(rng, dims, jnp.float32) * width * level
    return jnp.minimum(jnp.maximum(array, -most), most).astype(kind)


def setup_inputs(seed: int = 0) -> dict:
    key_of = jax.random.split(jax.random.key(seed), 6)
    green = normal_values(key_of[0], (NK, NE, NA, 2 * NO * NO), 1.0, 6.0, ((0, 4), (1, 8)))
    coupling = normal_values(key_of[1], (NK, 2 * NW, 9, NB, NA), 0.02, 0.12, ((0, 4),), jnp.float32)
    gradient = normal_values(key_of[2], (NB, 3, NA, NO * NO), NO ** -0.5, 1.0)
    neighbours = draw_neighbours(jax.random.fold_in(key_of[5], 71), 0)
    offsets = draw_offsets(jax.random.fold_in(key_of[5], 71), 0)
    return {"green": green, "coupling": coupling, "gradient": gradient, "neighbours": neighbours, "offsets": offsets}


def shifted_stack(window, offsets, count, margin):
    pieces = []
    for phonon in range(NW):
        for direction in (1, -1):
            start = (margin - direction * offsets[phonon]).astype(jnp.int32)
            pieces.append(lax.dynamic_slice_in_dim(window, start, count, 0))
    return jnp.stack(pieces, 0)


def sandwich(shifted, weights, gradient, neighbours):
    count = shifted.shape[1]
    natoms = shifted.shape[2]
    blocks = shifted.reshape(2 * NW, count, natoms, 2, NO, NO).astype(jnp.float32)
    derivs_all = gradient.astype(jnp.float32)

    def one_slot(total, slot):
        table = lax.dynamic_index_in_dim(weights, slot, 2, keepdims=False).reshape(2 * NW, 3, 3, natoms)
        derivs = lax.dynamic_index_in_dim(derivs_all, slot, 0, keepdims=False).reshape(3, natoms, NO, NO)
        kernel = jnp.einsum("sija,janl->aslin", table, derivs).astype(jnp.bfloat16)
        kernel = lax.optimization_barrier(kernel).astype(jnp.float32)
        column = lax.dynamic_index_in_dim(neighbours, slot, 1, keepdims=False).astype(jnp.int32)
        gathered = jnp.take(blocks, column, axis=2)
        middle = jnp.einsum("seacml,aslin->aiecmn", gathered, kernel).astype(jnp.bfloat16)
        middle = lax.optimization_barrier(middle).astype(jnp.float32)
        total = total + jnp.einsum("iapm,aiecmn->eacpn", derivs, middle)
        return total, None

    start_total = jnp.zeros((count, natoms, 2, NO, NO), jnp.float32)
    total, _ = lax.scan(one_slot, start_total, jnp.arange(NB, dtype=jnp.int32))
    return total


def reference(green, coupling, gradient, neighbours, offsets):
    margin = 2 * E_DEV
    total = jnp.zeros((NE, NA, 2, NO, NO), jnp.float32)
    for momentum in range(NK):
        padded = jnp.pad(green[momentum], ((margin, margin), (0, 0), (0, 0)))
        shifted = shifted_stack(padded, offsets, NE, margin)
        total = total + sandwich(shifted, coupling[momentum], gradient, neighbours)
    return total.reshape(NE, NA, 2 * NO * NO)
```

```python
import functools

import jax
import jax.numpy as jnp
from jax import lax
from jax.experimental import pallas as pl
from jax.experimental.pallas import tpu as pltpu
from jax.sharding import PartitionSpec as P

NO = 32
NB = 5
NW = 3
NS = 2 * NW
LANES = 128
COPIES = LANES // NO
HI = NO // COPIES
VMEM_LIMIT = 40 * 1024 * 1024

NT = (((1,), (1,)), ((), ()))


def fold_matrix():
    row = lax.broadcasted_iota(jnp.int32, (LANES, COPIES * LANES), 0)
    col = lax.broadcasted_iota(jnp.int32, (LANES, COPIES * LANES), 1)
    inner = col % NO
    source = (col // LANES) * NO + (inner % HI) * COPIES + inner // HI
    return jnp.where(row == source, 1.0, 0.0).astype(jnp.bfloat16)


def spread_rows(spread, at, stacked, fold):
    wide = jnp.dot(stacked, fold, preferred_element_type=jnp.float32)
    for q in range(COPIES):
        spread[q, at : at + stacked.shape[0], :] = wide[:, q * LANES : (q + 1) * LANES]


def tables_kernel(natoms, gradient, coupling, kernel_out, derivs_out, spread, rows):
    fold = fold_matrix()
    tiles = NO * NO // LANES
    block = natoms * tiles
    for slot in range(NB):
        for direction in range(3):
            flat = gradient[slot, direction]
            stacked = jnp.concatenate(
                [flat[:, t * LANES : (t + 1) * LANES] for t in range(tiles)], axis=0
            )
            at = (slot * 3 + direction) * block
            spread_rows(spread, at, stacked, fold)

    pairs = 9
    row = lax.broadcasted_iota(jnp.int32, (NS * pairs, pairs * 2 * LANES), 0)
    col = lax.broadcasted_iota(jnp.int32, (NS * pairs, pairs * 2 * LANES), 1)
    source = ((col % (2 * LANES)) // NO) * pairs + col // (2 * LANES)
    expand = jnp.where(
        (row == source) & ((col % (2 * LANES)) // NO < NS), 1.0, 0.0
    ).astype(jnp.float32)
    wide = lax.dot_general(
        coupling[...],
        expand,
        (((0,), (0,)), ((), ())),
        precision=lax.Precision.HIGHEST,
        preferred_element_type=jnp.float32,
    )
    for k in range(pairs * 2):
        rows[k] = wide[:, k * LANES : (k + 1) * LANES]

    for slot in range(NB):

        def one_atom(atom, carry):
            at = slot * natoms + atom
            derivs = [
                [
                    spread[
                        q, pl.ds((slot * 3 + j) * block + atom, tiles, stride=natoms), :
                    ]
                    for q in range(COPIES)
                ]
                for j in range(3)
            ]
            for j in range(3):
                derivs_out[at, j * NO : (j + 1) * NO, :] = jnp.concatenate(
                    derivs[j], axis=0
                ).astype(jnp.bfloat16)
            for i in range(3):
                for half in range(2):
                    total = None
                    for j in range(3):
                        weight = rows[(3 * i + j) * 2 + half, pl.ds(at, 1), :]
                        term = jnp.concatenate([d * weight for d in derivs[j]], axis=0)
                        total = term if total is None else total + term
                    kernel_out[
                        at, i * NO : (i + 1) * NO, half * LANES : (half + 1) * LANES
                    ] = total.astype(jnp.bfloat16)
            return carry

        lax.fori_loop(0, natoms, one_atom, 0)


def tables(gradient, coupling):
    natoms = gradient.shape[2]
    count = NB * natoms
    tiles = NO * NO // LANES
    return pl.pallas_call(
        functools.partial(tables_kernel, natoms),
        out_shape=(
            jax.ShapeDtypeStruct((count, 3 * NO, 2 * LANES), jnp.bfloat16),
            jax.ShapeDtypeStruct((count, 3 * NO, LANES), jnp.bfloat16),
        ),
        in_specs=[pl.BlockSpec(memory_space=pltpu.VMEM)] * 2,
        out_specs=[pl.BlockSpec(memory_space=pltpu.VMEM)] * 2,
        scratch_shapes=[
            pltpu.VMEM((COPIES, NB * 3 * tiles * natoms, LANES), jnp.float32),
            pltpu.VMEM((9 * 2, count, LANES), jnp.float32),
        ],
        compiler_params=pltpu.CompilerParams(vmem_limit_bytes=VMEM_LIMIT),
        cost_estimate=pl.CostEstimate(
            flops=200_000_000, bytes_accessed=6_000_000, transcendentals=0
        ),
        name="tables",
    )(gradient, coupling)


def sandwich_kernel(
    count, natoms, neighbours, offsets, below2, below1, local, above1, above2,
    kernel, derivs, out, spread, blocks, sums,
):
    fold = fold_matrix()
    tiles = 2 * NO * NO // LANES
    energy_rows = tiles * natoms
    for piece, ref in enumerate((below2, below1, local, above1, above2)):
        for e in range(count):
            flat = ref[e]
            stacked = jnp.concatenate(
                [flat[:, t * LANES : (t + 1) * LANES] for t in range(tiles)], axis=0
            )
            at = (piece * count + e) * energy_rows
            spread_rows(spread, at, stacked, fold)

    group = lax.broadcasted_iota(jnp.int32, (HI, LANES), 1) // NO
    starts = []
    for phonon in range(NW):
        for sign in (1, -1):
            starts.append((2 * count - sign * offsets[phonon]) * energy_rows)

    def build(atom, carry):
        for e in range(count):
            for c in range(2):
                for half in range(2):
                    pieces = []
                    for q in range(COPIES):
                        total = jnp.zeros((HI, LANES), jnp.float32)
                        for g in range(COPIES):
                            s = half * COPIES + g
                            if s < NS:
                                base = starts[s] + (e * tiles + c * HI) * natoms + atom
                                part = spread[q, pl.ds(base, HI, stride=natoms), :]
                                total = jnp.where(group == g, part, total)
                        pieces.append(total)
                    at = (e * 2 + c) * NO
                    blocks[atom, at : at + NO, half * LANES : (half + 1) * LANES] = (
                        jnp.concatenate(pieces, axis=0).astype(jnp.bfloat16)
                    )
        return carry

    lax.fori_loop(0, natoms, build, 0)

    groups = 2 * count
    wide = lax.broadcasted_iota(jnp.int32, (NO, LANES), 1) // NO
    masks = [jnp.where(wide == g, 1.0, 0.0).astype(jnp.bfloat16) for g in range(groups)]

    def one_atom(atom, carry):
        lefts = []
        rights = []
        for slot in range(NB):
            at = slot * natoms + atom
            middle = lax.dot_general(
                kernel[at], blocks[neighbours[slot, atom]], NT,
                preferred_element_type=jnp.float32,
            ).astype(jnp.bfloat16)
            for i in range(3):
                rights.append(middle[i * NO : (i + 1) * NO, :])
                block = derivs[at, i * NO : (i + 1) * NO, :]
                lefts.append(jnp.concatenate([block * mask for mask in masks], axis=0))
        sigma = lax.dot_general(
            jnp.concatenate(lefts, axis=1), jnp.concatenate(rights, axis=1), NT,
            preferred_element_type=jnp.float32,
        )
        for q in range(COPIES):
            part = jnp.concatenate(
                [sigma[g * NO + q * HI : g * NO + (q + 1) * HI, :] for g in range(groups)],
                axis=0,
            )
            sums[q, pl.ds(atom * groups * HI, groups * HI), :] = part.astype(jnp.bfloat16)
        return carry

    lax.fori_loop(0, natoms, one_atom, 0)

    row = lax.broadcasted_iota(jnp.int32, (NO, LANES), 0)
    col = lax.broadcasted_iota(jnp.int32, (NO, LANES), 1)
    placed = None
    for q in range(COPIES):
        place = jnp.where(
            (col // NO == q) & ((row % HI) * COPIES + row // HI == col % NO), 1.0, 0.0
        ).astype(jnp.bfloat16)
        term = jnp.dot(sums[q], place, preferred_element_type=jnp.float32)
        placed = term if placed is None else placed + term
    out[...] = placed.astype(jnp.bfloat16).reshape(out.shape)


def sandwich(window, kernel, derivs, neighbours, offsets, shares):
    count, natoms, _ = window[0].shape
    groups = 2 * count
    tiles = 2 * NO * NO // LANES
    rows = natoms * groups * HI
    return pl.pallas_call(
        functools.partial(sandwich_kernel, count, natoms),
        out_shape=jax.ShapeDtypeStruct((shares, rows // shares, LANES), jnp.bfloat16),
        in_specs=[pl.BlockSpec(memory_space=pltpu.SMEM)] * 2
        + [pl.BlockSpec(memory_space=pltpu.VMEM)] * 7,
        out_specs=pl.BlockSpec(memory_space=pltpu.VMEM),
        scratch_shapes=[
            pltpu.VMEM((COPIES, 5 * count * tiles * natoms, LANES), jnp.float32),
            pltpu.VMEM((natoms, groups * NO, 2 * LANES), jnp.bfloat16),
            pltpu.VMEM((COPIES, rows, NO), jnp.bfloat16),
        ],
        compiler_params=pltpu.CompilerParams(vmem_limit_bytes=VMEM_LIMIT),
        cost_estimate=pl.CostEstimate(
            flops=800_000_000, bytes_accessed=7_000_000, transcendentals=0
        ),
        name="sandwich",
    )(neighbours, offsets, *window, kernel, derivs)


def combine_kernel(parts, out, total):
    count, share, width = out.shape
    tiles = width // LANES
    summed = parts[0].astype(jnp.float32)
    for k in range(1, parts.shape[0]):
        summed = summed + parts[k].astype(jnp.float32)
    total[...] = summed
    for e in range(count):
        for t in range(tiles):
            out[e, :, t * LANES : (t + 1) * LANES] = total[
                pl.ds(e * tiles + t, share, stride=count * tiles), :
            ]


def combine(parts, count, share):
    return pl.pallas_call(
        combine_kernel,
        out_shape=jax.ShapeDtypeStruct((count, share, 2 * NO * NO), jnp.float32),
        in_specs=[pl.BlockSpec(memory_space=pltpu.VMEM)],
        out_specs=pl.BlockSpec(memory_space=pltpu.VMEM),
        scratch_shapes=[pltpu.VMEM(parts.shape[1:], jnp.float32)],
        name="combine",
    )(parts)


def shifted(array, axis, by):
    length = lax.axis_size(axis)
    pairs = [(i, i + by) for i in range(length) if 0 <= i + by < length]
    return lax.ppermute(array, axis, pairs)


def local_partial(window, coupling, gradient, neighbours, offsets, shares):
    kernel, derivs = tables(gradient, coupling.reshape(NS * 9, -1))
    return sandwich(window, kernel, derivs, neighbours.T, offsets, shares)


def body(green, coupling, gradient, neighbours, offsets):
    local_block = green[0]
    count, natoms, _ = local_block.shape
    shares = lax.axis_size("mom")
    window = (
        shifted(local_block, "energy", 2),
        shifted(local_block, "energy", 1),
        local_block,
        shifted(local_block, "energy", -1),
        shifted(local_block, "energy", -2),
    )
    partial_terms = local_partial(window, coupling[0], gradient, neighbours, offsets, shares)
    parts = lax.all_to_all(partial_terms, "mom", 0, 0, tiled=True)
    return combine(parts, count, natoms // shares)


def solution(mesh):
    in_specs = (P("mom", "energy", None, None), P("mom", None, None, None, None), P(), P(), P())
    out_specs = P("energy", "mom", None)
    return jax.shard_map(body, mesh=mesh, in_specs=in_specs, out_specs=out_specs, check_vma=False)
```

```python
import functools

import jax
import jax.numpy as jnp
from jax import lax
from jax.experimental import pallas as pl
from jax.experimental.pallas import tpu as pltpu
from jax.sharding import PartitionSpec as P

NO = 32
NB = 5
NW = 3
NS = 2 * NW
ND = 3
LANES = 128
COPIES = LANES // NO
HI = NO // COPIES
VMEM_LIMIT = 40 * 1024 * 1024

NT = (((1,), (1,)), ((), ()))


def in_hbm(array):
    return pltpu.with_memory_space_constraint(array, pltpu.HBM)


def iota(shape, dim):
    return lax.broadcasted_iota(jnp.int32, shape, dim)


def ones_where(condition):
    return jnp.where(condition, 1.0, 0.0).astype(jnp.bfloat16)


def mixed(lane):
    return (lane % HI) * COPIES + lane // HI


def fold_matrix():
    shape = (LANES, COPIES * LANES)
    row, col = iota(shape, 0), iota(shape, 1)
    return ones_where(row == (col // LANES) * NO + mixed(col % NO))


def lane_matrix():
    row, col = iota((LANES, LANES), 0), iota((LANES, LANES), 1)
    return ones_where(row == (col // NO) * NO + mixed(col % NO))


def row_matrix(tiles, natoms):
    size = tiles * natoms
    row, col = iota((size, size), 0), iota((size, size), 1)
    return ones_where(col == (row % tiles) * natoms + row // tiles)


def stack_tiles(flat):
    return jnp.concatenate(
        [flat[:, t : t + LANES] for t in range(0, flat.shape[1], LANES)], axis=0
    )


def exact_dot(left, right):
    return jnp.dot(left, right, preferred_element_type=jnp.float32)


def tables_kernel(
    natoms, gradient_hbm, coupling_hbm, kernel_out, derivs_out,
    gradient, coupling, spread, rows, gradient_sems, coupling_sem,
):
    copy_coupling = pltpu.make_async_copy(coupling_hbm.at[:, 0, :], coupling, coupling_sem)
    copy_coupling.start()
    copies = [
        pltpu.make_async_copy(gradient_hbm.at[b], gradient.at[b], gradient_sems.at[b])
        for b in range(NB)
    ]
    for copy in copies:
        copy.start()

    tiles = NO * NO // LANES
    block = natoms * tiles
    pairs = ND * ND
    cells = pairs * NB
    width = -(-NS * cells // LANES) * LANES
    fold = fold_matrix()
    order = row_matrix(tiles, natoms)
    lane = iota((width, 2 * LANES), 0)
    widen = ones_where((lane < NS * cells) & (lane // cells == iota((width, 2 * LANES), 1) // NO))
    cell = iota((natoms, width), 1)
    cell = jnp.where(cell < NS * cells, cell % cells, -1)

    copy_coupling.wait()
    table = jnp.transpose(coupling[...])
    table = jnp.concatenate(
        [table, jnp.zeros((natoms, width - NS * cells), jnp.float32)], axis=1
    )
    high = table.astype(jnp.bfloat16)
    low = (table - high.astype(jnp.float32)).astype(jnp.bfloat16)
    for half in (high, low):
        half32 = half.astype(jnp.float32)
        left = jnp.concatenate(
            [jnp.where(cell == k, half32, 0.0) for k in range(cells)], axis=0
        ).astype(jnp.bfloat16)
        wide = exact_dot(left, widen)
        for k in range(2):
            part = wide[:, k * LANES : (k + 1) * LANES]
            rows[k] = part if half is high else rows[k] + part

    for slot in range(NB):
        copies[slot].wait()
        for j in range(ND):
            ordered = exact_dot(order, stack_tiles(gradient[slot, j])).astype(jnp.bfloat16)
            wide = exact_dot(ordered, fold)
            for q in range(COPIES):
                spread[q, (slot * ND + j) * block : (slot * ND + j + 1) * block, :] = wide[
                    :, q * LANES : (q + 1) * LANES
                ]

    for slot in range(NB):

        def one_atom(atom, carry):
            at = slot * natoms + atom
            derivs = [
                [
                    spread[
                        q,
                        pl.ds(pl.multiple_of((slot * ND + j) * block + atom * tiles, tiles), tiles),
                        :,
                    ]
                    for q in range(COPIES)
                ]
                for j in range(ND)
            ]
            for j in range(ND):
                derivs_out[at, j * NO : (j + 1) * NO, :] = jnp.concatenate(
                    derivs[j], axis=0
                ).astype(jnp.bfloat16)
            for i in range(ND):
                for half in range(2):
                    total = None
                    for j in range(ND):
                        weight = rows[
                            half, pl.ds(((ND * i + j) * NB + slot) * natoms + atom, 1), :
                        ]
                        term = jnp.concatenate([d * weight for d in derivs[j]], axis=0)
                        total = term if total is None else total + term
                    kernel_out[
                        at, i * NO : (i + 1) * NO, half * LANES : (half + 1) * LANES
                    ] = total.astype(jnp.bfloat16)
            return carry

        lax.fori_loop(0, natoms, one_atom, 0, unroll=2)


def tables(gradient, coupling):
    natoms = gradient.shape[2]
    count = NB * natoms
    tiles = NO * NO // LANES
    return pl.pallas_call(
        functools.partial(tables_kernel, natoms),
        out_shape=(
            jax.ShapeDtypeStruct((count, ND * NO, 2 * LANES), jnp.bfloat16),
            jax.ShapeDtypeStruct((count, ND * NO, LANES), jnp.bfloat16),
        ),
        in_specs=[pl.BlockSpec(memory_space=pltpu.HBM)] * 2,
        out_specs=[pl.BlockSpec(memory_space=pltpu.VMEM)] * 2,
        scratch_shapes=[
            pltpu.VMEM(gradient.shape, gradient.dtype),
            pltpu.VMEM((coupling.shape[0], natoms), jnp.float32),
            pltpu.VMEM((COPIES, count * ND * tiles, LANES), jnp.float32),
            pltpu.VMEM((2, ND * ND * count, LANES), jnp.float32),
            pltpu.SemaphoreType.DMA((NB,)),
            pltpu.SemaphoreType.DMA,
        ],
        compiler_params=pltpu.CompilerParams(vmem_limit_bytes=VMEM_LIMIT),
        cost_estimate=pl.CostEstimate(
            flops=200_000_000, bytes_accessed=6_000_000, transcendentals=0
        ),
        name="tables",
    )(in_hbm(gradient), in_hbm(coupling))


def sandwich_kernel(
    count, natoms, shares, neighbours_hbm, offsets_hbm, local_hbm, below2, below1, above1, above2,
    kernel, derivs, out, neighbours, offsets, local, planes, blocks, sums, sems,
):
    copies = [
        pltpu.make_async_copy(source, target, sems.at[k])
        for k, (source, target) in enumerate(
            ((local_hbm, local), (neighbours_hbm, neighbours), (offsets_hbm, offsets))
        )
    ]
    for copy in copies:
        copy.start()

    tiles = 2 * NO * NO // LANES
    size = tiles * natoms
    lanes = lane_matrix()
    order = row_matrix(tiles, natoms)
    for piece, ref in ((0, below2), (1, below1), (3, above1), (4, above2), (2, local)):
        if ref is local:
            copies[0].wait()
        mixes = [
            exact_dot(stack_tiles(ref[e]), lanes).astype(jnp.bfloat16) for e in range(count)
        ]
        ordered = exact_dot(order, jnp.concatenate(mixes, axis=1))
        for e in range(count):
            planes[piece * count + e] = ordered[:, e * LANES : (e + 1) * LANES]

    copies[1].wait()
    copies[2].wait()
    group = iota((HI, LANES), 1) // NO
    starts = []
    for phonon in range(NW):
        for sign in (1, -1):
            starts.append(2 * count - sign * offsets[phonon])

    def build(atom, carry):
        for e in range(count):
            turned = []
            for s in range(NS):
                part = planes[starts[s] + e, pl.ds(pl.multiple_of(atom * tiles, tiles), tiles), :]
                turned.append(
                    [part] + [pltpu.roll(part, r * NO, axis=1) for r in range(1, COPIES)]
                )
            for c in range(2):
                at = (e * 2 + c) * NO
                for half in range(2):
                    pieces = []
                    for q in range(COPIES):
                        total = None
                        for g in range(min(COPIES, NS - half * COPIES)):
                            part = turned[half * COPIES + g][(g - q) % COPIES][
                                c * HI : (c + 1) * HI
                            ]
                            total = part if total is None else jnp.where(group == g, part, total)
                        pieces.append(total)
                    blocks[atom, at : at + NO, half * LANES : (half + 1) * LANES] = (
                        jnp.concatenate(pieces, axis=0).astype(jnp.bfloat16)
                    )
        return carry

    lax.fori_loop(0, natoms, build, 0, unroll=2)

    groups = 2 * count
    wide = iota((NO, LANES), 1) // NO
    masks = [ones_where(wide == g) for g in range(groups)]
    share = natoms // shares

    def some_atoms(step, carry):
        middles = []
        for k in range(share):
            atom = step * share + k
            middles.append(
                [
                    lax.dot_general(
                        kernel[slot * natoms + atom], blocks[neighbours[slot, atom]], NT,
                        preferred_element_type=jnp.float32,
                    ).astype(jnp.bfloat16)
                    for slot in range(NB)
                ]
            )
        for k in range(share):
            atom = step * share + k
            lefts = []
            rights = []
            for slot in range(NB):
                for i in range(ND):
                    rights.append(middles[k][slot][i * NO : (i + 1) * NO, :])
                    block = derivs[slot * natoms + atom, i * NO : (i + 1) * NO, :]
                    lefts.append(jnp.concatenate([block * mask for mask in masks], axis=0))
            sigma = lax.dot_general(
                jnp.concatenate(lefts, axis=1), jnp.concatenate(rights, axis=1), NT,
                preferred_element_type=jnp.float32,
            )
            for q in range(COPIES):
                part = jnp.concatenate(
                    [sigma[g * NO + q * HI : g * NO + (q + 1) * HI, :] for g in range(groups)],
                    axis=0,
                )
                sums[q, pl.ds(pl.multiple_of(atom * groups * HI, groups * HI), groups * HI), :] = (
                    part.astype(jnp.bfloat16)
                )
        return carry

    lax.fori_loop(0, shares, some_atoms, 0)

    row, col = iota((NO, LANES), 0), iota((NO, LANES), 1)
    placed = None
    for q in range(COPIES):
        place = ones_where((col // NO == q) & (mixed(row) == col % NO))
        term = exact_dot(sums[q], place)
        placed = term if placed is None else placed + term
    out[...] = placed.astype(jnp.bfloat16).reshape(out.shape)


def sandwich(window, kernel, derivs, neighbours, offsets, shares):
    below2, below1, local, above1, above2 = window
    count, natoms, _ = local.shape
    groups = 2 * count
    tiles = 2 * NO * NO // LANES
    rows = natoms * groups * HI
    return pl.pallas_call(
        functools.partial(sandwich_kernel, count, natoms, shares),
        out_shape=jax.ShapeDtypeStruct((shares, rows // shares, LANES), jnp.bfloat16),
        in_specs=[pl.BlockSpec(memory_space=pltpu.HBM)] * 3
        + [pl.BlockSpec(memory_space=pltpu.VMEM)] * 6,
        out_specs=pl.BlockSpec(memory_space=pltpu.VMEM),
        scratch_shapes=[
            pltpu.SMEM(neighbours.shape, jnp.int32),
            pltpu.SMEM(offsets.shape, jnp.int32),
            pltpu.VMEM(local.shape, local.dtype),
            pltpu.VMEM((5 * count, tiles * natoms, LANES), jnp.float32),
            pltpu.VMEM((natoms, groups * NO, 2 * LANES), jnp.bfloat16),
            pltpu.VMEM((COPIES, rows, NO), jnp.bfloat16),
            pltpu.SemaphoreType.DMA((3,)),
        ],
        compiler_params=pltpu.CompilerParams(vmem_limit_bytes=VMEM_LIMIT),
        cost_estimate=pl.CostEstimate(
            flops=800_000_000, bytes_accessed=7_000_000, transcendentals=0
        ),
        name="sandwich",
    )(
        in_hbm(neighbours), in_hbm(offsets), in_hbm(local),
        below2, below1, above1, above2, kernel, derivs,
    )


def combine_kernel(parts, out, total):
    count, share, width = out.shape
    tiles = width // LANES
    summed = parts[0].astype(jnp.float32)
    for k in range(1, parts.shape[0]):
        summed = summed + parts[k].astype(jnp.float32)
    total[...] = summed
    for e in range(count):
        for t in range(tiles):
            out[e, :, t * LANES : (t + 1) * LANES] = total[
                pl.ds(e * tiles + t, share, stride=count * tiles), :
            ]


def combine(parts, count, share):
    return pl.pallas_call(
        combine_kernel,
        out_shape=jax.ShapeDtypeStruct((count, share, 2 * NO * NO), jnp.float32),
        in_specs=[pl.BlockSpec(memory_space=pltpu.VMEM)],
        out_specs=pl.BlockSpec(memory_space=pltpu.VMEM),
        scratch_shapes=[pltpu.VMEM(parts.shape[1:], jnp.float32)],
        name="combine",
    )(parts)


def shifted(array, axis, by):
    length = lax.axis_size(axis)
    pairs = [(i, i + by) for i in range(length) if 0 <= i + by < length]
    return lax.ppermute(array, axis, pairs)


def local_partial(window, coupling, gradient, neighbours, offsets, shares):
    kernel, derivs = tables(gradient, coupling.reshape(-1, 1, coupling.shape[-1]))
    return sandwich(window, kernel, derivs, neighbours.T, offsets, shares)


def body(green, coupling, gradient, neighbours, offsets):
    local_block = green[0]
    count, natoms, _ = local_block.shape
    shares = lax.axis_size("mom")
    window = (
        shifted(local_block, "energy", 2),
        shifted(local_block, "energy", 1),
        local_block,
        shifted(local_block, "energy", -1),
        shifted(local_block, "energy", -2),
    )
    partial_terms = local_partial(window, coupling[0], gradient, neighbours, offsets, shares)
    parts = lax.all_to_all(partial_terms, "mom", 0, 0, tiled=True)
    return combine(parts, count, natoms // shares)


def solution(mesh):
    in_specs = (P("mom", "energy", None, None), P("mom", None, None, None, None), P(), P(), P())
    out_specs = P("energy", "mom", None)
    return jax.shard_map(body, mesh=mesh, in_specs=in_specs, out_specs=out_specs, check_vma=False)
```

```python
import functools

import jax
import jax.numpy as jnp
from jax import lax
from jax.experimental import pallas as pl
from jax.experimental.pallas import tpu as pltpu
from jax.sharding import PartitionSpec as P

NO = 32
NB = 5
NW = 3
NS = 2 * NW
ND = 3
LANES = 128
COPIES = LANES // NO
HI = NO // COPIES
VMEM_LIMIT = 40 * 1024 * 1024

NT = (((1,), (1,)), ((), ()))


def in_hbm(array):
    return pltpu.with_memory_space_constraint(array, pltpu.HBM)


def iota(shape, dim):
    return lax.broadcasted_iota(jnp.int32, shape, dim)


def ones_where(condition):
    return jnp.where(condition, 1.0, 0.0).astype(jnp.bfloat16)


def mixed(lane):
    return (lane % HI) * COPIES + lane // HI


def fold_matrix():
    shape = (LANES, COPIES * LANES)
    row, col = iota(shape, 0), iota(shape, 1)
    return ones_where(row == (col // LANES) * NO + mixed(col % NO))


def lane_matrix():
    row, col = iota((LANES, LANES), 0), iota((LANES, LANES), 1)
    return ones_where(row == (col // NO) * NO + mixed(col % NO))


def row_matrix(tiles, natoms):
    size = tiles * natoms
    row, col = iota((size, size), 0), iota((size, size), 1)
    return ones_where(col == (row % tiles) * natoms + row // tiles)


def stack_tiles(flat):
    return jnp.concatenate(
        [flat[:, t : t + LANES] for t in range(0, flat.shape[1], LANES)], axis=0
    )


def exact_dot(left, right):
    return jnp.dot(left, right, preferred_element_type=jnp.float32)


def tables_kernel(
    natoms, gradient_hbm, coupling_hbm, kernel_out, derivs_out,
    gradient, coupling, rows, sems,
):
    copies = [
        pltpu.make_async_copy(coupling_hbm.at[:, 0, :], coupling, sems.at[0]),
        pltpu.make_async_copy(gradient_hbm, gradient, sems.at[1]),
    ]
    for copy in copies:
        copy.start()

    tiles = NO * NO // LANES
    block = natoms * tiles
    cells = ND * ND * NB
    depth = rows.shape[2]
    width = -(-NS * cells // LANES) * LANES
    fold = fold_matrix()
    order = row_matrix(tiles, natoms)
    lane = iota((width, 2 * LANES), 0)
    widen = ones_where((lane < NS * cells) & (lane // cells == iota((width, 2 * LANES), 1) // NO))
    line, lane = iota((NB * depth, width), 0), iota((NB * depth, width), 1)
    chosen = (lane < NS * cells) & (lane % cells == (line % depth) * NB + line // depth)

    copies[0].wait()
    table = jnp.transpose(coupling[...])
    table = jnp.concatenate(
        [table, jnp.zeros((natoms, width - NS * cells), jnp.float32)], axis=1
    )
    for atom in range(natoms):
        left = jnp.where(chosen, table[atom : atom + 1, :], 0.0).astype(jnp.bfloat16)
        wide = exact_dot(left, widen)
        for slot in range(NB):
            for half in range(2):
                rows[atom * NB + slot, half] = wide[
                    slot * depth : (slot + 1) * depth, half * LANES : (half + 1) * LANES
                ]

    copies[1].wait()
    flats = [stack_tiles(gradient[slot, j]) for slot in range(NB) for j in range(ND)]
    ordered = exact_dot(order, jnp.concatenate(flats, axis=1)).astype(jnp.bfloat16)
    for slot in range(NB):
        for j in range(ND):
            at = (slot * ND + j) * LANES
            wide = exact_dot(ordered[:, at : at + LANES], fold)
            for atom in range(natoms):
                derivs_out[atom * NB + slot, j * NO : (j + 1) * NO, :] = jnp.concatenate(
                    [
                        wide[atom * tiles : (atom + 1) * tiles, q * LANES : (q + 1) * LANES]
                        for q in range(COPIES)
                    ],
                    axis=0,
                ).astype(jnp.bfloat16)

    def one_cell(at, carry):
        derivs = [
            derivs_out[at, j * NO : (j + 1) * NO, :].astype(jnp.float32) for j in range(ND)
        ]
        for i in range(ND):
            for half in range(2):
                total = None
                for j in range(ND):
                    term = derivs[j] * rows[at, half, ND * i + j : ND * i + j + 1, :]
                    total = term if total is None else total + term
                kernel_out[at, i * NO : (i + 1) * NO, half * LANES : (half + 1) * LANES] = (
                    total.astype(jnp.bfloat16)
                )
        return carry

    lax.fori_loop(0, natoms * NB, one_cell, 0, unroll=4)


def tables(gradient, coupling):
    natoms = gradient.shape[2]
    count = NB * natoms
    return pl.pallas_call(
        functools.partial(tables_kernel, natoms),
        out_shape=(
            jax.ShapeDtypeStruct((count, ND * NO, 2 * LANES), jnp.bfloat16),
            jax.ShapeDtypeStruct((count, ND * NO, LANES), jnp.bfloat16),
        ),
        in_specs=[pl.BlockSpec(memory_space=pltpu.HBM)] * 2,
        out_specs=[pl.BlockSpec(memory_space=pltpu.VMEM)] * 2,
        scratch_shapes=[
            pltpu.VMEM(gradient.shape, gradient.dtype),
            pltpu.VMEM((coupling.shape[0], natoms), jnp.float32),
            pltpu.VMEM((count, 2, 2 * HI, LANES), jnp.float32),
            pltpu.SemaphoreType.DMA((2,)),
        ],
        compiler_params=pltpu.CompilerParams(vmem_limit_bytes=VMEM_LIMIT),
        cost_estimate=pl.CostEstimate(
            flops=200_000_000, bytes_accessed=6_000_000, transcendentals=0
        ),
        name="tables",
    )(in_hbm(gradient), in_hbm(coupling))


def sandwich_kernel(
    count, natoms, shares, neighbours_hbm, offsets_hbm, local_hbm, below2, below1, above1, above2,
    kernel, derivs, out, neighbours, offsets, local, planes, blocks, sums, sems,
):
    copies = [
        pltpu.make_async_copy(source, target, sems.at[k])
        for k, (source, target) in enumerate(
            ((local_hbm, local), (neighbours_hbm, neighbours), (offsets_hbm, offsets))
        )
    ]
    for copy in copies:
        copy.start()

    tiles = 2 * NO * NO // LANES
    size = tiles * natoms
    lanes = lane_matrix()
    order = row_matrix(tiles, natoms)
    for piece, ref in ((0, below2), (1, below1), (3, above1), (4, above2), (2, local)):
        if ref is local:
            copies[0].wait()
        mixes = [
            exact_dot(stack_tiles(ref[e]), lanes).astype(jnp.bfloat16) for e in range(count)
        ]
        ordered = exact_dot(order, jnp.concatenate(mixes, axis=1))
        for e in range(count):
            planes[piece * count + e] = ordered[:, e * LANES : (e + 1) * LANES]

    copies[1].wait()
    copies[2].wait()
    group = iota((HI, LANES), 1) // NO
    starts = []
    for phonon in range(NW):
        for sign in (1, -1):
            starts.append(2 * count - sign * offsets[phonon])

    def build(atom, carry):
        for e in range(count):
            turned = []
            for s in range(NS):
                part = planes[starts[s] + e, pl.ds(pl.multiple_of(atom * tiles, tiles), tiles), :]
                turned.append(
                    [part] + [pltpu.roll(part, r * NO, axis=1) for r in range(1, COPIES)]
                )
            for c in range(2):
                at = (e * 2 + c) * NO
                for half in range(2):
                    pieces = []
                    for q in range(COPIES):
                        total = None
                        for g in range(min(COPIES, NS - half * COPIES)):
                            part = turned[half * COPIES + g][(g - q) % COPIES][
                                c * HI : (c + 1) * HI
                            ]
                            total = part if total is None else jnp.where(group == g, part, total)
                        pieces.append(total)
                    blocks[atom, at : at + NO, half * LANES : (half + 1) * LANES] = (
                        jnp.concatenate(pieces, axis=0).astype(jnp.bfloat16)
                    )
        return carry

    lax.fori_loop(0, natoms, build, 0, unroll=2)

    groups = 2 * count
    wide = iota((NO, LANES), 1) // NO
    masks = [ones_where(wide == g) for g in range(groups)]
    share = natoms // shares

    def some_atoms(step, carry):
        middles = []
        for k in range(share):
            atom = step * share + k
            middles.append(
                [
                    lax.dot_general(
                        kernel[atom * NB + slot], blocks[neighbours[slot, atom]], NT,
                        preferred_element_type=jnp.float32,
                    ).astype(jnp.bfloat16)
                    for slot in range(NB)
                ]
            )
        for k in range(share):
            atom = step * share + k
            lefts = []
            rights = []
            for slot in range(NB):
                for i in range(ND):
                    rights.append(middles[k][slot][i * NO : (i + 1) * NO, :])
                    block = derivs[atom * NB + slot, i * NO : (i + 1) * NO, :]
                    lefts.append(jnp.concatenate([block * mask for mask in masks], axis=0))
            sigma = lax.dot_general(
                jnp.concatenate(lefts, axis=1), jnp.concatenate(rights, axis=1), NT,
                preferred_element_type=jnp.float32,
            )
            for q in range(COPIES):
                part = jnp.concatenate(
                    [sigma[g * NO + q * HI : g * NO + (q + 1) * HI, :] for g in range(groups)],
                    axis=0,
                )
                sums[q, pl.ds(pl.multiple_of(atom * groups * HI, groups * HI), groups * HI), :] = (
                    part.astype(jnp.bfloat16)
                )
        return carry

    lax.fori_loop(0, shares, some_atoms, 0)

    row, col = iota((NO, LANES), 0), iota((NO, LANES), 1)
    placed = None
    for q in range(COPIES):
        place = ones_where((col // NO == q) & (mixed(row) == col % NO))
        term = exact_dot(sums[q], place)
        placed = term if placed is None else placed + term
    out[...] = placed.astype(jnp.bfloat16).reshape(out.shape)


def sandwich(window, kernel, derivs, neighbours, offsets, shares):
    below2, below1, local, above1, above2 = window
    count, natoms, _ = local.shape
    groups = 2 * count
    tiles = 2 * NO * NO // LANES
    rows = natoms * groups * HI
    return pl.pallas_call(
        functools.partial(sandwich_kernel, count, natoms, shares),
        out_shape=jax.ShapeDtypeStruct((shares, rows // shares, LANES), jnp.bfloat16),
        in_specs=[pl.BlockSpec(memory_space=pltpu.HBM)] * 3
        + [pl.BlockSpec(memory_space=pltpu.VMEM)] * 6,
        out_specs=pl.BlockSpec(memory_space=pltpu.VMEM),
        scratch_shapes=[
            pltpu.SMEM(neighbours.shape, jnp.int32),
            pltpu.SMEM(offsets.shape, jnp.int32),
            pltpu.VMEM(local.shape, local.dtype),
            pltpu.VMEM((5 * count, tiles * natoms, LANES), jnp.float32),
            pltpu.VMEM((natoms, groups * NO, 2 * LANES), jnp.bfloat16),
            pltpu.VMEM((COPIES, rows, NO), jnp.bfloat16),
            pltpu.SemaphoreType.DMA((3,)),
        ],
        compiler_params=pltpu.CompilerParams(vmem_limit_bytes=VMEM_LIMIT),
        cost_estimate=pl.CostEstimate(
            flops=800_000_000, bytes_accessed=7_000_000, transcendentals=0
        ),
        name="sandwich",
    )(
        in_hbm(neighbours), in_hbm(offsets), in_hbm(local),
        below2, below1, above1, above2, kernel, derivs,
    )


def combine_kernel(parts, out, total):
    count, share, width = out.shape
    tiles = width // LANES
    summed = parts[0].astype(jnp.float32)
    for k in range(1, parts.shape[0]):
        summed = summed + parts[k].astype(jnp.float32)
    total[...] = summed
    for e in range(count):
        for t in range(tiles):
            out[e, :, t * LANES : (t + 1) * LANES] = total[
                pl.ds(e * tiles + t, share, stride=count * tiles), :
            ]


def combine(parts, count, share):
    return pl.pallas_call(
        combine_kernel,
        out_shape=jax.ShapeDtypeStruct((count, share, 2 * NO * NO), jnp.float32),
        in_specs=[pl.BlockSpec(memory_space=pltpu.VMEM)],
        out_specs=pl.BlockSpec(memory_space=pltpu.VMEM),
        scratch_shapes=[pltpu.VMEM(parts.shape[1:], jnp.float32)],
        name="combine",
    )(parts)


def shifted(array, axis, by):
    length = lax.axis_size(axis)
    pairs = [(i, i + by) for i in range(length) if 0 <= i + by < length]
    return lax.ppermute(array, axis, pairs)


def local_partial(window, coupling, gradient, neighbours, offsets, shares):
    kernel, derivs = tables(gradient, coupling.reshape(-1, 1, coupling.shape[-1]))
    return sandwich(window, kernel, derivs, neighbours.T, offsets, shares)


def body(green, coupling, gradient, neighbours, offsets):
    local_block = green[0]
    count, natoms, _ = local_block.shape
    shares = lax.axis_size("mom")
    window = (
        shifted(local_block, "energy", 2),
        shifted(local_block, "energy", 1),
        local_block,
        shifted(local_block, "energy", -1),
        shifted(local_block, "energy", -2),
    )
    partial_terms = local_partial(window, coupling[0], gradient, neighbours, offsets, shares)
    parts = lax.all_to_all(partial_terms, "mom", 0, 0, tiled=True)
    return combine(parts, count, natoms // shares)


def solution(mesh):
    in_specs = (P("mom", "energy", None, None), P("mom", None, None, None, None), P(), P(), P())
    out_specs = P("energy", "mom", None)
    return jax.shard_map(body, mesh=mesh, in_specs=in_specs, out_specs=out_specs, check_vma=False)
```

```python
import functools

import jax
import jax.numpy as jnp
from jax import lax
from jax.experimental import pallas as pl
from jax.experimental.pallas import tpu as pltpu
from jax.sharding import PartitionSpec as P

NO = 32
NB = 5
NW = 3
NS = 2 * NW
ND = 3
LANES = 128
COPIES = LANES // NO
HI = NO // COPIES
VMEM_LIMIT = 40 * 1024 * 1024

NT = (((1,), (1,)), ((), ()))


def in_hbm(array):
    return pltpu.with_memory_space_constraint(array, pltpu.HBM)


def iota(shape, dim):
    return lax.broadcasted_iota(jnp.int32, shape, dim)


def ones_where(condition):
    return jnp.where(condition, 1.0, 0.0).astype(jnp.bfloat16)


def mixed(lane):
    return (lane % HI) * COPIES + lane // HI


def fold_matrix():
    shape = (LANES, COPIES * LANES)
    row, col = iota(shape, 0), iota(shape, 1)
    return ones_where(row == (col // LANES) * NO + mixed(col % NO))


def lane_matrix():
    row, col = iota((LANES, LANES), 0), iota((LANES, LANES), 1)
    return ones_where(row == (col // NO) * NO + mixed(col % NO))


def row_matrix(tiles, natoms):
    size = tiles * natoms
    row, col = iota((size, size), 0), iota((size, size), 1)
    return ones_where(col == (row % tiles) * natoms + row // tiles)


def stack_tiles(flat):
    return jnp.concatenate(
        [flat[:, t : t + LANES] for t in range(0, flat.shape[1], LANES)], axis=0
    )


def exact_dot(left, right):
    return jnp.dot(left, right, preferred_element_type=jnp.float32)


def make_planes(block, planes, at):
    count, natoms, size = block.shape
    mixes = [
        exact_dot(stack_tiles(block[e]), lane_matrix()).astype(jnp.bfloat16)
        for e in range(count)
    ]
    ordered = exact_dot(
        row_matrix(size // LANES, natoms), jnp.concatenate(mixes, axis=1)
    )
    for e in range(count):
        planes[at + e] = ordered[:, e * LANES : (e + 1) * LANES]


def tables_kernel(
    natoms, local_hbm, gradient_hbm, coupling_hbm, kernel_out, derivs_out, planes_out,
    local, gradient, coupling, rows, sems,
):
    copies = [
        pltpu.make_async_copy(coupling_hbm.at[:, 0, :], coupling, sems.at[0]),
        pltpu.make_async_copy(gradient_hbm, gradient, sems.at[1]),
        pltpu.make_async_copy(local_hbm, local, sems.at[2]),
    ]
    for copy in copies:
        copy.start()

    tiles = NO * NO // LANES
    block = natoms * tiles
    cells = ND * ND * NB
    depth = rows.shape[2]
    width = -(-NS * cells // LANES) * LANES
    fold = fold_matrix()
    order = row_matrix(tiles, natoms)
    lane = iota((width, 2 * LANES), 0)
    widen = ones_where((lane < NS * cells) & (lane // cells == iota((width, 2 * LANES), 1) // NO))
    line, lane = iota((NB * depth, width), 0), iota((NB * depth, width), 1)
    chosen = (lane < NS * cells) & (lane % cells == (line % depth) * NB + line // depth)

    copies[0].wait()
    table = jnp.transpose(coupling[...])
    table = jnp.concatenate(
        [table, jnp.zeros((natoms, width - NS * cells), jnp.float32)], axis=1
    )
    for atom in range(natoms):
        left = jnp.where(chosen, table[atom : atom + 1, :], 0.0).astype(jnp.bfloat16)
        wide = exact_dot(left, widen)
        for slot in range(NB):
            for half in range(2):
                rows[atom * NB + slot, half] = wide[
                    slot * depth : (slot + 1) * depth, half * LANES : (half + 1) * LANES
                ]

    copies[1].wait()
    flats = [stack_tiles(gradient[slot, j]) for slot in range(NB) for j in range(ND)]
    ordered = exact_dot(order, jnp.concatenate(flats, axis=1)).astype(jnp.bfloat16)
    for slot in range(NB):
        for j in range(ND):
            at = (slot * ND + j) * LANES
            wide = exact_dot(ordered[:, at : at + LANES], fold)
            for atom in range(natoms):
                derivs_out[atom * NB + slot, j * NO : (j + 1) * NO, :] = jnp.concatenate(
                    [
                        wide[atom * tiles : (atom + 1) * tiles, q * LANES : (q + 1) * LANES]
                        for q in range(COPIES)
                    ],
                    axis=0,
                ).astype(jnp.bfloat16)

    copies[2].wait()
    make_planes(local, planes_out, 0)

    def one_cell(at, carry):
        derivs = [
            derivs_out[at, j * NO : (j + 1) * NO, :].astype(jnp.float32) for j in range(ND)
        ]
        for i in range(ND):
            for half in range(2):
                total = None
                for j in range(ND):
                    term = derivs[j] * rows[at, half, ND * i + j : ND * i + j + 1, :]
                    total = term if total is None else total + term
                kernel_out[at, i * NO : (i + 1) * NO, half * LANES : (half + 1) * LANES] = (
                    total.astype(jnp.bfloat16)
                )
        return carry

    lax.fori_loop(0, natoms * NB, one_cell, 0, unroll=4)


def tables(local, gradient, coupling):
    energies, natoms, size = local.shape
    count = NB * natoms
    return pl.pallas_call(
        functools.partial(tables_kernel, natoms),
        out_shape=(
            jax.ShapeDtypeStruct((count, ND * NO, 2 * LANES), jnp.bfloat16),
            jax.ShapeDtypeStruct((count, ND * NO, LANES), jnp.bfloat16),
            jax.ShapeDtypeStruct((energies, natoms * size // LANES, LANES), jnp.float32),
        ),
        in_specs=[pl.BlockSpec(memory_space=pltpu.HBM)] * 3,
        out_specs=[pl.BlockSpec(memory_space=pltpu.VMEM)] * 3,
        scratch_shapes=[
            pltpu.VMEM(local.shape, local.dtype),
            pltpu.VMEM(gradient.shape, gradient.dtype),
            pltpu.VMEM((coupling.shape[0], natoms), jnp.float32),
            pltpu.VMEM((count, 2, 2 * HI, LANES), jnp.float32),
            pltpu.SemaphoreType.DMA((3,)),
        ],
        compiler_params=pltpu.CompilerParams(vmem_limit_bytes=VMEM_LIMIT),
        cost_estimate=pl.CostEstimate(
            flops=200_000_000, bytes_accessed=6_000_000, transcendentals=0
        ),
        name="tables",
    )(in_hbm(local), in_hbm(gradient), in_hbm(coupling))


def sandwich_kernel(
    count, natoms, neighbours_hbm, offsets_hbm, middle_planes, below2, below1, above1, above2,
    kernel, derivs, out, neighbours, offsets, planes, blocks, sems,
):
    copies = [
        pltpu.make_async_copy(neighbours_hbm, neighbours, sems.at[0]),
        pltpu.make_async_copy(offsets_hbm, offsets, sems.at[1]),
    ]
    for copy in copies:
        copy.start()

    tiles = 2 * NO * NO // LANES
    for piece, ref in ((0, below2), (1, below1), (3, above1), (4, above2)):
        make_planes(ref, planes, piece * count)
    planes[2 * count : 3 * count] = middle_planes[...]

    for copy in copies:
        copy.wait()
    group = iota((HI, LANES), 1) // NO
    starts = []
    for phonon in range(NW):
        for sign in (1, -1):
            starts.append(2 * count - sign * offsets[phonon])

    def build(atom, carry):
        for e in range(count):
            turned = []
            for s in range(NS):
                part = planes[starts[s] + e, pl.ds(pl.multiple_of(atom * tiles, tiles), tiles), :]
                turned.append(
                    [part] + [pltpu.roll(part, r * NO, axis=1) for r in range(1, COPIES)]
                )
            for c in range(2):
                at = (e * 2 + c) * NO
                for half in range(2):
                    pieces = []
                    for q in range(COPIES):
                        total = None
                        for g in range(min(COPIES, NS - half * COPIES)):
                            part = turned[half * COPIES + g][(g - q) % COPIES][
                                c * HI : (c + 1) * HI
                            ]
                            total = part if total is None else jnp.where(group == g, part, total)
                        pieces.append(total)
                    blocks[atom, at : at + NO, half * LANES : (half + 1) * LANES] = (
                        jnp.concatenate(pieces, axis=0).astype(jnp.bfloat16)
                    )
        return carry

    lax.fori_loop(0, natoms, build, 0, unroll=4)

    groups = 2 * count
    wide = iota((NO, LANES), 1) // NO
    masks = [ones_where(wide == g) for g in range(groups)]

    def middles(pair):
        parts = [[] for _ in pair]
        for slot in range(NB):
            wide = lax.dot_general(
                jnp.concatenate([kernel[atom * NB + slot] for atom in pair], axis=0),
                jnp.concatenate([blocks[neighbours[slot, atom]] for atom in pair], axis=0),
                NT,
                preferred_element_type=jnp.float32,
            )
            for k in range(len(pair)):
                own = wide[
                    k * ND * NO : (k + 1) * ND * NO, k * groups * NO : (k + 1) * groups * NO
                ].astype(jnp.bfloat16)
                for i in range(ND):
                    block = own[i * NO : (i + 1) * NO, :]
                    parts[k].append(jnp.concatenate([block * mask for mask in masks], axis=0))
        return jnp.concatenate([jnp.concatenate(part, axis=1) for part in parts], axis=0)

    def sigmas(pair, right):
        left = jnp.concatenate(
            [
                jnp.concatenate(
                    [
                        derivs[atom * NB + slot, i * NO : (i + 1) * NO, :]
                        for slot in range(NB)
                        for i in range(ND)
                    ],
                    axis=1,
                )
                for atom in pair
            ],
            axis=0,
        )
        wide = lax.dot_general(left, right, NT, preferred_element_type=jnp.float32)
        placed = []
        for k in range(len(pair)):
            own = wide[k * NO : (k + 1) * NO, k * groups * NO : (k + 1) * groups * NO]
            rows = [own[q * HI : (q + 1) * HI, :] for q in range(COPIES)]
            for g in range(groups):
                total = None
                for q in range(COPIES):
                    shift = (q - g) % COPIES * NO
                    part = pltpu.roll(rows[q], shift, axis=1) if shift else rows[q]
                    total = part if total is None else jnp.where(group == q, part, total)
                placed.append(total)
        return placed

    row, col = iota((LANES, LANES), 0), iota((LANES, LANES), 1)
    unmix = ones_where((row // NO == col // NO) & (mixed(row % NO) == col % NO))
    shares = out.shape[0]
    share = natoms // shares
    pairs = [tuple(range(a, min(a + 2, natoms))) for a in range(0, natoms, 2)]
    placed = []
    step = 0
    ready = middles(pairs[0])
    for at, pair in enumerate(pairs):
        later = middles(pairs[at + 1]) if at + 1 < len(pairs) else None
        placed.extend(sigmas(pair, ready))
        ready = later
        while len(placed) >= share * groups:
            mine, placed = placed[: share * groups], placed[share * groups :]
            out[step] = exact_dot(
                jnp.concatenate(mine, axis=0).astype(jnp.bfloat16), unmix
            ).astype(jnp.bfloat16)
            step += 1


def sandwich(window, middle_planes, kernel, derivs, neighbours, offsets, shares):
    below2, below1, above1, above2 = window
    count, natoms, size = below2.shape
    groups = 2 * count
    rows = natoms * groups * HI
    return pl.pallas_call(
        functools.partial(sandwich_kernel, count, natoms),
        out_shape=jax.ShapeDtypeStruct((shares, rows // shares, LANES), jnp.bfloat16),
        in_specs=[pl.BlockSpec(memory_space=pltpu.HBM)] * 2
        + [pl.BlockSpec(memory_space=pltpu.VMEM)] * 7,
        out_specs=pl.BlockSpec(memory_space=pltpu.VMEM),
        scratch_shapes=[
            pltpu.SMEM(neighbours.shape, jnp.int32),
            pltpu.SMEM(offsets.shape, jnp.int32),
            pltpu.VMEM((5 * count, natoms * size // LANES, LANES), jnp.float32),
            pltpu.VMEM((natoms, groups * NO, 2 * LANES), jnp.bfloat16),
            pltpu.SemaphoreType.DMA((2,)),
        ],
        compiler_params=pltpu.CompilerParams(vmem_limit_bytes=VMEM_LIMIT),
        cost_estimate=pl.CostEstimate(
            flops=800_000_000, bytes_accessed=7_000_000, transcendentals=0
        ),
        name="sandwich",
    )(
        in_hbm(neighbours), in_hbm(offsets),
        middle_planes, below2, below1, above1, above2, kernel, derivs,
    )


def combine_kernel(parts, out, total):
    count, share, width = out.shape
    tiles = width // LANES
    summed = parts[0].astype(jnp.float32)
    for k in range(1, parts.shape[0]):
        summed = summed + parts[k].astype(jnp.float32)
    total[...] = summed
    for e in range(count):
        for t in range(tiles):
            out[e, :, t * LANES : (t + 1) * LANES] = total[
                pl.ds(e * tiles + t, share, stride=count * tiles), :
            ]


def combine(parts, count, share):
    return pl.pallas_call(
        combine_kernel,
        out_shape=jax.ShapeDtypeStruct((count, share, 2 * NO * NO), jnp.float32),
        in_specs=[pl.BlockSpec(memory_space=pltpu.VMEM)],
        out_specs=pl.BlockSpec(memory_space=pltpu.VMEM),
        scratch_shapes=[pltpu.VMEM(parts.shape[1:], jnp.float32)],
        name="combine",
    )(parts)


def shifted(array, axis, by):
    length = lax.axis_size(axis)
    pairs = [(i, i + by) for i in range(length) if 0 <= i + by < length]
    return lax.ppermute(array, axis, pairs)


def local_partial(window, coupling, gradient, neighbours, offsets, shares):
    below2, below1, local, above1, above2 = window
    kernel, derivs, planes = tables(
        local, gradient, coupling.reshape(-1, 1, coupling.shape[-1])
    )
    remote = (below2, below1, above1, above2)
    return sandwich(remote, planes, kernel, derivs, neighbours.T, offsets, shares)


def body(green, coupling, gradient, neighbours, offsets):
    local_block = green[0]
    count, natoms, _ = local_block.shape
    shares = lax.axis_size("mom")
    window = (
        shifted(local_block, "energy", 2),
        shifted(local_block, "energy", 1),
        local_block,
        shifted(local_block, "energy", -1),
        shifted(local_block, "energy", -2),
    )
    partial_terms = local_partial(window, coupling[0], gradient, neighbours, offsets, shares)
    parts = lax.all_to_all(partial_terms, "mom", 0, 0, tiled=True)
    return combine(parts, count, natoms // shares)


def solution(mesh):
    in_specs = (P("mom", "energy", None, None), P("mom", None, None, None, None), P(), P(), P())
    out_specs = P("energy", "mom", None)
    return jax.shard_map(body, mesh=mesh, in_specs=in_specs, out_specs=out_specs, check_vma=False)
```

```python
import functools

import jax
import jax.numpy as jnp
from jax import lax
from jax.experimental import pallas as pl
from jax.experimental.pallas import tpu as pltpu
from jax.sharding import PartitionSpec as P

NO = 32
NB = 5
NW = 3
NS = 2 * NW
ND = 3
LANES = 128
COPIES = LANES // NO
HI = NO // COPIES
VMEM_LIMIT = 40 * 1024 * 1024

NT = (((1,), (1,)), ((), ()))


def in_hbm(array):
    return pltpu.with_memory_space_constraint(array, pltpu.HBM)


def iota(shape, dim):
    return lax.broadcasted_iota(jnp.int32, shape, dim)


def ones_where(condition):
    return jnp.where(condition, 1.0, 0.0).astype(jnp.bfloat16)


def over(value, size):
    return value >> (size.bit_length() - 1) if size & (size - 1) == 0 else value // size


def rest(value, size):
    return value & (size - 1) if size & (size - 1) == 0 else value % size


def mixed(lane):
    return rest(lane, HI) * COPIES + over(lane, HI)


def fold_matrix():
    shape = (LANES, COPIES * LANES)
    row, col = iota(shape, 0), iota(shape, 1)
    return ones_where(row == over(col, LANES) * NO + mixed(rest(col, NO)))


def lane_matrix():
    row, col = iota((LANES, LANES), 0), iota((LANES, LANES), 1)
    return ones_where(row == (col - rest(col, NO)) + mixed(rest(col, NO)))


def row_matrix(tiles, natoms):
    size = tiles * natoms
    row, col = iota((size, size), 0), iota((size, size), 1)
    return ones_where(col == rest(row, tiles) * natoms + over(row, tiles))


def stack_tiles(flat):
    return jnp.concatenate(
        [flat[:, t : t + LANES] for t in range(0, flat.shape[1], LANES)], axis=0
    )


def exact_dot(left, right):
    return jnp.dot(left, right, preferred_element_type=jnp.float32)


def make_planes(block, planes, at, lanes, order):
    count = block.shape[0]
    mixes = [
        exact_dot(stack_tiles(block[e]), lanes).astype(jnp.bfloat16) for e in range(count)
    ]
    ordered = exact_dot(order, jnp.concatenate(mixes, axis=1))
    for e in range(count):
        planes[at + e] = ordered[:, e * LANES : (e + 1) * LANES]


def tables_kernel(
    natoms, local_hbm, gradient_hbm, coupling_hbm, kernel_out, derivs_out, planes_out,
    local, gradient, coupling, rows, sems,
):
    copies = [
        pltpu.make_async_copy(coupling_hbm.at[:, 0, :], coupling, sems.at[0]),
        pltpu.make_async_copy(gradient_hbm, gradient, sems.at[1]),
        pltpu.make_async_copy(local_hbm, local, sems.at[2]),
    ]
    for copy in copies:
        copy.start()

    tiles = NO * NO // LANES
    block = natoms * tiles
    cells = ND * ND * NB
    depth = rows.shape[2]
    width = -(-NS * cells // LANES) * LANES
    fold = fold_matrix()
    order = row_matrix(tiles, natoms)
    branch = over(iota((width, 2 * LANES), 1), NO)
    lane = iota((width, 2 * LANES), 0) - branch * cells
    widen = ones_where((lane >= 0) & (lane < cells) & (branch < NS))
    line, lane = iota((NB * depth, width), 0), iota((NB * depth, width), 1)
    lane = lane - (rest(line, depth) * NB + over(line, depth))
    chosen = lane == 0
    for s in range(1, NS):
        chosen = chosen | (lane == s * cells)

    copies[0].wait()
    table = jnp.transpose(coupling[...])
    table = jnp.concatenate(
        [table, jnp.zeros((natoms, width - NS * cells), jnp.float32)], axis=1
    )
    for atom in range(natoms):
        left = jnp.where(chosen, table[atom : atom + 1, :], 0.0).astype(jnp.bfloat16)
        wide = exact_dot(left, widen)
        for slot in range(NB):
            for half in range(2):
                rows[atom * NB + slot, half] = wide[
                    slot * depth : (slot + 1) * depth, half * LANES : (half + 1) * LANES
                ]

    copies[1].wait()
    flats = [stack_tiles(gradient[slot, j]) for slot in range(NB) for j in range(ND)]
    ordered = exact_dot(order, jnp.concatenate(flats, axis=1)).astype(jnp.bfloat16)
    for slot in range(NB):
        for j in range(ND):
            at = (slot * ND + j) * LANES
            wide = exact_dot(ordered[:, at : at + LANES], fold)
            for atom in range(natoms):
                derivs_out[atom * NB + slot, j * NO : (j + 1) * NO, :] = jnp.concatenate(
                    [
                        wide[atom * tiles : (atom + 1) * tiles, q * LANES : (q + 1) * LANES]
                        for q in range(COPIES)
                    ],
                    axis=0,
                ).astype(jnp.bfloat16)

    copies[2].wait()
    make_planes(local, planes_out, 0, lane_matrix(), row_matrix(2 * tiles, natoms))

    def one_cell(at, carry):
        derivs = [
            derivs_out[at, j * NO : (j + 1) * NO, :].astype(jnp.float32) for j in range(ND)
        ]
        for i in range(ND):
            for half in range(2):
                total = None
                for j in range(ND):
                    term = derivs[j] * rows[at, half, ND * i + j : ND * i + j + 1, :]
                    total = term if total is None else total + term
                kernel_out[at, i * NO : (i + 1) * NO, half * LANES : (half + 1) * LANES] = (
                    total.astype(jnp.bfloat16)
                )
        return carry

    lax.fori_loop(0, natoms * NB, one_cell, 0, unroll=4)


def tables(local, gradient, coupling):
    energies, natoms, size = local.shape
    count = NB * natoms
    return pl.pallas_call(
        functools.partial(tables_kernel, natoms),
        out_shape=(
            jax.ShapeDtypeStruct((count, ND * NO, 2 * LANES), jnp.bfloat16),
            jax.ShapeDtypeStruct((count, ND * NO, LANES), jnp.bfloat16),
            jax.ShapeDtypeStruct((energies, natoms * size // LANES, LANES), jnp.float32),
        ),
        in_specs=[pl.BlockSpec(memory_space=pltpu.HBM)] * 3,
        out_specs=[pl.BlockSpec(memory_space=pltpu.VMEM)] * 3,
        scratch_shapes=[
            pltpu.VMEM(local.shape, local.dtype),
            pltpu.VMEM(gradient.shape, gradient.dtype),
            pltpu.VMEM((coupling.shape[0], natoms), jnp.float32),
            pltpu.VMEM((count, 2, 2 * HI, LANES), jnp.float32),
            pltpu.SemaphoreType.DMA((3,)),
        ],
        compiler_params=pltpu.CompilerParams(vmem_limit_bytes=VMEM_LIMIT),
        cost_estimate=pl.CostEstimate(
            flops=200_000_000, bytes_accessed=6_000_000, transcendentals=0
        ),
        name="tables",
    )(in_hbm(local), in_hbm(gradient), in_hbm(coupling))


def sandwich_kernel(
    count, natoms, neighbours_hbm, offsets_hbm, middle_planes, below2, below1, above1, above2,
    kernel, derivs, out, neighbours, offsets, planes, blocks, sems,
):
    copies = [
        pltpu.make_async_copy(neighbours_hbm, neighbours, sems.at[0]),
        pltpu.make_async_copy(offsets_hbm, offsets, sems.at[1]),
    ]
    for copy in copies:
        copy.start()

    tiles = 2 * NO * NO // LANES
    lanes = lane_matrix()
    order = row_matrix(tiles, natoms)
    for piece, ref in ((0, below2), (1, below1), (3, above1), (4, above2)):
        make_planes(ref, planes, piece * count, lanes, order)
    planes[2 * count : 3 * count] = middle_planes[...]

    for copy in copies:
        copy.wait()
    group = over(iota((HI, LANES), 1), NO)
    starts = []
    for phonon in range(NW):
        for sign in (1, -1):
            starts.append(2 * count - sign * offsets[phonon])

    def build(atom, carry):
        for e in range(count):
            turned = []
            for s in range(NS):
                part = planes[starts[s] + e, pl.ds(pl.multiple_of(atom * tiles, tiles), tiles), :]
                turned.append(
                    [part] + [pltpu.roll(part, r * NO, axis=1) for r in range(1, COPIES)]
                )
            for c in range(2):
                at = (e * 2 + c) * NO
                for half in range(2):
                    pieces = []
                    for q in range(COPIES):
                        total = None
                        for g in range(min(COPIES, NS - half * COPIES)):
                            part = turned[half * COPIES + g][(g - q) % COPIES][
                                c * HI : (c + 1) * HI
                            ]
                            total = part if total is None else jnp.where(group == g, part, total)
                        pieces.append(total)
                    blocks[atom, at : at + NO, half * LANES : (half + 1) * LANES] = (
                        jnp.concatenate(pieces, axis=0).astype(jnp.bfloat16)
                    )
        return carry

    lax.fori_loop(0, natoms, build, 0, unroll=4)

    groups = 2 * count
    wide = over(iota((NO, LANES), 1), NO)
    masks = [ones_where(wide == g) for g in range(groups)]

    def middles(pair):
        parts = [[] for _ in pair]
        for slot in range(NB):
            wide = lax.dot_general(
                jnp.concatenate([kernel[atom * NB + slot] for atom in pair], axis=0),
                jnp.concatenate([blocks[neighbours[slot, atom]] for atom in pair], axis=0),
                NT,
                preferred_element_type=jnp.float32,
            )
            for k in range(len(pair)):
                own = wide[
                    k * ND * NO : (k + 1) * ND * NO, k * groups * NO : (k + 1) * groups * NO
                ].astype(jnp.bfloat16)
                for i in range(ND):
                    block = own[i * NO : (i + 1) * NO, :]
                    parts[k].append(jnp.concatenate([block * mask for mask in masks], axis=0))
        return jnp.concatenate([jnp.concatenate(part, axis=1) for part in parts], axis=0)

    def sigmas(pair, right):
        left = jnp.concatenate(
            [
                jnp.concatenate(
                    [
                        derivs[atom * NB + slot, i * NO : (i + 1) * NO, :]
                        for slot in range(NB)
                        for i in range(ND)
                    ],
                    axis=1,
                )
                for atom in pair
            ],
            axis=0,
        )
        wide = lax.dot_general(left, right, NT, preferred_element_type=jnp.float32)
        placed = []
        for k in range(len(pair)):
            own = wide[k * NO : (k + 1) * NO, k * groups * NO : (k + 1) * groups * NO]
            rows = [own[q * HI : (q + 1) * HI, :] for q in range(COPIES)]
            for g in range(groups):
                total = None
                for q in range(COPIES):
                    shift = (q - g) % COPIES * NO
                    part = pltpu.roll(rows[q], shift, axis=1) if shift else rows[q]
                    total = part if total is None else jnp.where(group == q, part, total)
                placed.append(total)
        return placed

    row, col = iota((LANES, LANES), 0), iota((LANES, LANES), 1)
    unmix = ones_where(col == (row - rest(row, NO)) + mixed(rest(row, NO)))
    shares = out.shape[0]
    share = natoms // shares
    pairs = [tuple(range(a, min(a + 2, natoms))) for a in range(0, natoms, 2)]
    placed = []
    step = 0
    ready = middles(pairs[0])
    for at, pair in enumerate(pairs):
        later = middles(pairs[at + 1]) if at + 1 < len(pairs) else None
        placed.extend(sigmas(pair, ready))
        ready = later
        while len(placed) >= share * groups:
            mine, placed = placed[: share * groups], placed[share * groups :]
            out[step] = exact_dot(
                jnp.concatenate(mine, axis=0).astype(jnp.bfloat16), unmix
            ).astype(jnp.bfloat16)
            step += 1


def sandwich(window, middle_planes, kernel, derivs, neighbours, offsets, shares):
    below2, below1, above1, above2 = window
    count, natoms, size = below2.shape
    groups = 2 * count
    rows = natoms * groups * HI
    return pl.pallas_call(
        functools.partial(sandwich_kernel, count, natoms),
        out_shape=jax.ShapeDtypeStruct((shares, rows // shares, LANES), jnp.bfloat16),
        in_specs=[pl.BlockSpec(memory_space=pltpu.HBM)] * 2
        + [pl.BlockSpec(memory_space=pltpu.VMEM)] * 7,
        out_specs=pl.BlockSpec(memory_space=pltpu.VMEM),
        scratch_shapes=[
            pltpu.SMEM(neighbours.shape, jnp.int32),
            pltpu.SMEM(offsets.shape, jnp.int32),
            pltpu.VMEM((5 * count, natoms * size // LANES, LANES), jnp.float32),
            pltpu.VMEM((natoms, groups * NO, 2 * LANES), jnp.bfloat16),
            pltpu.SemaphoreType.DMA((2,)),
        ],
        compiler_params=pltpu.CompilerParams(vmem_limit_bytes=VMEM_LIMIT),
        cost_estimate=pl.CostEstimate(
            flops=800_000_000, bytes_accessed=7_000_000, transcendentals=0
        ),
        name="sandwich",
    )(
        in_hbm(neighbours), in_hbm(offsets),
        middle_planes, below2, below1, above1, above2, kernel, derivs,
    )


def combine_kernel(parts, out, total):
    count, share, width = out.shape
    tiles = width // LANES
    summed = parts[0].astype(jnp.float32)
    for k in range(1, parts.shape[0]):
        summed = summed + parts[k].astype(jnp.float32)
    total[...] = summed
    for e in range(count):
        for t in range(tiles):
            out[e, :, t * LANES : (t + 1) * LANES] = total[
                pl.ds(e * tiles + t, share, stride=count * tiles), :
            ]


def combine(parts, count, share):
    return pl.pallas_call(
        combine_kernel,
        out_shape=jax.ShapeDtypeStruct((count, share, 2 * NO * NO), jnp.float32),
        in_specs=[pl.BlockSpec(memory_space=pltpu.VMEM)],
        out_specs=pl.BlockSpec(memory_space=pltpu.VMEM),
        scratch_shapes=[pltpu.VMEM(parts.shape[1:], jnp.float32)],
        name="combine",
    )(parts)


def shifted(array, axis, by):
    length = lax.axis_size(axis)
    pairs = [(i, i + by) for i in range(length) if 0 <= i + by < length]
    return lax.ppermute(array, axis, pairs)


def local_partial(window, coupling, gradient, neighbours, offsets, shares):
    below2, below1, local, above1, above2 = window
    kernel, derivs, planes = tables(
        local, gradient, coupling.reshape(-1, 1, coupling.shape[-1])
    )
    remote = (below2, below1, above1, above2)
    return sandwich(remote, planes, kernel, derivs, neighbours.T, offsets, shares)


def body(green, coupling, gradient, neighbours, offsets):
    local_block = green[0]
    count, natoms, _ = local_block.shape
    shares = lax.axis_size("mom")
    window = (
        shifted(local_block, "energy", 2),
        shifted(local_block, "energy", 1),
        local_block,
        shifted(local_block, "energy", -1),
        shifted(local_block, "energy", -2),
    )
    partial_terms = local_partial(window, coupling[0], gradient, neighbours, offsets, shares)
    parts = lax.all_to_all(partial_terms, "mom", 0, 0, tiled=True)
    return combine(parts, count, natoms // shares)


def solution(mesh):
    in_specs = (P("mom", "energy", None, None), P("mom", None, None, None, None), P(), P(), P())
    out_specs = P("energy", "mom", None)
    return jax.shard_map(body, mesh=mesh, in_specs=in_specs, out_specs=out_specs, check_vma=False)
```

```python
import functools

import jax
import jax.numpy as jnp
from jax import lax
from jax.experimental import pallas as pl
from jax.experimental.pallas import tpu as pltpu
from jax.sharding import PartitionSpec as P

NO = 32
NB = 5
NW = 3
NS = 2 * NW
ND = 3
LANES = 128
COPIES = LANES // NO
HI = NO // COPIES
VMEM_LIMIT = 40 * 1024 * 1024

NT = (((1,), (1,)), ((), ()))


def in_hbm(array):
    return pltpu.with_memory_space_constraint(array, pltpu.HBM)


def iota(shape, dim):
    return lax.broadcasted_iota(jnp.int32, shape, dim)


def ones_where(condition):
    return jnp.where(condition, 1.0, 0.0).astype(jnp.bfloat16)


def over(value, size):
    return value >> (size.bit_length() - 1) if size & (size - 1) == 0 else value // size


def rest(value, size):
    return value & (size - 1) if size & (size - 1) == 0 else value % size


def mixed(lane):
    return rest(lane, HI) * COPIES + over(lane, HI)


def group_of(lane):
    return over(lane, 2 * NO) * 2 + rest(over(lane, HI), 2)


def orbital_of(lane):
    return rest(lane, HI) * COPIES + rest(over(lane, 2 * HI), COPIES)


def fold_matrix():
    shape = (LANES, COPIES * LANES)
    row, col = iota(shape, 0), iota(shape, 1)
    return ones_where(row == over(col, LANES) * NO + orbital_of(rest(col, LANES)))


def row_matrix(tiles, natoms):
    size = tiles * natoms
    row, col = iota((size, size), 0), iota((size, size), 1)
    return ones_where(col == rest(row, tiles) * natoms + over(row, tiles))


def stack_tiles(flat):
    return jnp.concatenate(
        [flat[:, t : t + LANES] for t in range(0, flat.shape[1], LANES)], axis=0
    )


def exact_dot(left, right):
    return jnp.dot(left, right, preferred_element_type=jnp.float32)


def make_planes(block, planes, at, order):
    count = block.shape[0]
    ordered = exact_dot(
        order, jnp.concatenate([stack_tiles(block[e]) for e in range(count)], axis=1)
    ).astype(jnp.bfloat16)
    for e in range(count):
        planes[at + e] = ordered[:, e * LANES : (e + 1) * LANES]


def tables_kernel(
    natoms, local_hbm, gradient_hbm, coupling_hbm, kernel_out, derivs_out, planes_out,
    local, gradient, coupling, rows, sems,
):
    copies = [
        pltpu.make_async_copy(coupling_hbm.at[:, 0, :], coupling, sems.at[0]),
        pltpu.make_async_copy(gradient_hbm, gradient, sems.at[1]),
        pltpu.make_async_copy(local_hbm, local, sems.at[2]),
    ]
    for copy in copies:
        copy.start()

    tiles = NO * NO // LANES
    block = natoms * tiles
    cells = ND * ND * NB
    depth = rows.shape[2]
    width = -(-NS * cells // LANES) * LANES
    fold = fold_matrix()
    order = row_matrix(tiles, natoms)
    lane = iota((width, 2 * LANES), 1)
    branch = over(lane, LANES) * COPIES + group_of(rest(lane, LANES))
    lane = iota((width, 2 * LANES), 0) - branch * cells
    widen = ones_where((lane >= 0) & (lane < cells) & (branch < NS))
    line, lane = iota((NB * depth, width), 0), iota((NB * depth, width), 1)
    lane = lane - (rest(line, depth) * NB + over(line, depth))
    chosen = lane == 0
    for s in range(1, NS):
        chosen = chosen | (lane == s * cells)

    copies[0].wait()
    table = jnp.transpose(coupling[...])
    table = jnp.concatenate(
        [table, jnp.zeros((natoms, width - NS * cells), jnp.float32)], axis=1
    )
    for atom in range(natoms):
        left = jnp.where(chosen, table[atom : atom + 1, :], 0.0).astype(jnp.bfloat16)
        wide = exact_dot(left, widen)
        for slot in range(NB):
            for half in range(2):
                rows[atom * NB + slot, half] = wide[
                    slot * depth : (slot + 1) * depth, half * LANES : (half + 1) * LANES
                ]

    copies[1].wait()
    flats = [stack_tiles(gradient[slot, j]) for slot in range(NB) for j in range(ND)]
    ordered = exact_dot(order, jnp.concatenate(flats, axis=1)).astype(jnp.bfloat16)
    for slot in range(NB):
        for j in range(ND):
            at = (slot * ND + j) * LANES
            wide = exact_dot(ordered[:, at : at + LANES], fold)
            for atom in range(natoms):
                derivs_out[atom * NB + slot, j * NO : (j + 1) * NO, :] = jnp.concatenate(
                    [
                        wide[atom * tiles : (atom + 1) * tiles, q * LANES : (q + 1) * LANES]
                        for q in range(COPIES)
                    ],
                    axis=0,
                ).astype(jnp.bfloat16)

    copies[2].wait()
    make_planes(local, planes_out, 0, row_matrix(2 * tiles, natoms))

    def one_cell(at, carry):
        derivs = [
            derivs_out[at, j * NO : (j + 1) * NO, :].astype(jnp.float32) for j in range(ND)
        ]
        for i in range(ND):
            for half in range(2):
                total = None
                for j in range(ND):
                    term = derivs[j] * rows[at, half, ND * i + j : ND * i + j + 1, :]
                    total = term if total is None else total + term
                kernel_out[at, i * NO : (i + 1) * NO, half * LANES : (half + 1) * LANES] = (
                    total.astype(jnp.bfloat16)
                )
        return carry

    lax.fori_loop(0, natoms * NB, one_cell, 0, unroll=4)


def tables(local, gradient, coupling):
    energies, natoms, size = local.shape
    count = NB * natoms
    return pl.pallas_call(
        functools.partial(tables_kernel, natoms),
        out_shape=(
            jax.ShapeDtypeStruct((count, ND * NO, 2 * LANES), jnp.bfloat16),
            jax.ShapeDtypeStruct((count, ND * NO, LANES), jnp.bfloat16),
            jax.ShapeDtypeStruct((energies, natoms * size // LANES, LANES), jnp.bfloat16),
        ),
        in_specs=[pl.BlockSpec(memory_space=pltpu.HBM)] * 3,
        out_specs=[pl.BlockSpec(memory_space=pltpu.VMEM)] * 3,
        scratch_shapes=[
            pltpu.VMEM(local.shape, local.dtype),
            pltpu.VMEM(gradient.shape, gradient.dtype),
            pltpu.VMEM((coupling.shape[0], natoms), jnp.float32),
            pltpu.VMEM((count, 2, 2 * HI, LANES), jnp.float32),
            pltpu.SemaphoreType.DMA((3,)),
        ],
        compiler_params=pltpu.CompilerParams(vmem_limit_bytes=VMEM_LIMIT),
        cost_estimate=pl.CostEstimate(
            flops=200_000_000, bytes_accessed=6_000_000, transcendentals=0
        ),
        name="tables",
    )(in_hbm(local), in_hbm(gradient), in_hbm(coupling))


def sandwich_kernel(
    count, natoms, neighbours_hbm, offsets_hbm, middle_planes, below2, below1, above1, above2,
    kernel, derivs, out, neighbours, offsets, planes, blocks, sems,
):
    copies = [
        pltpu.make_async_copy(neighbours_hbm, neighbours, sems.at[0]),
        pltpu.make_async_copy(offsets_hbm, offsets, sems.at[1]),
    ]
    for copy in copies:
        copy.start()

    tiles = 2 * NO * NO // LANES
    groups = 2 * count
    order = row_matrix(tiles, natoms)
    for piece, ref in ((0, below2), (1, below1), (3, above1), (4, above2)):
        make_planes(ref, planes, piece * count, order)
    planes[2 * count : 3 * count] = middle_planes[...]

    fold = fold_matrix()
    group = group_of(rest(iota(fold.shape, 1), LANES))
    places = [fold * ones_where(group == g) for g in range(COPIES)]
    for copy in copies:
        copy.wait()
    for e in range(count):
        for half in range(2):
            branches = range(half * COPIES, min(NS, (half + 1) * COPIES))
            shifted_planes = [
                planes[2 * count + e - (1 - 2 * (s % 2)) * offsets[s // 2]] for s in branches
            ]
            wide = exact_dot(
                jnp.concatenate(shifted_planes, axis=1),
                jnp.concatenate(places[: len(branches)], axis=0),
            ).astype(jnp.bfloat16)
            for atom in range(natoms):
                for q in range(COPIES):
                    at = (e * COPIES + q) * tiles
                    blocks[atom, at : at + tiles, half * LANES : (half + 1) * LANES] = wide[
                        atom * tiles : (atom + 1) * tiles, q * LANES : (q + 1) * LANES
                    ]

    lane_group = group_of(iota((NO, LANES), 1))
    masks = [ones_where(lane_group == g) for g in range(groups)]
    group = over(iota((HI, LANES), 1), NO)

    def middles(pair):
        parts = [[] for _ in pair]
        for slot in range(NB):
            wide = lax.dot_general(
                jnp.concatenate([kernel[atom * NB + slot] for atom in pair], axis=0),
                jnp.concatenate([blocks[neighbours[slot, atom]] for atom in pair], axis=0),
                NT,
                preferred_element_type=jnp.float32,
            )
            for k in range(len(pair)):
                own = wide[
                    k * ND * NO : (k + 1) * ND * NO, k * groups * NO : (k + 1) * groups * NO
                ].astype(jnp.bfloat16)
                for i in range(ND):
                    block = own[i * NO : (i + 1) * NO, :]
                    parts[k].append(jnp.concatenate([block * mask for mask in masks], axis=0))
        return jnp.concatenate([jnp.concatenate(part, axis=1) for part in parts], axis=0)

    def sigmas(pair, right):
        left = jnp.concatenate(
            [
                jnp.concatenate(
                    [
                        derivs[atom * NB + slot, i * NO : (i + 1) * NO, :]
                        for slot in range(NB)
                        for i in range(ND)
                    ],
                    axis=1,
                )
                for atom in pair
            ],
            axis=0,
        )
        wide = lax.dot_general(left, right, NT, preferred_element_type=jnp.float32)
        placed = []
        for k in range(len(pair)):
            own = wide[k * NO : (k + 1) * NO, k * groups * NO : (k + 1) * groups * NO]
            rows = [own[q * HI : (q + 1) * HI, :] for q in range(COPIES)]
            for g in range(groups):
                total = None
                for q in range(COPIES):
                    shift = (q - g) % COPIES * NO
                    part = pltpu.roll(rows[q], shift, axis=1) if shift else rows[q]
                    total = part if total is None else jnp.where(group == q, part, total)
                placed.append(total)
        return placed

    row, col = iota((LANES, LANES), 0), iota((LANES, LANES), 1)
    unmix = ones_where(col == (row - rest(row, NO)) + mixed(rest(row, NO)))
    shares = out.shape[0]
    share = natoms // shares
    pairs = [tuple(range(a, min(a + 2, natoms))) for a in range(0, natoms, 2)]
    placed = []
    step = 0
    ready = middles(pairs[0])
    for at, pair in enumerate(pairs):
        later = middles(pairs[at + 1]) if at + 1 < len(pairs) else None
        placed.extend(sigmas(pair, ready))
        ready = later
        while len(placed) >= share * groups:
            mine, placed = placed[: share * groups], placed[share * groups :]
            out[step] = exact_dot(
                jnp.concatenate(mine, axis=0).astype(jnp.bfloat16), unmix
            ).astype(jnp.bfloat16)
            step += 1


def sandwich(window, middle_planes, kernel, derivs, neighbours, offsets, shares):
    below2, below1, above1, above2 = window
    count, natoms, size = below2.shape
    groups = 2 * count
    rows = natoms * groups * HI
    return pl.pallas_call(
        functools.partial(sandwich_kernel, count, natoms),
        out_shape=jax.ShapeDtypeStruct((shares, rows // shares, LANES), jnp.bfloat16),
        in_specs=[pl.BlockSpec(memory_space=pltpu.HBM)] * 2
        + [pl.BlockSpec(memory_space=pltpu.VMEM)] * 7,
        out_specs=pl.BlockSpec(memory_space=pltpu.VMEM),
        scratch_shapes=[
            pltpu.SMEM(neighbours.shape, jnp.int32),
            pltpu.SMEM(offsets.shape, jnp.int32),
            pltpu.VMEM((5 * count, natoms * size // LANES, LANES), jnp.bfloat16),
            pltpu.VMEM((natoms, groups * NO, 2 * LANES), jnp.bfloat16),
            pltpu.SemaphoreType.DMA((2,)),
        ],
        compiler_params=pltpu.CompilerParams(vmem_limit_bytes=VMEM_LIMIT),
        cost_estimate=pl.CostEstimate(
            flops=800_000_000, bytes_accessed=7_000_000, transcendentals=0
        ),
        name="sandwich",
    )(
        in_hbm(neighbours), in_hbm(offsets),
        middle_planes, below2, below1, above1, above2, kernel, derivs,
    )


def combine_kernel(parts, out, total):
    count, share, width = out.shape
    tiles = width // LANES
    summed = parts[0].astype(jnp.float32)
    for k in range(1, parts.shape[0]):
        summed = summed + parts[k].astype(jnp.float32)
    total[...] = summed
    for e in range(count):
        for t in range(tiles):
            out[e, :, t * LANES : (t + 1) * LANES] = total[
                pl.ds(e * tiles + t, share, stride=count * tiles), :
            ]


def combine(parts, count, share):
    return pl.pallas_call(
        combine_kernel,
        out_shape=jax.ShapeDtypeStruct((count, share, 2 * NO * NO), jnp.float32),
        in_specs=[pl.BlockSpec(memory_space=pltpu.VMEM)],
        out_specs=pl.BlockSpec(memory_space=pltpu.VMEM),
        scratch_shapes=[pltpu.VMEM(parts.shape[1:], jnp.float32)],
        name="combine",
    )(parts)


def shifted(array, axis, by):
    length = lax.axis_size(axis)
    pairs = [(i, i + by) for i in range(length) if 0 <= i + by < length]
    return lax.ppermute(array, axis, pairs)


def local_partial(window, coupling, gradient, neighbours, offsets, shares):
    below2, below1, local, above1, above2 = window
    kernel, derivs, planes = tables(
        local, gradient, coupling.reshape(-1, 1, coupling.shape[-1])
    )
    remote = (below2, below1, above1, above2)
    return sandwich(remote, planes, kernel, derivs, neighbours.T, offsets, shares)


def body(green, coupling, gradient, neighbours, offsets):
    local_block = green[0]
    count, natoms, _ = local_block.shape
    shares = lax.axis_size("mom")
    window = (
        shifted(local_block, "energy", 2),
        shifted(local_block, "energy", 1),
        local_block,
        shifted(local_block, "energy", -1),
        shifted(local_block, "energy", -2),
    )
    partial_terms = local_partial(window, coupling[0], gradient, neighbours, offsets, shares)
    parts = lax.all_to_all(partial_terms, "mom", 0, 0, tiled=True)
    return combine(parts, count, natoms // shares)


def solution(mesh):
    in_specs = (P("mom", "energy", None, None), P("mom", None, None, None, None), P(), P(), P())
    out_specs = P("energy", "mom", None)
    return jax.shard_map(body, mesh=mesh, in_specs=in_specs, out_specs=out_specs, check_vma=False)
```

```python
import functools

import jax
import jax.numpy as jnp
from jax import lax
from jax.experimental import pallas as pl
from jax.experimental.pallas import tpu as pltpu
from jax.sharding import PartitionSpec as P

NO = 32
NB = 5
NW = 3
NS = 2 * NW
ND = 3
LANES = 128
COPIES = LANES // NO
HI = NO // COPIES
VMEM_LIMIT = 40 * 1024 * 1024

NT = (((1,), (1,)), ((), ()))


def in_hbm(array):
    return pltpu.with_memory_space_constraint(array, pltpu.HBM)


def iota(shape, dim):
    return lax.broadcasted_iota(jnp.int32, shape, dim)


def ones_where(condition):
    return jnp.where(condition, 1.0, 0.0).astype(jnp.bfloat16)


def over(value, size):
    return value >> (size.bit_length() - 1) if size & (size - 1) == 0 else value // size


def rest(value, size):
    return value & (size - 1) if size & (size - 1) == 0 else value % size


def mixed(lane):
    return rest(lane, HI) * COPIES + over(lane, HI)


def group_of(lane):
    return over(lane, 2 * NO) * 2 + rest(over(lane, HI), 2)


def orbital_of(lane):
    return rest(lane, HI) * COPIES + rest(over(lane, 2 * HI), COPIES)


def fold_matrix():
    shape = (LANES, COPIES * LANES)
    row, col = iota(shape, 0), iota(shape, 1)
    return ones_where(row == over(col, LANES) * NO + orbital_of(rest(col, LANES)))


def row_matrix(tiles, natoms):
    size = tiles * natoms
    row, col = iota((size, size), 0), iota((size, size), 1)
    return ones_where(col == rest(row, tiles) * natoms + over(row, tiles))


def stack_tiles(flat):
    return jnp.concatenate(
        [flat[:, t : t + LANES] for t in range(0, flat.shape[1], LANES)], axis=0
    )


def exact_dot(left, right):
    return jnp.dot(left, right, preferred_element_type=jnp.float32)


def make_planes(block, planes, at, order):
    count = block.shape[0]
    ordered = exact_dot(
        order, jnp.concatenate([stack_tiles(block[e]) for e in range(count)], axis=1)
    ).astype(jnp.bfloat16)
    for e in range(count):
        planes[at + e] = ordered[:, e * LANES : (e + 1) * LANES]


def tables_kernel(
    natoms, local_hbm, gradient_hbm, coupling_hbm, kernel_out, derivs_out, planes_out,
    local, gradient, coupling, rows, sems,
):
    copies = [
        pltpu.make_async_copy(coupling_hbm.at[:, 0, :], coupling, sems.at[0]),
        pltpu.make_async_copy(gradient_hbm, gradient, sems.at[1]),
        pltpu.make_async_copy(local_hbm, local, sems.at[2]),
    ]
    for copy in copies:
        copy.start()

    tiles = NO * NO // LANES
    block = natoms * tiles
    cells = ND * ND * NB
    depth = rows.shape[2]
    width = -(-NS * cells // LANES) * LANES
    fold = fold_matrix()
    order = row_matrix(tiles, natoms)
    lane = iota((width, 2 * LANES), 1)
    branch = over(lane, LANES) * COPIES + group_of(rest(lane, LANES))
    lane = iota((width, 2 * LANES), 0) - branch * cells
    widen = ones_where((lane >= 0) & (lane < cells) & (branch < NS))
    line, lane = iota((NB * depth, width), 0), iota((NB * depth, width), 1)
    lane = lane - (rest(line, depth) * NB + over(line, depth))
    chosen = lane == 0
    for s in range(1, NS):
        chosen = chosen | (lane == s * cells)

    copies[0].wait()
    table = jnp.transpose(coupling[...])
    table = jnp.concatenate(
        [table, jnp.zeros((natoms, width - NS * cells), jnp.float32)], axis=1
    )
    for atom in range(natoms):
        left = jnp.where(chosen, table[atom : atom + 1, :], 0.0).astype(jnp.bfloat16)
        wide = exact_dot(left, widen)
        for slot in range(NB):
            for half in range(2):
                rows[atom * NB + slot, half] = wide[
                    slot * depth : (slot + 1) * depth, half * LANES : (half + 1) * LANES
                ]

    copies[1].wait()
    flats = [stack_tiles(gradient[slot, j]) for slot in range(NB) for j in range(ND)]
    ordered = exact_dot(order, jnp.concatenate(flats, axis=1)).astype(jnp.bfloat16)
    for slot in range(NB):
        for j in range(ND):
            at = (slot * ND + j) * LANES
            wide = exact_dot(ordered[:, at : at + LANES], fold)
            for atom in range(natoms):
                derivs_out[atom * NB + slot, j * NO : (j + 1) * NO, :] = jnp.concatenate(
                    [
                        wide[atom * tiles : (atom + 1) * tiles, q * LANES : (q + 1) * LANES]
                        for q in range(COPIES)
                    ],
                    axis=0,
                ).astype(jnp.bfloat16)

    copies[2].wait()
    make_planes(local, planes_out, 0, row_matrix(2 * tiles, natoms))

    def one_cell(at, carry):
        derivs = [
            derivs_out[at, j * NO : (j + 1) * NO, :].astype(jnp.float32) for j in range(ND)
        ]
        for i in range(ND):
            for half in range(2):
                total = None
                for j in range(ND):
                    term = derivs[j] * rows[at, half, ND * i + j : ND * i + j + 1, :]
                    total = term if total is None else total + term
                kernel_out[at, i * NO : (i + 1) * NO, half * LANES : (half + 1) * LANES] = (
                    total.astype(jnp.bfloat16)
                )
        return carry

    lax.fori_loop(0, natoms * NB, one_cell, 0, unroll=4)


def tables(local, gradient, coupling):
    energies, natoms, size = local.shape
    count = NB * natoms
    return pl.pallas_call(
        functools.partial(tables_kernel, natoms),
        out_shape=(
            jax.ShapeDtypeStruct((count, ND * NO, 2 * LANES), jnp.bfloat16),
            jax.ShapeDtypeStruct((count, ND * NO, LANES), jnp.bfloat16),
            jax.ShapeDtypeStruct((energies, natoms * size // LANES, LANES), jnp.bfloat16),
        ),
        in_specs=[pl.BlockSpec(memory_space=pltpu.HBM)] * 3,
        out_specs=[pl.BlockSpec(memory_space=pltpu.VMEM)] * 3,
        scratch_shapes=[
            pltpu.VMEM(local.shape, local.dtype),
            pltpu.VMEM(gradient.shape, gradient.dtype),
            pltpu.VMEM((coupling.shape[0], natoms), jnp.float32),
            pltpu.VMEM((count, 2, 2 * HI, LANES), jnp.float32),
            pltpu.SemaphoreType.DMA((3,)),
        ],
        compiler_params=pltpu.CompilerParams(vmem_limit_bytes=VMEM_LIMIT),
        cost_estimate=pl.CostEstimate(
            flops=200_000_000, bytes_accessed=6_000_000, transcendentals=0
        ),
        name="tables",
    )(in_hbm(local), in_hbm(gradient), in_hbm(coupling))


def sandwich_kernel(
    count, natoms, neighbours_hbm, offsets_hbm, middle_planes, below2, below1, above1, above2,
    kernel, derivs, out, neighbours, offsets, planes, blocks, sems,
):
    copies = [
        pltpu.make_async_copy(neighbours_hbm, neighbours, sems.at[0]),
        pltpu.make_async_copy(offsets_hbm, offsets, sems.at[1]),
    ]
    for copy in copies:
        copy.start()

    tiles = 2 * NO * NO // LANES
    groups = 2 * count
    order = row_matrix(tiles, natoms)
    for piece, ref in ((0, below2), (1, below1), (3, above1), (4, above2)):
        make_planes(ref, planes, piece * count, order)
    planes[2 * count : 3 * count] = middle_planes[...]

    fold = fold_matrix()
    group = group_of(rest(iota(fold.shape, 1), LANES))
    places = [fold * ones_where(group == g) for g in range(COPIES)]
    for copy in copies:
        copy.wait()
    for e in range(count):
        for half in range(2):
            branches = range(half * COPIES, min(NS, (half + 1) * COPIES))
            shifted_planes = [
                planes[2 * count + e - (1 - 2 * (s % 2)) * offsets[s // 2]] for s in branches
            ]
            wide = exact_dot(
                jnp.concatenate(shifted_planes, axis=1),
                jnp.concatenate(places[: len(branches)], axis=0),
            ).astype(jnp.bfloat16)
            for atom in range(natoms):
                for q in range(COPIES):
                    at = (e * COPIES + q) * tiles
                    blocks[atom, at : at + tiles, half * LANES : (half + 1) * LANES] = wide[
                        atom * tiles : (atom + 1) * tiles, q * LANES : (q + 1) * LANES
                    ]

    lane_group = group_of(iota((NO, LANES), 1))
    masks = [ones_where(lane_group == g) for g in range(groups)]
    group = over(iota((HI, LANES), 1), NO)

    def middles(pair):
        parts = [[] for _ in pair]
        for slot in range(NB):
            wide = lax.dot_general(
                jnp.concatenate([kernel[atom * NB + slot] for atom in pair], axis=0),
                jnp.concatenate([blocks[neighbours[slot, atom]] for atom in pair], axis=0),
                NT,
                preferred_element_type=jnp.float32,
            )
            for k in range(len(pair)):
                own = wide[
                    k * ND * NO : (k + 1) * ND * NO, k * groups * NO : (k + 1) * groups * NO
                ].astype(jnp.bfloat16)
                for i in range(ND):
                    block = own[i * NO : (i + 1) * NO, :]
                    parts[k].append(jnp.concatenate([block * mask for mask in masks], axis=0))
        return jnp.concatenate([jnp.concatenate(part, axis=1) for part in parts], axis=0)

    def sigmas(pair, right):
        left = jnp.concatenate(
            [
                jnp.concatenate(
                    [
                        derivs[atom * NB + slot, i * NO : (i + 1) * NO, :]
                        for slot in range(NB)
                        for i in range(ND)
                    ],
                    axis=1,
                )
                for atom in pair
            ],
            axis=0,
        )
        wide = lax.dot_general(left, right, NT, preferred_element_type=jnp.float32)
        placed = []
        for k in range(len(pair)):
            own = wide[k * NO : (k + 1) * NO, k * groups * NO : (k + 1) * groups * NO]
            rows = [own[q * HI : (q + 1) * HI, :] for q in range(COPIES)]
            for g in range(groups):
                total = None
                for q in range(COPIES):
                    shift = (q - g) % COPIES * NO
                    part = pltpu.roll(rows[q], shift, axis=1) if shift else rows[q]
                    total = part if total is None else jnp.where(group == q, part, total)
                placed.append(total)
        return placed

    row, col = iota((LANES, LANES), 0), iota((LANES, LANES), 1)
    unmix = ones_where(col == (row - rest(row, NO)) + mixed(rest(row, NO)))
    shares = out.shape[0]
    share = natoms // shares

    def one_share(step, carry):
        atoms = [step * share + k for k in range(share)]
        pairs = [atoms[k : k + 2] for k in range(0, share, 2)]
        placed = []
        for pair, right in zip(pairs, [middles(pair) for pair in pairs]):
            placed.extend(sigmas(pair, right))
        out[step] = exact_dot(
            jnp.concatenate(placed, axis=0).astype(jnp.bfloat16), unmix
        ).astype(jnp.bfloat16)
        return carry

    lax.fori_loop(0, shares, one_share, 0)


def sandwich(window, middle_planes, kernel, derivs, neighbours, offsets, shares):
    below2, below1, above1, above2 = window
    count, natoms, size = below2.shape
    groups = 2 * count
    rows = natoms * groups * HI
    return pl.pallas_call(
        functools.partial(sandwich_kernel, count, natoms),
        out_shape=jax.ShapeDtypeStruct((shares, rows // shares, LANES), jnp.bfloat16),
        in_specs=[pl.BlockSpec(memory_space=pltpu.HBM)] * 2
        + [pl.BlockSpec(memory_space=pltpu.VMEM)] * 7,
        out_specs=pl.BlockSpec(memory_space=pltpu.VMEM),
        scratch_shapes=[
            pltpu.SMEM(neighbours.shape, jnp.int32),
            pltpu.SMEM(offsets.shape, jnp.int32),
            pltpu.VMEM((5 * count, natoms * size // LANES, LANES), jnp.bfloat16),
            pltpu.VMEM((natoms, groups * NO, 2 * LANES), jnp.bfloat16),
            pltpu.SemaphoreType.DMA((2,)),
        ],
        compiler_params=pltpu.CompilerParams(vmem_limit_bytes=VMEM_LIMIT),
        cost_estimate=pl.CostEstimate(
            flops=800_000_000, bytes_accessed=7_000_000, transcendentals=0
        ),
        name="sandwich",
    )(
        in_hbm(neighbours), in_hbm(offsets),
        middle_planes, below2, below1, above1, above2, kernel, derivs,
    )


def combine_kernel(parts, out, total):
    count, share, width = out.shape
    tiles = width // LANES
    summed = parts[0].astype(jnp.float32)
    for k in range(1, parts.shape[0]):
        summed = summed + parts[k].astype(jnp.float32)
    total[...] = summed
    for e in range(count):
        for t in range(tiles):
            out[e, :, t * LANES : (t + 1) * LANES] = total[
                pl.ds(e * tiles + t, share, stride=count * tiles), :
            ]


def combine(parts, count, share):
    return pl.pallas_call(
        combine_kernel,
        out_shape=jax.ShapeDtypeStruct((count, share, 2 * NO * NO), jnp.float32),
        in_specs=[pl.BlockSpec(memory_space=pltpu.VMEM)],
        out_specs=pl.BlockSpec(memory_space=pltpu.VMEM),
        scratch_shapes=[pltpu.VMEM(parts.shape[1:], jnp.float32)],
        name="combine",
    )(parts)


def shifted(array, axis, by):
    length = lax.axis_size(axis)
    pairs = [(i, i + by) for i in range(length) if 0 <= i + by < length]
    return lax.ppermute(array, axis, pairs)


def local_partial(window, coupling, gradient, neighbours, offsets, shares):
    below2, below1, local, above1, above2 = window
    kernel, derivs, planes = tables(
        local, gradient, coupling.reshape(-1, 1, coupling.shape[-1])
    )
    remote = (below2, below1, above1, above2)
    return sandwich(remote, planes, kernel, derivs, neighbours.T, offsets, shares)


def body(green, coupling, gradient, neighbours, offsets):
    local_block = green[0]
    count, natoms, _ = local_block.shape
    shares = lax.axis_size("mom")
    window = (
        shifted(local_block, "energy", 2),
        shifted(local_block, "energy", 1),
        local_block,
        shifted(local_block, "energy", -1),
        shifted(local_block, "energy", -2),
    )
    partial_terms = local_partial(window, coupling[0], gradient, neighbours, offsets, shares)
    parts = lax.all_to_all(partial_terms, "mom", 0, 0, tiled=True)
    return combine(parts, count, natoms // shares)


def solution(mesh):
    in_specs = (P("mom", "energy", None, None), P("mom", None, None, None, None), P(), P(), P())
    out_specs = P("energy", "mom", None)
    return jax.shard_map(body, mesh=mesh, in_specs=in_specs, out_specs=out_specs, check_vma=False)
```

```python
import functools

import jax
import jax.numpy as jnp
from jax import lax
from jax.experimental import pallas as pl
from jax.experimental.pallas import tpu as pltpu
from jax.sharding import PartitionSpec as P

NO = 32
NB = 5
NW = 3
NS = 2 * NW
ND = 3
LANES = 128
COPIES = LANES // NO
HI = NO // COPIES
VMEM_LIMIT = 40 * 1024 * 1024

NT = (((1,), (1,)), ((), ()))


def in_hbm(array):
    return pltpu.with_memory_space_constraint(array, pltpu.HBM)


def iota(shape, dim):
    return lax.broadcasted_iota(jnp.int32, shape, dim)


def ones_where(condition):
    return jnp.where(condition, 1.0, 0.0).astype(jnp.bfloat16)


def over(value, size):
    return value >> (size.bit_length() - 1) if size & (size - 1) == 0 else value // size


def rest(value, size):
    return value & (size - 1) if size & (size - 1) == 0 else value % size


def mixed(lane):
    return rest(lane, HI) * COPIES + over(lane, HI)


def group_of(lane):
    return over(lane, 2 * NO) * 2 + rest(over(lane, HI), 2)


def orbital_of(lane):
    return rest(lane, HI) * COPIES + rest(over(lane, 2 * HI), COPIES)


def fold_matrix():
    shape = (LANES, COPIES * LANES)
    row, col = iota(shape, 0), iota(shape, 1)
    return ones_where(row == over(col, LANES) * NO + orbital_of(rest(col, LANES)))


def row_matrix(tiles, natoms):
    size = tiles * natoms
    row, col = iota((size, size), 0), iota((size, size), 1)
    return ones_where(col == rest(row, tiles) * natoms + over(row, tiles))


def stack_tiles(flat):
    return jnp.concatenate(
        [flat[:, t : t + LANES] for t in range(0, flat.shape[1], LANES)], axis=0
    )


def dot(left, right):
    return jnp.dot(left, right, preferred_element_type=jnp.float32)


def make_planes(block, planes, at, order):
    count = block.shape[0]
    ordered = dot(
        order, jnp.concatenate([stack_tiles(block[e]) for e in range(count)], axis=1)
    ).astype(jnp.bfloat16)
    for e in range(count):
        planes[at + e] = ordered[:, e * LANES : (e + 1) * LANES]


def tables_kernel(
    natoms, local_hbm, gradient_hbm, coupling_hbm, kernel_out, derivs_out, planes_out,
    local, gradient, coupling, rows, sems,
):
    copies = [
        pltpu.make_async_copy(coupling_hbm.at[:, 0, :], coupling, sems.at[0]),
        pltpu.make_async_copy(gradient_hbm, gradient, sems.at[1]),
        pltpu.make_async_copy(local_hbm, local, sems.at[2]),
    ]
    for copy in copies:
        copy.start()

    tiles = NO * NO // LANES
    block = natoms * tiles
    cells = ND * ND * NB
    depth = rows.shape[2]
    width = -(-NS * cells // LANES) * LANES
    fold = fold_matrix()
    order = row_matrix(tiles, natoms)
    lane = iota((width, 2 * LANES), 1)
    branch = over(lane, LANES) * COPIES + group_of(rest(lane, LANES))
    lane = iota((width, 2 * LANES), 0) - branch * cells
    widen = ones_where((lane >= 0) & (lane < cells) & (branch < NS))
    line, lane = iota((NB * depth, width), 0), iota((NB * depth, width), 1)
    lane = lane - (rest(line, depth) * NB + over(line, depth))
    chosen = lane == 0
    for s in range(1, NS):
        chosen = chosen | (lane == s * cells)

    copies[0].wait()
    table = jnp.transpose(coupling[...])
    table = jnp.concatenate(
        [table, jnp.zeros((natoms, width - NS * cells), jnp.float32)], axis=1
    )
    for atom in range(natoms):
        left = jnp.where(chosen, table[atom : atom + 1, :], 0.0).astype(jnp.bfloat16)
        wide = dot(left, widen)
        for slot in range(NB):
            for half in range(2):
                rows[atom * NB + slot, half] = wide[
                    slot * depth : (slot + 1) * depth, half * LANES : (half + 1) * LANES
                ]

    copies[1].wait()
    flats = [stack_tiles(gradient[slot, j]) for slot in range(NB) for j in range(ND)]
    ordered = dot(order, jnp.concatenate(flats, axis=1)).astype(jnp.bfloat16)
    for slot in range(NB):
        for j in range(ND):
            at = (slot * ND + j) * LANES
            wide = dot(ordered[:, at : at + LANES], fold)
            for atom in range(natoms):
                derivs_out[atom * NB + slot, j * NO : (j + 1) * NO, :] = jnp.concatenate(
                    [
                        wide[atom * tiles : (atom + 1) * tiles, q * LANES : (q + 1) * LANES]
                        for q in range(COPIES)
                    ],
                    axis=0,
                ).astype(jnp.bfloat16)

    copies[2].wait()
    make_planes(local, planes_out, 0, row_matrix(2 * tiles, natoms))

    def one_cell(at, carry):
        derivs = [
            derivs_out[at, j * NO : (j + 1) * NO, :].astype(jnp.float32) for j in range(ND)
        ]
        for i in range(ND):
            for half in range(2):
                total = None
                for j in range(ND):
                    term = derivs[j] * rows[at, half, ND * i + j : ND * i + j + 1, :]
                    total = term if total is None else total + term
                kernel_out[at, i * NO : (i + 1) * NO, half * LANES : (half + 1) * LANES] = (
                    total.astype(jnp.bfloat16)
                )
        return carry

    lax.fori_loop(0, natoms * NB, one_cell, 0, unroll=4)


def tables(local, gradient, coupling):
    energies, natoms, size = local.shape
    count = NB * natoms
    return pl.pallas_call(
        functools.partial(tables_kernel, natoms),
        out_shape=(
            jax.ShapeDtypeStruct((count, ND * NO, 2 * LANES), jnp.bfloat16),
            jax.ShapeDtypeStruct((count, ND * NO, LANES), jnp.bfloat16),
            jax.ShapeDtypeStruct((energies, natoms * size // LANES, LANES), jnp.bfloat16),
        ),
        in_specs=[pl.BlockSpec(memory_space=pltpu.HBM)] * 3,
        out_specs=[pl.BlockSpec(memory_space=pltpu.VMEM)] * 3,
        scratch_shapes=[
            pltpu.VMEM(local.shape, local.dtype),
            pltpu.VMEM(gradient.shape, gradient.dtype),
            pltpu.VMEM((coupling.shape[0], natoms), jnp.float32),
            pltpu.VMEM((count, 2, 2 * HI, LANES), jnp.float32),
            pltpu.SemaphoreType.DMA((3,)),
        ],
        compiler_params=pltpu.CompilerParams(vmem_limit_bytes=VMEM_LIMIT),
        cost_estimate=pl.CostEstimate(
            flops=200_000_000, bytes_accessed=6_000_000, transcendentals=0
        ),
        name="tables",
    )(in_hbm(local), in_hbm(gradient), in_hbm(coupling))


def sandwich_kernel(
    count, natoms, neighbours_hbm, offsets_hbm, middle_planes, below2, below1, above1, above2,
    kernel, derivs, out, neighbours, offsets, planes, blocks, sems,
):
    copies = [
        pltpu.make_async_copy(neighbours_hbm, neighbours, sems.at[0]),
        pltpu.make_async_copy(offsets_hbm, offsets, sems.at[1]),
    ]
    for copy in copies:
        copy.start()

    tiles = 2 * NO * NO // LANES
    groups = 2 * count
    order = row_matrix(tiles, natoms)
    for piece, ref in ((0, below2), (1, below1), (3, above1), (4, above2)):
        make_planes(ref, planes, piece * count, order)
    planes[2 * count : 3 * count] = middle_planes[...]

    fold = fold_matrix()
    group = group_of(rest(iota(fold.shape, 1), LANES))
    places = [fold * ones_where(group == g) for g in range(COPIES)]
    for copy in copies:
        copy.wait()
    for e in range(count):
        for half in range(2):
            branches = range(half * COPIES, min(NS, (half + 1) * COPIES))
            shifted_planes = [
                planes[2 * count + e - (1 - 2 * (s % 2)) * offsets[s // 2]] for s in branches
            ]
            wide = dot(
                jnp.concatenate(shifted_planes, axis=1),
                jnp.concatenate(places[: len(branches)], axis=0),
            ).astype(jnp.bfloat16)
            for atom in range(natoms):
                for q in range(COPIES):
                    at = (e * COPIES + q) * tiles
                    blocks[atom, at : at + tiles, half * LANES : (half + 1) * LANES] = wide[
                        atom * tiles : (atom + 1) * tiles, q * LANES : (q + 1) * LANES
                    ]

    lane_group = group_of(iota((NO, LANES), 1))
    masks = [ones_where(lane_group == g) for g in range(COPIES)]
    group = over(iota((NO, LANES), 1), NO)
    row_group = over(iota((HI, LANES), 1), NO)
    spans = -(-NB * ND // COPIES)

    def middles(atom):
        blocked = []
        for slot in range(NB):
            wide = lax.dot_general(
                blocks[neighbours[slot, atom]], kernel[atom * NB + slot], NT,
                preferred_element_type=jnp.float32,
            )
            wide = jnp.concatenate(
                [wide, jnp.zeros((groups * NO, LANES - ND * NO), jnp.float32)], axis=1
            )
            rows = []
            for g in range(groups):
                starts = [((g // 2) * COPIES + q) * tiles + (g % 2) * HI for q in range(COPIES)]
                rows.append(jnp.concatenate([wide[at : at + HI] for at in starts], axis=0))
            turned = []
            for d in range(COPIES):
                total = rows[-d % COPIES]
                for lane in range(1, COPIES):
                    total = jnp.where(group == lane, rows[(lane - d) % COPIES], total)
                turned.append(pltpu.roll(total, (COPIES - d) * NO, axis=1) if d else total)
            for i in range(ND):
                total = turned[i]
                for g in range(1, groups):
                    total = jnp.where(group == g, turned[(i - g) % COPIES], total)
                blocked.append(total)
        blocked.extend([jnp.zeros((NO, LANES), jnp.float32)] * (spans * COPIES - len(blocked)))
        pieces = []
        for span in range(spans):
            for u in range(COPIES // 2):
                for q in range(COPIES):
                    for v in range(2):
                        pieces.append(
                            blocked[span * COPIES + 2 * u + v][q * HI : (q + 1) * HI]
                        )
        return jnp.concatenate(pieces, axis=0).astype(jnp.bfloat16)

    def sigmas(atom, right):
        left = []
        for span in range(spans):
            total = None
            for g in range(COPIES):
                k = span * COPIES + g
                if k < NB * ND:
                    at = (k % ND) * NO
                    part = derivs[atom * NB + k // ND, at : at + NO, :] * masks[g]
                    total = part if total is None else total + part
            left.append(total)
        own = dot(jnp.concatenate(left, axis=1), right)
        rows = [own[q * HI : (q + 1) * HI, :] for q in range(COPIES)]
        placed = []
        for g in range(groups):
            total = None
            for q in range(COPIES):
                shift = (q - g) % COPIES * NO
                part = pltpu.roll(rows[q], shift, axis=1) if shift else rows[q]
                total = part if total is None else jnp.where(row_group == q, part, total)
            placed.append(total)
        return placed

    row, col = iota((LANES, LANES), 0), iota((LANES, LANES), 1)
    unmix = ones_where(col == (row - rest(row, NO)) + mixed(rest(row, NO)))
    shares = out.shape[0]
    share = natoms // shares

    def one_share(step, carry):
        atoms = [step * share + k for k in range(share)]
        placed = []
        for atom, right in zip(atoms, [middles(atom) for atom in atoms]):
            placed.extend(sigmas(atom, right))
        out[step] = dot(
            jnp.concatenate(placed, axis=0).astype(jnp.bfloat16), unmix
        ).astype(jnp.bfloat16)
        return carry

    lax.fori_loop(0, shares, one_share, 0)


def sandwich(window, middle_planes, kernel, derivs, neighbours, offsets, shares):
    below2, below1, above1, above2 = window
    count, natoms, size = below2.shape
    groups = 2 * count
    rows = natoms * groups * HI
    return pl.pallas_call(
        functools.partial(sandwich_kernel, count, natoms),
        out_shape=jax.ShapeDtypeStruct((shares, rows // shares, LANES), jnp.bfloat16),
        in_specs=[pl.BlockSpec(memory_space=pltpu.HBM)] * 2
        + [pl.BlockSpec(memory_space=pltpu.VMEM)] * 7,
        out_specs=pl.BlockSpec(memory_space=pltpu.VMEM),
        scratch_shapes=[
            pltpu.SMEM(neighbours.shape, jnp.int32),
            pltpu.SMEM(offsets.shape, jnp.int32),
            pltpu.VMEM((5 * count, natoms * size // LANES, LANES), jnp.bfloat16),
            pltpu.VMEM((natoms, groups * NO, 2 * LANES), jnp.bfloat16),
            pltpu.SemaphoreType.DMA((2,)),
        ],
        compiler_params=pltpu.CompilerParams(vmem_limit_bytes=VMEM_LIMIT),
        cost_estimate=pl.CostEstimate(
            flops=800_000_000, bytes_accessed=7_000_000, transcendentals=0
        ),
        name="sandwich",
    )(
        in_hbm(neighbours), in_hbm(offsets),
        middle_planes, below2, below1, above1, above2, kernel, derivs,
    )


def combine_kernel(parts, out, total):
    count, share, width = out.shape
    tiles = width // LANES
    summed = parts[0].astype(jnp.float32)
    for k in range(1, parts.shape[0]):
        summed = summed + parts[k].astype(jnp.float32)
    total[...] = summed
    for e in range(count):
        for t in range(tiles):
            out[e, :, t * LANES : (t + 1) * LANES] = total[
                pl.ds(e * tiles + t, share, stride=count * tiles), :
            ]


def combine(parts, count, share):
    return pl.pallas_call(
        combine_kernel,
        out_shape=jax.ShapeDtypeStruct((count, share, 2 * NO * NO), jnp.float32),
        in_specs=[pl.BlockSpec(memory_space=pltpu.VMEM)],
        out_specs=pl.BlockSpec(memory_space=pltpu.VMEM),
        scratch_shapes=[pltpu.VMEM(parts.shape[1:], jnp.float32)],
        name="combine",
    )(parts)


def shifted(array, axis, by):
    length = lax.axis_size(axis)
    pairs = [(i, i + by) for i in range(length) if 0 <= i + by < length]
    return lax.ppermute(array, axis, pairs)


def local_partial(window, coupling, gradient, neighbours, offsets, shares):
    below2, below1, local, above1, above2 = window
    kernel, derivs, planes = tables(
        local, gradient, coupling.reshape(-1, 1, coupling.shape[-1])
    )
    remote = (below2, below1, above1, above2)
    return sandwich(remote, planes, kernel, derivs, neighbours.T, offsets, shares)


def body(green, coupling, gradient, neighbours, offsets):
    local_block = green[0]
    count, natoms, _ = local_block.shape
    shares = lax.axis_size("mom")
    window = (
        shifted(local_block, "energy", 2),
        shifted(local_block, "energy", 1),
        local_block,
        shifted(local_block, "energy", -1),
        shifted(local_block, "energy", -2),
    )
    partial_terms = local_partial(window, coupling[0], gradient, neighbours, offsets, shares)
    parts = lax.all_to_all(partial_terms, "mom", 0, 0, tiled=True)
    return combine(parts, count, natoms // shares)


def solution(mesh):
    in_specs = (P("mom", "energy", None, None), P("mom", None, None, None, None), P(), P(), P())
    out_specs = P("energy", "mom", None)
    return jax.shard_map(body, mesh=mesh, in_specs=in_specs, out_specs=out_specs, check_vma=False)
```

```python
import functools

import jax
import jax.numpy as jnp
from jax import lax
from jax.experimental import pallas as pl
from jax.experimental.pallas import tpu as pltpu
from jax.sharding import PartitionSpec as P

NO = 32
NB = 5
NW = 3
NS = 2 * NW
ND = 3
LANES = 128
COPIES = LANES // NO
HI = NO // COPIES
VMEM_LIMIT = 40 * 1024 * 1024

NT = (((1,), (1,)), ((), ()))


def in_hbm(array):
    return pltpu.with_memory_space_constraint(array, pltpu.HBM)


def iota(shape, dim):
    return lax.broadcasted_iota(jnp.int32, shape, dim)


def ones_where(condition):
    return jnp.where(condition, 1.0, 0.0).astype(jnp.bfloat16)


def over(value, size):
    return value >> (size.bit_length() - 1) if size & (size - 1) == 0 else value // size


def rest(value, size):
    return value & (size - 1) if size & (size - 1) == 0 else value % size


def mixed(lane):
    return rest(lane, HI) * COPIES + over(lane, HI)


def group_of(lane):
    return over(lane, 2 * NO) * 2 + rest(over(lane, HI), 2)


def orbital_of(lane):
    return rest(lane, HI) * COPIES + rest(over(lane, 2 * HI), COPIES)


def fold_matrix():
    shape = (LANES, COPIES * LANES)
    row, col = iota(shape, 0), iota(shape, 1)
    return ones_where(row == over(col, LANES) * NO + orbital_of(rest(col, LANES)))


def row_matrix(tiles, natoms):
    size = tiles * natoms
    row, col = iota((size, size), 0), iota((size, size), 1)
    return ones_where(col == rest(row, tiles) * natoms + over(row, tiles))


def stack_tiles(flat):
    return jnp.concatenate(
        [flat[:, t : t + LANES] for t in range(0, flat.shape[1], LANES)], axis=0
    )


def dot(left, right):
    return jnp.dot(left, right, preferred_element_type=jnp.float32)


def make_planes(block, planes, at, order):
    count = block.shape[0]
    ordered = dot(
        order, jnp.concatenate([stack_tiles(block[e]) for e in range(count)], axis=1)
    ).astype(jnp.bfloat16)
    for e in range(count):
        planes[at + e] = ordered[:, e * LANES : (e + 1) * LANES]


def tables_kernel(
    natoms, local_hbm, gradient_hbm, coupling_hbm, kernel_out, derivs_out, planes_out,
    local, gradient, coupling, rows, sems,
):
    copies = [
        pltpu.make_async_copy(coupling_hbm.at[:, 0, :], coupling, sems.at[0]),
        pltpu.make_async_copy(gradient_hbm, gradient, sems.at[1]),
        pltpu.make_async_copy(local_hbm, local, sems.at[2]),
    ]
    for copy in copies:
        copy.start()

    tiles = NO * NO // LANES
    block = natoms * tiles
    cells = ND * ND * NB
    depth = rows.shape[2]
    width = -(-NS * cells // LANES) * LANES
    fold = fold_matrix()
    order = row_matrix(tiles, natoms)
    lane = iota((width, 2 * LANES), 1)
    branch = over(lane, LANES) * COPIES + group_of(rest(lane, LANES))
    lane = iota((width, 2 * LANES), 0) - branch * cells
    widen = ones_where((lane >= 0) & (lane < cells) & (branch < NS))
    line, lane = iota((NB * depth, width), 0), iota((NB * depth, width), 1)
    lane = lane - (rest(line, depth) * NB + over(line, depth))
    chosen = lane == 0
    for s in range(1, NS):
        chosen = chosen | (lane == s * cells)

    copies[0].wait()
    table = jnp.transpose(coupling[...])
    table = jnp.concatenate(
        [table, jnp.zeros((natoms, width - NS * cells), jnp.float32)], axis=1
    )
    lefts = [
        jnp.where(chosen, table[atom : atom + 1, :], 0.0).astype(jnp.bfloat16)
        for atom in range(natoms)
    ]
    wide = dot(jnp.concatenate(lefts, axis=0), widen)
    for at in range(natoms * NB):
        for half in range(2):
            rows[at, half] = wide[
                at * depth : (at + 1) * depth, half * LANES : (half + 1) * LANES
            ]

    copies[1].wait()
    flats = [stack_tiles(gradient[slot, j]) for slot in range(NB) for j in range(ND)]
    ordered = dot(order, jnp.concatenate(flats, axis=1)).astype(jnp.bfloat16)
    stacked = [ordered[:, at : at + LANES] for at in range(0, NB * ND * LANES, LANES)]
    wide = dot(jnp.concatenate(stacked, axis=0), fold)
    for slot in range(NB):
        for j in range(ND):
            for atom in range(natoms):
                at = (slot * ND + j) * block + atom * tiles
                derivs_out[atom * NB + slot, j * NO : (j + 1) * NO, :] = jnp.concatenate(
                    [
                        wide[at : at + tiles, q * LANES : (q + 1) * LANES]
                        for q in range(COPIES)
                    ],
                    axis=0,
                ).astype(jnp.bfloat16)

    copies[2].wait()
    make_planes(local, planes_out, 0, row_matrix(2 * tiles, natoms))

    def one_cell(at, carry):
        derivs = [
            derivs_out[at, j * NO : (j + 1) * NO, :].astype(jnp.float32) for j in range(ND)
        ]
        for i in range(ND):
            for half in range(2):
                total = None
                for j in range(ND):
                    term = derivs[j] * rows[at, half, ND * i + j : ND * i + j + 1, :]
                    total = term if total is None else total + term
                kernel_out[at, i * NO : (i + 1) * NO, half * LANES : (half + 1) * LANES] = (
                    total.astype(jnp.bfloat16)
                )
        return carry

    lax.fori_loop(0, natoms * NB, one_cell, 0, unroll=4)


def tables(local, gradient, coupling):
    energies, natoms, size = local.shape
    count = NB * natoms
    return pl.pallas_call(
        functools.partial(tables_kernel, natoms),
        out_shape=(
            jax.ShapeDtypeStruct((count, ND * NO, 2 * LANES), jnp.bfloat16),
            jax.ShapeDtypeStruct((count, ND * NO, LANES), jnp.bfloat16),
            jax.ShapeDtypeStruct((energies, natoms * size // LANES, LANES), jnp.bfloat16),
        ),
        in_specs=[pl.BlockSpec(memory_space=pltpu.HBM)] * 3,
        out_specs=[pl.BlockSpec(memory_space=pltpu.VMEM)] * 3,
        scratch_shapes=[
            pltpu.VMEM(local.shape, local.dtype),
            pltpu.VMEM(gradient.shape, gradient.dtype),
            pltpu.VMEM((coupling.shape[0], natoms), jnp.float32),
            pltpu.VMEM((count, 2, 2 * HI, LANES), jnp.float32),
            pltpu.SemaphoreType.DMA((3,)),
        ],
        compiler_params=pltpu.CompilerParams(vmem_limit_bytes=VMEM_LIMIT),
        cost_estimate=pl.CostEstimate(
            flops=200_000_000, bytes_accessed=6_000_000, transcendentals=0
        ),
        name="tables",
    )(in_hbm(local), in_hbm(gradient), in_hbm(coupling))


def sandwich_kernel(
    count, natoms, neighbours_hbm, offsets_hbm, middle_planes, below2, below1, above1, above2,
    kernel, derivs, out, neighbours, offsets, planes, blocks, sems,
):
    copies = [
        pltpu.make_async_copy(neighbours_hbm, neighbours, sems.at[0]),
        pltpu.make_async_copy(offsets_hbm, offsets, sems.at[1]),
    ]
    for copy in copies:
        copy.start()

    tiles = 2 * NO * NO // LANES
    groups = 2 * count
    order = row_matrix(tiles, natoms)
    for piece, ref in ((0, below2), (1, below1), (3, above1), (4, above2)):
        make_planes(ref, planes, piece * count, order)
    planes[2 * count : 3 * count] = middle_planes[...]

    fold = fold_matrix()
    group = group_of(rest(iota(fold.shape, 1), LANES))
    places = [fold * ones_where(group == g) for g in range(COPIES)]
    for copy in copies:
        copy.wait()
    for half in range(2):
        branches = range(half * COPIES, min(NS, (half + 1) * COPIES))
        shifted_planes = [
            jnp.concatenate(
                [
                    planes[2 * count + e - (1 - 2 * (s % 2)) * offsets[s // 2]]
                    for e in range(count)
                ],
                axis=0,
            )
            for s in branches
        ]
        wide = dot(
            jnp.concatenate(shifted_planes, axis=1),
            jnp.concatenate(places[: len(branches)], axis=0),
        ).astype(jnp.bfloat16)
        for e in range(count):
            for atom in range(natoms):
                for q in range(COPIES):
                    at = (e * COPIES + q) * tiles
                    start = (e * natoms + atom) * tiles
                    blocks[atom, at : at + tiles, half * LANES : (half + 1) * LANES] = wide[
                        start : start + tiles, q * LANES : (q + 1) * LANES
                    ]

    lane_group = group_of(iota((NO, LANES), 1))
    masks = [ones_where(lane_group == g) for g in range(COPIES)]
    group = over(iota((NO, LANES), 1), NO)
    row_group = over(iota((HI, LANES), 1), NO)
    spans = -(-NB * ND // COPIES)

    def middles(atom):
        blocked = []
        for slot in range(NB):
            wide = lax.dot_general(
                blocks[neighbours[slot, atom]], kernel[atom * NB + slot], NT,
                preferred_element_type=jnp.float32,
            )
            wide = jnp.concatenate(
                [wide, jnp.zeros((groups * NO, LANES - ND * NO), jnp.float32)], axis=1
            )
            rows = []
            for g in range(groups):
                starts = [((g // 2) * COPIES + q) * tiles + (g % 2) * HI for q in range(COPIES)]
                rows.append(jnp.concatenate([wide[at : at + HI] for at in starts], axis=0))
            turned = []
            for d in range(COPIES):
                total = rows[-d % COPIES]
                for lane in range(1, COPIES):
                    total = jnp.where(group == lane, rows[(lane - d) % COPIES], total)
                turned.append(pltpu.roll(total, (COPIES - d) * NO, axis=1) if d else total)
            for i in range(ND):
                total = turned[i]
                for g in range(1, groups):
                    total = jnp.where(group == g, turned[(i - g) % COPIES], total)
                blocked.append(total)
        blocked.extend([jnp.zeros((NO, LANES), jnp.float32)] * (spans * COPIES - len(blocked)))
        pieces = []
        for span in range(spans):
            for u in range(COPIES // 2):
                for q in range(COPIES):
                    for v in range(2):
                        pieces.append(
                            blocked[span * COPIES + 2 * u + v][q * HI : (q + 1) * HI]
                        )
        return jnp.concatenate(pieces, axis=0).astype(jnp.bfloat16)

    def sigmas(atom, right):
        left = []
        for span in range(spans):
            total = None
            for g in range(COPIES):
                k = span * COPIES + g
                if k < NB * ND:
                    at = (k % ND) * NO
                    part = derivs[atom * NB + k // ND, at : at + NO, :] * masks[g]
                    total = part if total is None else total + part
            left.append(total)
        own = dot(jnp.concatenate(left, axis=1), right)
        rows = [own[q * HI : (q + 1) * HI, :] for q in range(COPIES)]
        placed = []
        for g in range(groups):
            total = None
            for q in range(COPIES):
                shift = (q - g) % COPIES * NO
                part = pltpu.roll(rows[q], shift, axis=1) if shift else rows[q]
                total = part if total is None else jnp.where(row_group == q, part, total)
            placed.append(total)
        return placed

    row, col = iota((LANES, LANES), 0), iota((LANES, LANES), 1)
    unmix = ones_where(col == (row - rest(row, NO)) + mixed(rest(row, NO)))
    shares = out.shape[0]
    share = natoms // shares

    def one_share(step, carry):
        atoms = [step * share + k for k in range(share)]
        placed = []
        for atom, right in zip(atoms, [middles(atom) for atom in atoms]):
            placed.extend(sigmas(atom, right))
        out[step] = dot(
            jnp.concatenate(placed, axis=0).astype(jnp.bfloat16), unmix
        ).astype(jnp.bfloat16)
        return carry

    lax.fori_loop(0, shares, one_share, 0)


def sandwich(window, middle_planes, kernel, derivs, neighbours, offsets, shares):
    below2, below1, above1, above2 = window
    count, natoms, size = below2.shape
    groups = 2 * count
    rows = natoms * groups * HI
    return pl.pallas_call(
        functools.partial(sandwich_kernel, count, natoms),
        out_shape=jax.ShapeDtypeStruct((shares, rows // shares, LANES), jnp.bfloat16),
        in_specs=[pl.BlockSpec(memory_space=pltpu.HBM)] * 2
        + [pl.BlockSpec(memory_space=pltpu.VMEM)] * 7,
        out_specs=pl.BlockSpec(memory_space=pltpu.VMEM),
        scratch_shapes=[
            pltpu.SMEM(neighbours.shape, jnp.int32),
            pltpu.SMEM(offsets.shape, jnp.int32),
            pltpu.VMEM((5 * count, natoms * size // LANES, LANES), jnp.bfloat16),
            pltpu.VMEM((natoms, groups * NO, 2 * LANES), jnp.bfloat16),
            pltpu.SemaphoreType.DMA((2,)),
        ],
        compiler_params=pltpu.CompilerParams(vmem_limit_bytes=VMEM_LIMIT),
        cost_estimate=pl.CostEstimate(
            flops=800_000_000, bytes_accessed=7_000_000, transcendentals=0
        ),
        name="sandwich",
    )(
        in_hbm(neighbours), in_hbm(offsets),
        middle_planes, below2, below1, above1, above2, kernel, derivs,
    )


def combine_kernel(parts, out, total):
    count, share, width = out.shape
    tiles = width // LANES
    summed = parts[0].astype(jnp.float32)
    for k in range(1, parts.shape[0]):
        summed = summed + parts[k].astype(jnp.float32)
    total[...] = summed
    for e in range(count):
        for t in range(tiles):
            out[e, :, t * LANES : (t + 1) * LANES] = total[
                pl.ds(e * tiles + t, share, stride=count * tiles), :
            ]


def combine(parts, count, share):
    return pl.pallas_call(
        combine_kernel,
        out_shape=jax.ShapeDtypeStruct((count, share, 2 * NO * NO), jnp.float32),
        in_specs=[pl.BlockSpec(memory_space=pltpu.VMEM)],
        out_specs=pl.BlockSpec(memory_space=pltpu.VMEM),
        scratch_shapes=[pltpu.VMEM(parts.shape[1:], jnp.float32)],
        name="combine",
    )(parts)


def shifted(array, axis, by):
    length = lax.axis_size(axis)
    pairs = [(i, i + by) for i in range(length) if 0 <= i + by < length]
    return lax.ppermute(array, axis, pairs)


def local_partial(window, coupling, gradient, neighbours, offsets, shares):
    below2, below1, local, above1, above2 = window
    kernel, derivs, planes = tables(
        local, gradient, coupling.reshape(-1, 1, coupling.shape[-1])
    )
    remote = (below2, below1, above1, above2)
    return sandwich(remote, planes, kernel, derivs, neighbours.T, offsets, shares)


def body(green, coupling, gradient, neighbours, offsets):
    local_block = green[0]
    count, natoms, _ = local_block.shape
    shares = lax.axis_size("mom")
    window = (
        shifted(local_block, "energy", 2),
        shifted(local_block, "energy", 1),
        local_block,
        shifted(local_block, "energy", -1),
        shifted(local_block, "energy", -2),
    )
    partial_terms = local_partial(window, coupling[0], gradient, neighbours, offsets, shares)
    parts = lax.all_to_all(partial_terms, "mom", 0, 0, tiled=True)
    return combine(parts, count, natoms // shares)


def solution(mesh):
    in_specs = (P("mom", "energy", None, None), P("mom", None, None, None, None), P(), P(), P())
    out_specs = P("energy", "mom", None)
    return jax.shard_map(body, mesh=mesh, in_specs=in_specs, out_specs=out_specs, check_vma=False)
```

```python
import functools

import jax
import jax.numpy as jnp
from jax import lax
from jax.experimental import pallas as pl
from jax.experimental.pallas import tpu as pltpu
from jax.sharding import PartitionSpec as P

NO = 32
NB = 5
NW = 3
NS = 2 * NW
ND = 3
LANES = 128
COPIES = LANES // NO
HI = NO // COPIES
VMEM_LIMIT = 40 * 1024 * 1024

NT = (((1,), (1,)), ((), ()))


def in_hbm(array):
    return pltpu.with_memory_space_constraint(array, pltpu.HBM)


def iota(shape, dim):
    return lax.broadcasted_iota(jnp.int32, shape, dim)


def ones_where(condition):
    return jnp.where(condition, 1.0, 0.0).astype(jnp.bfloat16)


def over(value, size):
    return value >> (size.bit_length() - 1) if size & (size - 1) == 0 else value // size


def rest(value, size):
    return value & (size - 1) if size & (size - 1) == 0 else value % size


def mixed(lane):
    return rest(lane, HI) * COPIES + over(lane, HI)


def group_of(lane):
    return over(lane, 2 * NO) * 2 + rest(over(lane, HI), 2)


def orbital_of(lane):
    return rest(lane, HI) * COPIES + rest(over(lane, 2 * HI), COPIES)


def fold_matrix():
    shape = (LANES, COPIES * LANES)
    row, col = iota(shape, 0), iota(shape, 1)
    return ones_where(row == over(col, LANES) * NO + orbital_of(rest(col, LANES)))


def row_matrix(tiles, natoms):
    size = tiles * natoms
    row, col = iota((size, size), 0), iota((size, size), 1)
    return ones_where(col == rest(row, tiles) * natoms + over(row, tiles))


def stack_tiles(flat):
    return jnp.concatenate(
        [flat[:, t : t + LANES] for t in range(0, flat.shape[1], LANES)], axis=0
    )


def dot(left, right):
    return jnp.dot(left, right, preferred_element_type=jnp.float32)


def make_planes(block, planes, at, order):
    count = block.shape[0]
    ordered = dot(
        order, jnp.concatenate([stack_tiles(block[e]) for e in range(count)], axis=1)
    ).astype(jnp.bfloat16)
    for e in range(count):
        planes[at + e] = ordered[:, e * LANES : (e + 1) * LANES]


def tables_kernel(
    natoms, local_hbm, gradient_hbm, coupling_hbm, kernel_out, derivs_out, planes_out,
    local, gradient, coupling, rows, sems,
):
    copies = [
        pltpu.make_async_copy(coupling_hbm.at[:, 0, :], coupling, sems.at[0]),
        pltpu.make_async_copy(gradient_hbm, gradient, sems.at[1]),
        pltpu.make_async_copy(local_hbm, local, sems.at[2]),
    ]
    for copy in copies:
        copy.start()

    tiles = NO * NO // LANES
    block = natoms * tiles
    cells = ND * ND * NB
    depth = rows.shape[2]
    width = -(-NS * cells // LANES) * LANES
    fold = fold_matrix()
    order = row_matrix(tiles, natoms)
    lane = iota((width, 2 * LANES), 1)
    branch = over(lane, LANES) * COPIES + group_of(rest(lane, LANES))
    lane = iota((width, 2 * LANES), 0) - branch * cells
    widen = ones_where((lane >= 0) & (lane < cells) & (branch < NS))
    line, lane = iota((NB * depth, width), 0), iota((NB * depth, width), 1)
    lane = lane - (rest(line, depth) * NB + over(line, depth))
    chosen = lane == 0
    for s in range(1, NS):
        chosen = chosen | (lane == s * cells)

    copies[0].wait()
    table = jnp.transpose(coupling[...])
    table = jnp.concatenate(
        [table, jnp.zeros((natoms, width - NS * cells), jnp.float32)], axis=1
    )
    lefts = [
        jnp.where(chosen, table[atom : atom + 1, :], 0.0).astype(jnp.bfloat16)
        for atom in range(natoms)
    ]
    wide = dot(jnp.concatenate(lefts, axis=0), widen)
    for at in range(natoms * NB):
        for half in range(2):
            rows[at, half] = wide[
                at * depth : (at + 1) * depth, half * LANES : (half + 1) * LANES
            ]

    copies[1].wait()
    flats = [stack_tiles(gradient[slot, j]) for slot in range(NB) for j in range(ND)]
    ordered = dot(order, jnp.concatenate(flats, axis=1)).astype(jnp.bfloat16)
    stacked = [ordered[:, at : at + LANES] for at in range(0, NB * ND * LANES, LANES)]
    wide = dot(jnp.concatenate(stacked, axis=0), fold)
    for slot in range(NB):
        for j in range(ND):
            for atom in range(natoms):
                at = (slot * ND + j) * block + atom * tiles
                derivs_out[atom * NB + slot, j * NO : (j + 1) * NO, :] = jnp.concatenate(
                    [
                        wide[at : at + tiles, q * LANES : (q + 1) * LANES]
                        for q in range(COPIES)
                    ],
                    axis=0,
                ).astype(jnp.bfloat16)

    copies[2].wait()
    make_planes(local, planes_out, 0, row_matrix(2 * tiles, natoms))

    def one_cell(at, carry):
        derivs = [derivs_out[at, j * NO : (j + 1) * NO, :] for j in range(ND)]
        for i in range(ND):
            for half in range(2):
                total = None
                for j in range(ND):
                    row = rows[at, half, ND * i + j : ND * i + j + 1, :]
                    weight = jnp.broadcast_to(row, (NO, LANES)).astype(jnp.bfloat16)
                    term = derivs[j] * weight
                    total = term if total is None else total + term
                kernel_out[at, i * NO : (i + 1) * NO, half * LANES : (half + 1) * LANES] = total
        return carry

    lax.fori_loop(0, natoms * NB, one_cell, 0, unroll=4)


def tables(local, gradient, coupling):
    energies, natoms, size = local.shape
    count = NB * natoms
    return pl.pallas_call(
        functools.partial(tables_kernel, natoms),
        out_shape=(
            jax.ShapeDtypeStruct((count, ND * NO, 2 * LANES), jnp.bfloat16),
            jax.ShapeDtypeStruct((count, ND * NO, LANES), jnp.bfloat16),
            jax.ShapeDtypeStruct((energies, natoms * size // LANES, LANES), jnp.bfloat16),
        ),
        in_specs=[pl.BlockSpec(memory_space=pltpu.HBM)] * 3,
        out_specs=[pl.BlockSpec(memory_space=pltpu.VMEM)] * 3,
        scratch_shapes=[
            pltpu.VMEM(local.shape, local.dtype),
            pltpu.VMEM(gradient.shape, gradient.dtype),
            pltpu.VMEM((coupling.shape[0], natoms), jnp.float32),
            pltpu.VMEM((count, 2, 2 * HI, LANES), jnp.float32),
            pltpu.SemaphoreType.DMA((3,)),
        ],
        compiler_params=pltpu.CompilerParams(vmem_limit_bytes=VMEM_LIMIT),
        cost_estimate=pl.CostEstimate(
            flops=200_000_000, bytes_accessed=6_000_000, transcendentals=0
        ),
        name="tables",
    )(in_hbm(local), in_hbm(gradient), in_hbm(coupling))


def partner(index, step, size):
    return index ^ step if size & (size - 1) == 0 else (index + step) % size


def share_terms(atoms, groups, block_of, kernel, derivs):
    tiles = groups * HI // 2
    lane_group = group_of(iota((NO, LANES), 1))
    masks = [ones_where(lane_group == g) for g in range(COPIES)]
    group = over(iota((NO, LANES), 1), NO)
    row_group = over(iota((HI, LANES), 1), NO)
    spans = -(-NB * ND // COPIES)

    def middles(k):
        blocked = []
        for slot in range(NB):
            wide = lax.dot_general(
                block_of(k, slot), kernel[atoms[k] * NB + slot], NT,
                preferred_element_type=jnp.float32,
            )
            wide = jnp.concatenate(
                [wide, jnp.zeros((groups * NO, LANES - ND * NO), jnp.float32)], axis=1
            )
            rows = []
            for g in range(groups):
                starts = [((g // 2) * COPIES + q) * tiles + (g % 2) * HI for q in range(COPIES)]
                rows.append(jnp.concatenate([wide[at : at + HI] for at in starts], axis=0))
            turned = []
            for d in range(COPIES):
                total = rows[-d % COPIES]
                for lane in range(1, COPIES):
                    total = jnp.where(group == lane, rows[(lane - d) % COPIES], total)
                turned.append(pltpu.roll(total, (COPIES - d) * NO, axis=1) if d else total)
            for i in range(ND):
                total = turned[i]
                for g in range(1, groups):
                    total = jnp.where(group == g, turned[(i - g) % COPIES], total)
                blocked.append(total)
        blocked.extend([jnp.zeros((NO, LANES), jnp.float32)] * (spans * COPIES - len(blocked)))
        pieces = []
        for span in range(spans):
            for u in range(COPIES // 2):
                for q in range(COPIES):
                    for v in range(2):
                        pieces.append(
                            blocked[span * COPIES + 2 * u + v][q * HI : (q + 1) * HI]
                        )
        return jnp.concatenate(pieces, axis=0).astype(jnp.bfloat16)

    def sigmas(k, right):
        left = []
        for span in range(spans):
            total = None
            for g in range(COPIES):
                pair = span * COPIES + g
                if pair < NB * ND:
                    at = (pair % ND) * NO
                    part = derivs[atoms[k] * NB + pair // ND, at : at + NO, :] * masks[g]
                    total = part if total is None else total + part
            left.append(total)
        own = dot(jnp.concatenate(left, axis=1), right)
        rows = [own[q * HI : (q + 1) * HI, :] for q in range(COPIES)]
        placed = []
        for g in range(groups):
            total = None
            for q in range(COPIES):
                shift = (q - g) % COPIES * NO
                part = pltpu.roll(rows[q], shift, axis=1) if shift else rows[q]
                total = part if total is None else jnp.where(row_group == q, part, total)
            placed.append(total)
        return placed

    rights = [middles(k) for k in range(len(atoms))]
    placed = []
    for k, right in enumerate(rights):
        placed.extend(sigmas(k, right))
    row, col = iota((LANES, LANES), 0), iota((LANES, LANES), 1)
    unmix = ones_where(col == (row - rest(row, NO)) + mixed(rest(row, NO)))
    return dot(jnp.concatenate(placed, axis=0).astype(jnp.bfloat16), unmix)


def sandwich_kernel(
    count, natoms, shares, neighbours_hbm, offsets_hbm, middle_planes,
    below2, below1, above1, above2, kernel, derivs, *refs,
):
    outs, own_blocks = refs[: shares - 1], refs[shares - 1]
    neighbours, offsets, planes, blocks, results, sems = refs[shares:]
    copies = [
        pltpu.make_async_copy(neighbours_hbm, neighbours, sems.at[0]),
        pltpu.make_async_copy(offsets_hbm, offsets, sems.at[1]),
    ]
    for copy in copies:
        copy.start()

    tiles = 2 * NO * NO // LANES
    groups = 2 * count
    order = row_matrix(tiles, natoms)
    for piece, ref in ((0, below2), (1, below1), (3, above1), (4, above2)):
        make_planes(ref, planes, piece * count, order)
    planes[2 * count : 3 * count] = middle_planes[...]

    fold = fold_matrix()
    group = group_of(rest(iota(fold.shape, 1), LANES))
    places = [fold * ones_where(group == g) for g in range(COPIES)]
    for copy in copies:
        copy.wait()
    for half in range(2):
        branches = range(half * COPIES, min(NS, (half + 1) * COPIES))
        shifted_planes = [
            jnp.concatenate(
                [
                    planes[2 * count + e - (1 - 2 * (s % 2)) * offsets[s // 2]]
                    for e in range(count)
                ],
                axis=0,
            )
            for s in branches
        ]
        wide = dot(
            jnp.concatenate(shifted_planes, axis=1),
            jnp.concatenate(places[: len(branches)], axis=0),
        ).astype(jnp.bfloat16)
        for e in range(count):
            for atom in range(natoms):
                for q in range(COPIES):
                    at = (e * COPIES + q) * tiles
                    start = (e * natoms + atom) * tiles
                    blocks[atom, at : at + tiles, half * LANES : (half + 1) * LANES] = wide[
                        start : start + tiles, q * LANES : (q + 1) * LANES
                    ]

    me = lax.axis_index("mom")
    share = natoms // shares
    for k in range(share):
        for slot in range(NB):
            own_blocks[k * NB + slot] = blocks[neighbours[slot, me * share + k]]

    def one_share(step, carry):
        first = partner(me, step, shares) * share
        atoms = [first + k for k in range(share)]
        results[step] = share_terms(
            atoms, groups, lambda k, slot: blocks[neighbours[slot, atoms[k]]], kernel, derivs
        ).astype(jnp.bfloat16)
        return carry

    lax.fori_loop(1, shares, one_share, 0)
    for step in range(1, shares):
        outs[step - 1][...] = results[step]


def sandwich(window, middle_planes, kernel, derivs, neighbours, offsets, shares):
    below2, below1, above1, above2 = window
    count, natoms, size = below2.shape
    groups = 2 * count
    share = natoms // shares
    rows = share * groups * HI
    return pl.pallas_call(
        functools.partial(sandwich_kernel, count, natoms, shares),
        out_shape=(jax.ShapeDtypeStruct((rows, LANES), jnp.bfloat16),) * (shares - 1)
        + (jax.ShapeDtypeStruct((share * NB, groups * NO, 2 * LANES), jnp.bfloat16),),
        in_specs=[pl.BlockSpec(memory_space=pltpu.HBM)] * 2
        + [pl.BlockSpec(memory_space=pltpu.VMEM)] * 7,
        out_specs=[pl.BlockSpec(memory_space=pltpu.VMEM)] * shares,
        scratch_shapes=[
            pltpu.SMEM(neighbours.shape, jnp.int32),
            pltpu.SMEM(offsets.shape, jnp.int32),
            pltpu.VMEM((5 * count, natoms * size // LANES, LANES), jnp.bfloat16),
            pltpu.VMEM((natoms, groups * NO, 2 * LANES), jnp.bfloat16),
            pltpu.VMEM((shares, rows, LANES), jnp.bfloat16),
            pltpu.SemaphoreType.DMA((2,)),
        ],
        compiler_params=pltpu.CompilerParams(vmem_limit_bytes=VMEM_LIMIT),
        cost_estimate=pl.CostEstimate(
            flops=800_000_000, bytes_accessed=7_000_000, transcendentals=0
        ),
        name="sandwich",
    )(
        in_hbm(neighbours), in_hbm(offsets),
        middle_planes, below2, below1, above1, above2, kernel, derivs,
    )


def own_kernel(groups, blocks, kernel, derivs, out):
    share = blocks.shape[0] // NB
    first = lax.axis_index("mom") * share
    out[...] = share_terms(
        [first + k for k in range(share)], groups,
        lambda k, slot: blocks[k * NB + slot], kernel, derivs,
    )


def own_share(blocks, kernel, derivs):
    share = blocks.shape[0] // NB
    groups = blocks.shape[1] // NO
    return pl.pallas_call(
        functools.partial(own_kernel, groups),
        out_shape=jax.ShapeDtypeStruct((share * groups * HI, LANES), jnp.float32),
        in_specs=[pl.BlockSpec(memory_space=pltpu.VMEM)] * 3,
        out_specs=pl.BlockSpec(memory_space=pltpu.VMEM),
        compiler_params=pltpu.CompilerParams(vmem_limit_bytes=VMEM_LIMIT),
        cost_estimate=pl.CostEstimate(
            flops=200_000_000, bytes_accessed=2_000_000, transcendentals=0
        ),
        name="own_share",
    )(blocks, kernel, derivs)


def combine_kernel(own, *refs):
    parts, out, total = refs[:-2], refs[-2], refs[-1]
    count, share, width = out.shape
    tiles = width // LANES
    summed = own[...]
    for part in parts:
        summed = summed + part[...].astype(jnp.float32)
    total[...] = summed
    for e in range(count):
        for t in range(tiles):
            out[e, :, t * LANES : (t + 1) * LANES] = total[
                pl.ds(e * tiles + t, share, stride=count * tiles), :
            ]


def combine(own, parts, count, share):
    return pl.pallas_call(
        combine_kernel,
        out_shape=jax.ShapeDtypeStruct((count, share, 2 * NO * NO), jnp.float32),
        in_specs=[pl.BlockSpec(memory_space=pltpu.VMEM)] * (1 + len(parts)),
        out_specs=pl.BlockSpec(memory_space=pltpu.VMEM),
        scratch_shapes=[pltpu.VMEM(own.shape, jnp.float32)],
        compiler_params=pltpu.CompilerParams(vmem_limit_bytes=VMEM_LIMIT),
        name="combine",
    )(own, *parts)


def shifted(array, axis, by):
    length = lax.axis_size(axis)
    pairs = [(i, i + by) for i in range(length) if 0 <= i + by < length]
    return lax.ppermute(array, axis, pairs)


def body(green, coupling, gradient, neighbours, offsets):
    local = green[0]
    count, natoms, _ = local.shape
    shares = lax.axis_size("mom")
    remote = (
        shifted(local, "energy", 2),
        shifted(local, "energy", 1),
        shifted(local, "energy", -1),
        shifted(local, "energy", -2),
    )
    kernel, derivs, planes = tables(local, gradient, coupling.reshape(-1, 1, coupling.shape[-1]))
    *terms, own_blocks = sandwich(remote, planes, kernel, derivs, neighbours.T, offsets, shares)
    parts = [
        lax.ppermute(term, "mom", [(i, partner(i, step, shares)) for i in range(shares)])
        for step, term in enumerate(terms, 1)
    ]
    own = own_share(own_blocks, kernel, derivs)
    return combine(own, parts, count, natoms // shares)


def solution(mesh):
    in_specs = (P("mom", "energy", None, None), P("mom", None, None, None, None), P(), P(), P())
    out_specs = P("energy", "mom", None)
    return jax.shard_map(body, mesh=mesh, in_specs=in_specs, out_specs=out_specs, check_vma=False)
```

```python
import functools

import jax
import jax.numpy as jnp
from jax import lax
from jax.experimental import pallas as pl
from jax.experimental.pallas import tpu as pltpu
from jax.sharding import PartitionSpec as P

NO = 32
NB = 5
NW = 3
NS = 2 * NW
ND = 3
LANES = 128
COPIES = LANES // NO
HI = NO // COPIES
VMEM_LIMIT = 40 * 1024 * 1024

NT = (((1,), (1,)), ((), ()))


def in_hbm(array):
    return pltpu.with_memory_space_constraint(array, pltpu.HBM)


def iota(shape, dim):
    return lax.broadcasted_iota(jnp.int32, shape, dim)


def ones_where(condition):
    return jnp.where(condition, 1.0, 0.0).astype(jnp.bfloat16)


def over(value, size):
    return value >> (size.bit_length() - 1) if size & (size - 1) == 0 else value // size


def rest(value, size):
    return value & (size - 1) if size & (size - 1) == 0 else value % size


def mixed(lane):
    return rest(lane, HI) * COPIES + over(lane, HI)


def group_of(lane):
    return over(lane, 2 * NO) * 2 + rest(over(lane, HI), 2)


def orbital_of(lane):
    return rest(lane, HI) * COPIES + rest(over(lane, 2 * HI), COPIES)


def fold_matrix():
    shape = (LANES, COPIES * LANES)
    row, col = iota(shape, 0), iota(shape, 1)
    return ones_where(row == over(col, LANES) * NO + orbital_of(rest(col, LANES)))


def row_matrix(tiles, natoms):
    size = tiles * natoms
    row, col = iota((size, size), 0), iota((size, size), 1)
    return ones_where(col == rest(row, tiles) * natoms + over(row, tiles))


def stack_tiles(flat):
    return jnp.concatenate(
        [flat[:, t : t + LANES] for t in range(0, flat.shape[1], LANES)], axis=0
    )


def dot(left, right):
    return jnp.dot(left, right, preferred_element_type=jnp.float32)


def make_planes(block, planes, at, order, factor=None):
    count = block.shape[0]
    ordered = dot(order, jnp.concatenate([stack_tiles(block[e]) for e in range(count)], axis=1))
    if factor is not None:
        ordered = ordered * factor
    ordered = ordered.astype(jnp.bfloat16)
    for e in range(count):
        planes[at + e] = ordered[:, e * LANES : (e + 1) * LANES]


def tables_kernel(
    natoms, local_hbm, gradient_hbm, coupling_hbm, kernel_out, derivs_out, planes_out,
    local, gradient, coupling, rows, sems,
):
    copies = [
        pltpu.make_async_copy(coupling_hbm.at[:, 0, :], coupling, sems.at[0]),
        pltpu.make_async_copy(gradient_hbm, gradient, sems.at[1]),
        pltpu.make_async_copy(local_hbm, local, sems.at[2]),
    ]
    for copy in copies:
        copy.start()

    tiles = NO * NO // LANES
    block = natoms * tiles
    cells = ND * ND * NB
    depth = rows.shape[2]
    width = -(-NS * cells // LANES) * LANES
    fold = fold_matrix()
    order = row_matrix(tiles, natoms)
    lane = iota((width, 2 * LANES), 1)
    branch = over(lane, LANES) * COPIES + group_of(rest(lane, LANES))
    lane = iota((width, 2 * LANES), 0) - branch * cells
    widen = ones_where((lane >= 0) & (lane < cells) & (branch < NS))
    line, lane = iota((NB * depth, width), 0), iota((NB * depth, width), 1)
    lane = lane - (rest(line, depth) * NB + over(line, depth))
    chosen = lane == 0
    for s in range(1, NS):
        chosen = chosen | (lane == s * cells)

    copies[0].wait()
    table = jnp.transpose(coupling[...])
    table = jnp.concatenate(
        [table, jnp.zeros((natoms, width - NS * cells), jnp.float32)], axis=1
    )
    lefts = [
        jnp.where(chosen, table[atom : atom + 1, :], 0.0).astype(jnp.bfloat16)
        for atom in range(natoms)
    ]
    wide = dot(jnp.concatenate(lefts, axis=0), widen)
    for at in range(natoms * NB):
        for half in range(2):
            rows[at, half] = wide[
                at * depth : (at + 1) * depth, half * LANES : (half + 1) * LANES
            ]

    copies[1].wait()
    flats = [stack_tiles(gradient[slot, j]) for slot in range(NB) for j in range(ND)]
    ordered = dot(order, jnp.concatenate(flats, axis=1)).astype(jnp.bfloat16)
    stacked = [ordered[:, at : at + LANES] for at in range(0, NB * ND * LANES, LANES)]
    wide = dot(jnp.concatenate(stacked, axis=0), fold)
    for slot in range(NB):
        for j in range(ND):
            for atom in range(natoms):
                at = (slot * ND + j) * block + atom * tiles
                derivs_out[atom * NB + slot, j * NO : (j + 1) * NO, :] = jnp.concatenate(
                    [
                        wide[at : at + tiles, q * LANES : (q + 1) * LANES]
                        for q in range(COPIES)
                    ],
                    axis=0,
                ).astype(jnp.bfloat16)

    copies[2].wait()
    make_planes(local, planes_out, 0, row_matrix(2 * tiles, natoms))

    def one_cell(at, carry):
        derivs = [derivs_out[at, j * NO : (j + 1) * NO, :] for j in range(ND)]
        for i in range(ND):
            for half in range(2):
                total = None
                for j in range(ND):
                    row = rows[at, half, ND * i + j : ND * i + j + 1, :]
                    weight = jnp.broadcast_to(row, (NO, LANES)).astype(jnp.bfloat16)
                    term = derivs[j] * weight
                    total = term if total is None else total + term
                kernel_out[at, i * NO : (i + 1) * NO, half * LANES : (half + 1) * LANES] = total
        return carry

    lax.fori_loop(0, natoms * NB, one_cell, 0, unroll=4)


def tables(local, gradient, coupling):
    energies, natoms, size = local.shape
    count = NB * natoms
    return pl.pallas_call(
        functools.partial(tables_kernel, natoms),
        out_shape=(
            jax.ShapeDtypeStruct((count, ND * NO, 2 * LANES), jnp.bfloat16),
            jax.ShapeDtypeStruct((count, ND * NO, LANES), jnp.bfloat16),
            jax.ShapeDtypeStruct((energies, natoms * size // LANES, LANES), jnp.bfloat16),
        ),
        in_specs=[pl.BlockSpec(memory_space=pltpu.HBM)] * 3,
        out_specs=[pl.BlockSpec(memory_space=pltpu.VMEM)] * 3,
        scratch_shapes=[
            pltpu.VMEM(local.shape, local.dtype),
            pltpu.VMEM(gradient.shape, gradient.dtype),
            pltpu.VMEM((coupling.shape[0], natoms), jnp.float32),
            pltpu.VMEM((count, 2, 2 * HI, LANES), jnp.float32),
            pltpu.SemaphoreType.DMA((3,)),
        ],
        compiler_params=pltpu.CompilerParams(vmem_limit_bytes=VMEM_LIMIT),
        cost_estimate=pl.CostEstimate(
            flops=200_000_000, bytes_accessed=6_000_000, transcendentals=0
        ),
        name="tables",
    )(in_hbm(local), in_hbm(gradient), in_hbm(coupling))


def partner(index, step, size):
    return index ^ step if size & (size - 1) == 0 else (index + step) % size


def share_terms(atoms, groups, block_of, kernel, derivs):
    tiles = groups * HI // 2
    lane_group = group_of(iota((NO, LANES), 1))
    masks = [ones_where(lane_group == g) for g in range(COPIES)]
    group = over(iota((NO, LANES), 1), NO)
    row_group = over(iota((HI, LANES), 1), NO)
    spans = -(-NB * ND // COPIES)

    def middles(k):
        blocked = []
        for slot in range(NB):
            wide = lax.dot_general(
                block_of(k, slot), kernel[atoms[k] * NB + slot], NT,
                preferred_element_type=jnp.float32,
            )
            wide = jnp.concatenate(
                [wide, jnp.zeros((groups * NO, LANES - ND * NO), jnp.float32)], axis=1
            )
            rows = []
            for g in range(groups):
                starts = [((g // 2) * COPIES + q) * tiles + (g % 2) * HI for q in range(COPIES)]
                rows.append(jnp.concatenate([wide[at : at + HI] for at in starts], axis=0))
            turned = []
            for d in range(COPIES):
                total = rows[-d % COPIES]
                for lane in range(1, COPIES):
                    total = jnp.where(group == lane, rows[(lane - d) % COPIES], total)
                turned.append(pltpu.roll(total, (COPIES - d) * NO, axis=1) if d else total)
            for i in range(ND):
                total = turned[i]
                for g in range(1, groups):
                    total = jnp.where(group == g, turned[(i - g) % COPIES], total)
                blocked.append(total)
        blocked.extend([jnp.zeros((NO, LANES), jnp.float32)] * (spans * COPIES - len(blocked)))
        pieces = []
        for span in range(spans):
            for u in range(COPIES // 2):
                for q in range(COPIES):
                    for v in range(2):
                        pieces.append(
                            blocked[span * COPIES + 2 * u + v][q * HI : (q + 1) * HI]
                        )
        return jnp.concatenate(pieces, axis=0).astype(jnp.bfloat16)

    def sigmas(k, right):
        left = []
        for span in range(spans):
            total = None
            for g in range(COPIES):
                pair = span * COPIES + g
                if pair < NB * ND:
                    at = (pair % ND) * NO
                    part = derivs[atoms[k] * NB + pair // ND, at : at + NO, :] * masks[g]
                    total = part if total is None else total + part
            left.append(total)
        own = dot(jnp.concatenate(left, axis=1), right)
        rows = [own[q * HI : (q + 1) * HI, :] for q in range(COPIES)]
        placed = []
        for g in range(groups):
            total = None
            for q in range(COPIES):
                shift = (q - g) % COPIES * NO
                part = pltpu.roll(rows[q], shift, axis=1) if shift else rows[q]
                total = part if total is None else jnp.where(row_group == q, part, total)
            placed.append(total)
        return placed

    rights = [middles(k) for k in range(len(atoms))]
    placed = []
    for k, right in enumerate(rights):
        placed.extend(sigmas(k, right))
    row, col = iota((LANES, LANES), 0), iota((LANES, LANES), 1)
    unmix = ones_where(col == (row - rest(row, NO)) + mixed(rest(row, NO)))
    return dot(jnp.concatenate(placed, axis=0).astype(jnp.bfloat16), unmix)


def sandwich_kernel(
    count, natoms, shares, neighbours_hbm, offsets_hbm, middle_planes,
    near_even, near_odd, far_odd, far_even, kernel, derivs, *refs,
):
    outs, own_blocks = refs[: shares - 1], refs[shares - 1]
    neighbours, offsets, planes, blocks, results, sems = refs[shares:]
    copies = [
        pltpu.make_async_copy(neighbours_hbm, neighbours, sems.at[0]),
        pltpu.make_async_copy(offsets_hbm, offsets, sems.at[1]),
    ]
    for copy in copies:
        copy.start()

    tiles = 2 * NO * NO // LANES
    groups = 2 * count
    order = row_matrix(tiles, natoms)
    place, length = lax.axis_index("energy"), lax.axis_size("energy")
    for ref, reach, odd in (
        (near_even, 1, 0), (near_odd, 1, 1), (far_odd, 2, 1), (far_even, 2, 0)
    ):
        other = neighbour(place, reach, odd)
        exists = ((other >= 0) & (other < length)).astype(jnp.float32)
        make_planes(ref, planes, (2 + other - place) * count, order, exists)
    planes[2 * count : 3 * count] = middle_planes[...]

    fold = fold_matrix()
    group = group_of(rest(iota(fold.shape, 1), LANES))
    places = [fold * ones_where(group == g) for g in range(COPIES)]
    for copy in copies:
        copy.wait()
    for half in range(2):
        branches = range(half * COPIES, min(NS, (half + 1) * COPIES))
        shifted_planes = [
            jnp.concatenate(
                [
                    planes[2 * count + e - (1 - 2 * (s % 2)) * offsets[s // 2]]
                    for e in range(count)
                ],
                axis=0,
            )
            for s in branches
        ]
        wide = dot(
            jnp.concatenate(shifted_planes, axis=1),
            jnp.concatenate(places[: len(branches)], axis=0),
        ).astype(jnp.bfloat16)
        for e in range(count):
            for atom in range(natoms):
                for q in range(COPIES):
                    at = (e * COPIES + q) * tiles
                    start = (e * natoms + atom) * tiles
                    blocks[atom, at : at + tiles, half * LANES : (half + 1) * LANES] = wide[
                        start : start + tiles, q * LANES : (q + 1) * LANES
                    ]

    me = lax.axis_index("mom")
    share = natoms // shares
    for k in range(share):
        for slot in range(NB):
            own_blocks[k * NB + slot] = blocks[neighbours[slot, me * share + k]]

    def one_share(step, carry):
        first = partner(me, step, shares) * share
        atoms = [first + k for k in range(share)]
        results[step] = share_terms(
            atoms, groups, lambda k, slot: blocks[neighbours[slot, atoms[k]]], kernel, derivs
        ).astype(jnp.bfloat16)
        return carry

    lax.fori_loop(1, shares, one_share, 0)
    for step in range(1, shares):
        outs[step - 1][...] = results[step]


def sandwich(window, middle_planes, kernel, derivs, neighbours, offsets, shares):
    count, natoms, size = window[0].shape
    groups = 2 * count
    share = natoms // shares
    rows = share * groups * HI
    return pl.pallas_call(
        functools.partial(sandwich_kernel, count, natoms, shares),
        out_shape=(jax.ShapeDtypeStruct((rows, LANES), jnp.bfloat16),) * (shares - 1)
        + (jax.ShapeDtypeStruct((share * NB, groups * NO, 2 * LANES), jnp.bfloat16),),
        in_specs=[pl.BlockSpec(memory_space=pltpu.HBM)] * 2
        + [pl.BlockSpec(memory_space=pltpu.VMEM)] * 7,
        out_specs=[pl.BlockSpec(memory_space=pltpu.VMEM)] * shares,
        scratch_shapes=[
            pltpu.SMEM(neighbours.shape, jnp.int32),
            pltpu.SMEM(offsets.shape, jnp.int32),
            pltpu.VMEM((5 * count, natoms * size // LANES, LANES), jnp.bfloat16),
            pltpu.VMEM((natoms, groups * NO, 2 * LANES), jnp.bfloat16),
            pltpu.VMEM((shares, rows, LANES), jnp.bfloat16),
            pltpu.SemaphoreType.DMA((2,)),
        ],
        compiler_params=pltpu.CompilerParams(vmem_limit_bytes=VMEM_LIMIT),
        cost_estimate=pl.CostEstimate(
            flops=800_000_000, bytes_accessed=7_000_000, transcendentals=0
        ),
        name="sandwich",
    )(
        in_hbm(neighbours), in_hbm(offsets),
        middle_planes, *window, kernel, derivs,
    )


def own_kernel(groups, blocks, kernel, derivs, out):
    share = blocks.shape[0] // NB
    first = lax.axis_index("mom") * share
    out[...] = share_terms(
        [first + k for k in range(share)], groups,
        lambda k, slot: blocks[k * NB + slot], kernel, derivs,
    )


def own_share(blocks, kernel, derivs):
    share = blocks.shape[0] // NB
    groups = blocks.shape[1] // NO
    return pl.pallas_call(
        functools.partial(own_kernel, groups),
        out_shape=jax.ShapeDtypeStruct((share * groups * HI, LANES), jnp.float32),
        in_specs=[pl.BlockSpec(memory_space=pltpu.VMEM)] * 3,
        out_specs=pl.BlockSpec(memory_space=pltpu.VMEM),
        compiler_params=pltpu.CompilerParams(vmem_limit_bytes=VMEM_LIMIT),
        cost_estimate=pl.CostEstimate(
            flops=200_000_000, bytes_accessed=2_000_000, transcendentals=0
        ),
        name="own_share",
    )(blocks, kernel, derivs)


def combine_kernel(own, *refs):
    parts, out, total = refs[:-2], refs[-2], refs[-1]
    count, share, width = out.shape
    tiles = width // LANES
    summed = own[...]
    for part in parts:
        summed = summed + part[...].astype(jnp.float32)
    total[...] = summed
    for e in range(count):
        for t in range(tiles):
            out[e, :, t * LANES : (t + 1) * LANES] = total[
                pl.ds(e * tiles + t, share, stride=count * tiles), :
            ]


def combine(own, parts, count, share):
    return pl.pallas_call(
        combine_kernel,
        out_shape=jax.ShapeDtypeStruct((count, share, 2 * NO * NO), jnp.float32),
        in_specs=[pl.BlockSpec(memory_space=pltpu.VMEM)] * (1 + len(parts)),
        out_specs=pl.BlockSpec(memory_space=pltpu.VMEM),
        scratch_shapes=[pltpu.VMEM(own.shape, jnp.float32)],
        compiler_params=pltpu.CompilerParams(vmem_limit_bytes=VMEM_LIMIT),
        name="combine",
    )(own, *parts)


def neighbour(index, reach, odd):
    return ((index + odd * reach) ^ reach) - odd * reach


def exchanged(array, axis, reach, odd):
    length = lax.axis_size(axis)
    others = [neighbour(i, reach, odd) for i in range(length)]
    pairs = [(i, other if 0 <= other < length else i) for i, other in enumerate(others)]
    return lax.ppermute(array, axis, pairs)


def body(green, coupling, gradient, neighbours, offsets):
    local = green[0]
    count, natoms, _ = local.shape
    shares = lax.axis_size("mom")
    remote = (
        exchanged(local, "energy", 1, 0),
        exchanged(local, "energy", 1, 1),
        exchanged(local, "energy", 2, 1),
        exchanged(local, "energy", 2, 0),
    )
    kernel, derivs, planes = tables(local, gradient, coupling.reshape(-1, 1, coupling.shape[-1]))
    *terms, own_blocks = sandwich(remote, planes, kernel, derivs, neighbours.T, offsets, shares)
    parts = [
        lax.ppermute(term, "mom", [(i, partner(i, step, shares)) for i in range(shares)])
        for step, term in enumerate(terms, 1)
    ]
    own = own_share(own_blocks, kernel, derivs)
    return combine(own, parts, count, natoms // shares)


def solution(mesh):
    in_specs = (P("mom", "energy", None, None), P("mom", None, None, None, None), P(), P(), P())
    out_specs = P("energy", "mom", None)
    return jax.shard_map(body, mesh=mesh, in_specs=in_specs, out_specs=out_specs, check_vma=False)
```

```python
import functools

import jax
import jax.numpy as jnp
from jax import lax
from jax.experimental import pallas as pl
from jax.experimental.pallas import tpu as pltpu
from jax.sharding import PartitionSpec as P

NO = 32
NB = 5
NW = 3
NS = 2 * NW
ND = 3
LANES = 128
COPIES = LANES // NO
HI = NO // COPIES
VMEM_LIMIT = 40 * 1024 * 1024

NT = (((1,), (1,)), ((), ()))


def in_hbm(array):
    return pltpu.with_memory_space_constraint(array, pltpu.HBM)


def iota(shape, dim):
    return lax.broadcasted_iota(jnp.int32, shape, dim)


def ones_where(condition):
    return jnp.where(condition, 1.0, 0.0).astype(jnp.bfloat16)


def over(value, size):
    return value >> (size.bit_length() - 1) if size & (size - 1) == 0 else value // size


def rest(value, size):
    return value & (size - 1) if size & (size - 1) == 0 else value % size


def mixed(lane):
    return rest(lane, HI) * COPIES + over(lane, HI)


def group_of(lane):
    return over(lane, 2 * NO) * 2 + rest(over(lane, HI), 2)


def orbital_of(lane):
    return rest(lane, HI) * COPIES + rest(over(lane, 2 * HI), COPIES)


def fold_matrix():
    shape = (LANES, COPIES * LANES)
    row, col = iota(shape, 0), iota(shape, 1)
    return ones_where(row == over(col, LANES) * NO + orbital_of(rest(col, LANES)))


def row_matrix(tiles, natoms):
    size = tiles * natoms
    row, col = iota((size, size), 0), iota((size, size), 1)
    return ones_where(col == rest(row, tiles) * natoms + over(row, tiles))


def stack_tiles(flat):
    return jnp.concatenate(
        [flat[:, t : t + LANES] for t in range(0, flat.shape[1], LANES)], axis=0
    )


def dot(left, right):
    return jnp.dot(left, right, preferred_element_type=jnp.float32)


def make_planes(block, planes, at, order):
    count = block.shape[0]
    ordered = dot(order, jnp.concatenate([stack_tiles(block[e]) for e in range(count)], axis=1))
    ordered = ordered.astype(jnp.bfloat16)
    for e in range(count):
        planes[at + e] = ordered[:, e * LANES : (e + 1) * LANES]


def weights_kernel(
    natoms, local_hbm, gradient_hbm, coupling_hbm, rows, planes_out, local_out, gradient_out,
    coupling, sems,
):
    copies = [
        pltpu.make_async_copy(coupling_hbm.at[:, 0, :], coupling, sems.at[0]),
        pltpu.make_async_copy(local_hbm, local_out, sems.at[1]),
        pltpu.make_async_copy(gradient_hbm, gradient_out, sems.at[2]),
    ]
    for copy in copies:
        copy.start()

    cells = ND * ND * NB
    depth = rows.shape[2]
    width = -(-NS * cells // LANES) * LANES
    lane = iota((width, 2 * LANES), 1)
    branch = over(lane, LANES) * COPIES + group_of(rest(lane, LANES))
    lane = iota((width, 2 * LANES), 0) - branch * cells
    widen = ones_where((lane >= 0) & (lane < cells) & (branch < NS))
    line, lane = iota((NB * depth, width), 0), iota((NB * depth, width), 1)
    lane = lane - (rest(line, depth) * NB + over(line, depth))
    chosen = lane == 0
    for s in range(1, NS):
        chosen = chosen | (lane == s * cells)
    order = row_matrix(2 * NO * NO // LANES, natoms)

    copies[0].wait()
    copies[1].wait()
    make_planes(local_out, planes_out, 0, order)
    table = jnp.transpose(coupling[...])
    table = jnp.concatenate(
        [table, jnp.zeros((natoms, width - NS * cells), jnp.float32)], axis=1
    )
    lefts = [
        jnp.where(chosen, table[atom : atom + 1, :], 0.0).astype(jnp.bfloat16)
        for atom in range(natoms)
    ]
    wide = dot(jnp.concatenate(lefts, axis=0), widen)
    for at in range(natoms * NB):
        for half in range(2):
            rows[at, half] = wide[
                at * depth : (at + 1) * depth, half * LANES : (half + 1) * LANES
            ]
    copies[2].wait()


def slots_kernel(natoms, gradient, local, received, derivs_out, local_out, planes_out):
    local_out[...] = local[...]
    make_planes(received, planes_out, 0, row_matrix(received.shape[2] // LANES, natoms))
    tiles = NO * NO // LANES
    block = natoms * tiles
    fold = fold_matrix()
    order = row_matrix(tiles, natoms)
    flats = [stack_tiles(gradient[slot, j]) for slot in range(NB) for j in range(ND)]
    ordered = dot(order, jnp.concatenate(flats, axis=1)).astype(jnp.bfloat16)
    stacked = [ordered[:, at : at + LANES] for at in range(0, NB * ND * LANES, LANES)]
    wide = dot(jnp.concatenate(stacked, axis=0), fold)
    for slot in range(NB):
        for j in range(ND):
            for atom in range(natoms):
                at = (slot * ND + j) * block + atom * tiles
                derivs_out[atom * NB + slot, j * NO : (j + 1) * NO, :] = jnp.concatenate(
                    [
                        wide[at : at + tiles, q * LANES : (q + 1) * LANES]
                        for q in range(COPIES)
                    ],
                    axis=0,
                ).astype(jnp.bfloat16)


def tables_kernel(rows, derivs_in, local, received, kernel_out, local_out, planes_out):
    local_out[...] = local[...]
    make_planes(
        received, planes_out, 0, row_matrix(received.shape[2] // LANES, received.shape[1])
    )

    def one_cell(at, carry):
        derivs = [derivs_in[at, j * NO : (j + 1) * NO, :] for j in range(ND)]
        for i in range(ND):
            for half in range(2):
                total = None
                for j in range(ND):
                    row = rows[at, half, ND * i + j : ND * i + j + 1, :]
                    weight = jnp.broadcast_to(row, (NO, LANES)).astype(jnp.bfloat16)
                    term = derivs[j] * weight
                    total = term if total is None else total + term
                kernel_out[at, i * NO : (i + 1) * NO, half * LANES : (half + 1) * LANES] = total
        return carry

    lax.fori_loop(0, kernel_out.shape[0], one_cell, 0, unroll=4)


def on_device(kernel, name, outs, flops, scratch=()):
    def call(*operands, hbm=()):
        spaces = [pltpu.HBM] * len(hbm) + [pltpu.VMEM] * len(operands)
        return pl.pallas_call(
            kernel,
            out_shape=outs,
            in_specs=[pl.BlockSpec(memory_space=space) for space in spaces],
            out_specs=jax.tree.map(lambda _: pl.BlockSpec(memory_space=pltpu.VMEM), outs),
            scratch_shapes=list(scratch),
            compiler_params=pltpu.CompilerParams(vmem_limit_bytes=VMEM_LIMIT),
            cost_estimate=pl.CostEstimate(
                flops=flops, bytes_accessed=6_000_000, transcendentals=0
            ),
            name=name,
        )(*[in_hbm(array) for array in hbm], *operands)

    return call


def planes_of(block):
    energies, natoms, size = block.shape
    return jax.ShapeDtypeStruct((energies, natoms * size // LANES, LANES), block.dtype)


def like(array):
    return jax.ShapeDtypeStruct(array.shape, array.dtype)


def weights(local, gradient, coupling):
    count = NB * local.shape[1]
    return on_device(
        functools.partial(weights_kernel, local.shape[1]), "weights",
        (
            jax.ShapeDtypeStruct((count, 2, 2 * HI, LANES), jnp.float32),
            planes_of(local), like(local), like(gradient),
        ),
        200_000_000,
        (
            pltpu.VMEM((coupling.shape[0], local.shape[1]), jnp.float32),
            pltpu.SemaphoreType.DMA((3,)),
        ),
    )(hbm=(local, gradient, coupling))


def slots(gradient, local, received):
    natoms = gradient.shape[2]
    derivs = jax.ShapeDtypeStruct((NB * natoms, ND * NO, LANES), jnp.bfloat16)
    return on_device(
        functools.partial(slots_kernel, natoms), "slots",
        (derivs, like(local), planes_of(received)), 200_000_000,
    )(gradient, local, received)


def tables(rows, derivs, local, received):
    kernel = jax.ShapeDtypeStruct((rows.shape[0], ND * NO, 2 * LANES), jnp.bfloat16)
    return on_device(
        tables_kernel, "tables",
        (kernel, like(local), planes_of(received)), 200_000_000,
    )(rows, derivs, local, received)


def partner(index, step, size):
    return index ^ step if size & (size - 1) == 0 else (index + step) % size


def share_terms(atoms, groups, block_of, kernel, derivs):
    tiles = groups * HI // 2
    lane_group = group_of(iota((NO, LANES), 1))
    masks = [ones_where(lane_group == g) for g in range(COPIES)]
    group = over(iota((NO, LANES), 1), NO)
    row_group = over(iota((HI, LANES), 1), NO)
    spans = -(-NB * ND // COPIES)

    def middles(k):
        blocked = []
        for slot in range(NB):
            wide = lax.dot_general(
                block_of(k, slot), kernel[atoms[k] * NB + slot], NT,
                preferred_element_type=jnp.float32,
            )
            wide = jnp.concatenate(
                [wide, jnp.zeros((groups * NO, LANES - ND * NO), jnp.float32)], axis=1
            )
            rows = []
            for g in range(groups):
                starts = [((g // 2) * COPIES + q) * tiles + (g % 2) * HI for q in range(COPIES)]
                rows.append(jnp.concatenate([wide[at : at + HI] for at in starts], axis=0))
            turned = []
            for d in range(COPIES):
                total = rows[-d % COPIES]
                for lane in range(1, COPIES):
                    total = jnp.where(group == lane, rows[(lane - d) % COPIES], total)
                turned.append(pltpu.roll(total, (COPIES - d) * NO, axis=1) if d else total)
            for i in range(ND):
                total = turned[i]
                for g in range(1, groups):
                    total = jnp.where(group == g, turned[(i - g) % COPIES], total)
                blocked.append(total)
        blocked.extend([jnp.zeros((NO, LANES), jnp.float32)] * (spans * COPIES - len(blocked)))
        pieces = []
        for span in range(spans):
            for u in range(COPIES // 2):
                for q in range(COPIES):
                    for v in range(2):
                        pieces.append(
                            blocked[span * COPIES + 2 * u + v][q * HI : (q + 1) * HI]
                        )
        return jnp.concatenate(pieces, axis=0).astype(jnp.bfloat16)

    def sigmas(k, right):
        left = []
        for span in range(spans):
            total = None
            for g in range(COPIES):
                pair = span * COPIES + g
                if pair < NB * ND:
                    at = (pair % ND) * NO
                    part = derivs[atoms[k] * NB + pair // ND, at : at + NO, :] * masks[g]
                    total = part if total is None else total + part
            left.append(total)
        own = dot(jnp.concatenate(left, axis=1), right)
        rows = [own[q * HI : (q + 1) * HI, :] for q in range(COPIES)]
        placed = []
        for g in range(groups):
            total = None
            for q in range(COPIES):
                shift = (q - g) % COPIES * NO
                part = pltpu.roll(rows[q], shift, axis=1) if shift else rows[q]
                total = part if total is None else jnp.where(row_group == q, part, total)
            placed.append(total)
        return placed

    rights = [middles(k) for k in range(len(atoms))]
    placed = []
    for k, right in enumerate(rights):
        placed.extend(sigmas(k, right))
    row, col = iota((LANES, LANES), 0), iota((LANES, LANES), 1)
    unmix = ones_where(col == (row - rest(row, NO)) + mixed(rest(row, NO)))
    return dot(jnp.concatenate(placed, axis=0).astype(jnp.bfloat16), unmix)


def sandwich_kernel(
    count, natoms, shares, neighbours_hbm, offsets_hbm, middle_planes,
    far_even, far_odd, near_odd, near_even, kernel, derivs, *refs,
):
    outs, own_blocks = refs[: shares - 1], refs[shares - 1]
    neighbours, offsets, planes, blocks, results, sems = refs[shares:]
    copies = [
        pltpu.make_async_copy(neighbours_hbm, neighbours, sems.at[0]),
        pltpu.make_async_copy(offsets_hbm, offsets, sems.at[1]),
    ]
    for copy in copies:
        copy.start()

    tiles = 2 * NO * NO // LANES
    groups = 2 * count
    order = row_matrix(tiles, natoms)
    place, length = lax.axis_index("energy"), lax.axis_size("energy")
    for ref, reach, odd in (
        (far_even, 2, 0), (far_odd, 2, 1), (near_odd, 1, 1), (near_even, 1, 0)
    ):
        other = neighbour(place, reach, odd)
        exists = (other >= 0) & (other < length)
        at = (2 + other - place) * count
        if reach == 1:
            make_planes(ref, planes, at, order)
        else:
            for e in range(count):
                planes[at + e] = ref[e]

        @pl.when(jnp.logical_not(exists))
        def _():
            for e in range(count):
                planes[at + e] = jnp.zeros(planes.shape[1:], planes.dtype)

    planes[2 * count : 3 * count] = middle_planes[...]

    fold = fold_matrix()
    group = group_of(rest(iota(fold.shape, 1), LANES))
    places = [fold * ones_where(group == g) for g in range(COPIES)]
    for copy in copies:
        copy.wait()
    for half in range(2):
        branches = range(half * COPIES, min(NS, (half + 1) * COPIES))
        shifted_planes = [
            jnp.concatenate(
                [
                    planes[2 * count + e - (1 - 2 * (s % 2)) * offsets[s // 2]]
                    for e in range(count)
                ],
                axis=0,
            )
            for s in branches
        ]
        wide = dot(
            jnp.concatenate(shifted_planes, axis=1),
            jnp.concatenate(places[: len(branches)], axis=0),
        ).astype(jnp.bfloat16)
        for e in range(count):
            for atom in range(natoms):
                for q in range(COPIES):
                    at = (e * COPIES + q) * tiles
                    start = (e * natoms + atom) * tiles
                    blocks[atom, at : at + tiles, half * LANES : (half + 1) * LANES] = wide[
                        start : start + tiles, q * LANES : (q + 1) * LANES
                    ]

    me = lax.axis_index("mom")
    share = natoms // shares
    for k in range(share):
        for slot in range(NB):
            own_blocks[k * NB + slot] = blocks[neighbours[slot, me * share + k]]

    def one_share(step, carry):
        first = partner(me, step, shares) * share
        atoms = [first + k for k in range(share)]
        results[step] = share_terms(
            atoms, groups, lambda k, slot: blocks[neighbours[slot, atoms[k]]], kernel, derivs
        ).astype(jnp.bfloat16)
        return carry

    lax.fori_loop(1, shares, one_share, 0)
    for step in range(1, shares):
        outs[step - 1][...] = results[step]


def sandwich(window, middle_planes, kernel, derivs, neighbours, offsets, shares):
    count, natoms, size = window[-1].shape
    groups = 2 * count
    share = natoms // shares
    rows = share * groups * HI
    return pl.pallas_call(
        functools.partial(sandwich_kernel, count, natoms, shares),
        out_shape=(jax.ShapeDtypeStruct((rows, LANES), jnp.bfloat16),) * (shares - 1)
        + (jax.ShapeDtypeStruct((share * NB, groups * NO, 2 * LANES), jnp.bfloat16),),
        in_specs=[pl.BlockSpec(memory_space=pltpu.HBM)] * 2
        + [pl.BlockSpec(memory_space=pltpu.VMEM)] * 7,
        out_specs=[pl.BlockSpec(memory_space=pltpu.VMEM)] * shares,
        scratch_shapes=[
            pltpu.SMEM(neighbours.shape, jnp.int32),
            pltpu.SMEM(offsets.shape, jnp.int32),
            pltpu.VMEM((5 * count, natoms * size // LANES, LANES), jnp.bfloat16),
            pltpu.VMEM((natoms, groups * NO, 2 * LANES), jnp.bfloat16),
            pltpu.VMEM((shares, rows, LANES), jnp.bfloat16),
            pltpu.SemaphoreType.DMA((2,)),
        ],
        compiler_params=pltpu.CompilerParams(vmem_limit_bytes=VMEM_LIMIT),
        cost_estimate=pl.CostEstimate(
            flops=800_000_000, bytes_accessed=7_000_000, transcendentals=0
        ),
        name="sandwich",
    )(
        in_hbm(neighbours), in_hbm(offsets),
        middle_planes, *window, kernel, derivs,
    )


def own_kernel(groups, blocks, kernel, derivs, out):
    share = blocks.shape[0] // NB
    first = lax.axis_index("mom") * share
    out[...] = share_terms(
        [first + k for k in range(share)], groups,
        lambda k, slot: blocks[k * NB + slot], kernel, derivs,
    )


def own_share(blocks, kernel, derivs):
    share = blocks.shape[0] // NB
    groups = blocks.shape[1] // NO
    return pl.pallas_call(
        functools.partial(own_kernel, groups),
        out_shape=jax.ShapeDtypeStruct((share * groups * HI, LANES), jnp.float32),
        in_specs=[pl.BlockSpec(memory_space=pltpu.VMEM)] * 3,
        out_specs=pl.BlockSpec(memory_space=pltpu.VMEM),
        compiler_params=pltpu.CompilerParams(vmem_limit_bytes=VMEM_LIMIT),
        cost_estimate=pl.CostEstimate(
            flops=200_000_000, bytes_accessed=2_000_000, transcendentals=0
        ),
        name="own_share",
    )(blocks, kernel, derivs)


def combine_kernel(own, *refs):
    parts, out, total = refs[:-2], refs[-2], refs[-1]
    count, share, width = out.shape
    tiles = width // LANES
    summed = own[...]
    for part in parts:
        summed = summed + part[...].astype(jnp.float32)
    total[...] = summed
    for e in range(count):
        for t in range(tiles):
            out[e, :, t * LANES : (t + 1) * LANES] = total[
                pl.ds(e * tiles + t, share, stride=count * tiles), :
            ]


def combine(own, parts, count, share):
    return pl.pallas_call(
        combine_kernel,
        out_shape=jax.ShapeDtypeStruct((count, share, 2 * NO * NO), jnp.float32),
        in_specs=[pl.BlockSpec(memory_space=pltpu.VMEM)] * (1 + len(parts)),
        out_specs=pl.BlockSpec(memory_space=pltpu.VMEM),
        scratch_shapes=[pltpu.VMEM(own.shape, jnp.float32)],
        compiler_params=pltpu.CompilerParams(vmem_limit_bytes=VMEM_LIMIT),
        name="combine",
    )(own, *parts)


def neighbour(index, reach, odd):
    return ((index + odd * reach) ^ reach) - odd * reach


def exchanged(array, axis, reach, odd):
    length = lax.axis_size(axis)
    others = [neighbour(i, reach, odd) for i in range(length)]
    pairs = [(i, other if 0 <= other < length else i) for i, other in enumerate(others)]
    return lax.ppermute(array, axis, pairs)


def body(green, coupling, gradient, neighbours, offsets):
    local = green[0]
    count, natoms, _ = local.shape
    shares = lax.axis_size("mom")
    far_even = exchanged(local, "energy", 2, 0)
    rows, planes, local, gradient = weights(
        local, gradient, coupling.reshape(-1, 1, coupling.shape[-1])
    )
    far_odd = exchanged(local, "energy", 2, 1)
    derivs, local, far_even = slots(gradient, local, far_even)
    near_odd = exchanged(local, "energy", 1, 1)
    kernel, local, far_odd = tables(rows, derivs, local, far_odd)
    near_even = exchanged(local, "energy", 1, 0)
    remote = (far_even, far_odd, near_odd, near_even)
    *terms, own_blocks = sandwich(remote, planes, kernel, derivs, neighbours.T, offsets, shares)
    parts = [
        lax.ppermute(term, "mom", [(i, partner(i, step, shares)) for i in range(shares)])
        for step, term in enumerate(terms, 1)
    ]
    own = own_share(own_blocks, kernel, derivs)
    return combine(own, parts, count, natoms // shares)


def solution(mesh):
    in_specs = (P("mom", "energy", None, None), P("mom", None, None, None, None), P(), P(), P())
    out_specs = P("energy", "mom", None)
    return jax.shard_map(body, mesh=mesh, in_specs=in_specs, out_specs=out_specs, check_vma=False)
```

```python
import functools

import jax
import jax.numpy as jnp
from jax import lax
from jax.experimental import pallas as pl
from jax.experimental.pallas import tpu as pltpu
from jax.sharding import PartitionSpec as P

NO = 32
NB = 5
NW = 3
NS = 2 * NW
ND = 3
LANES = 128
COPIES = LANES // NO
HI = NO // COPIES
VMEM_LIMIT = 40 * 1024 * 1024

NT = (((1,), (1,)), ((), ()))


def in_hbm(array):
    return pltpu.with_memory_space_constraint(array, pltpu.HBM)


def iota(shape, dim):
    return lax.broadcasted_iota(jnp.int32, shape, dim)


def ones_where(condition):
    return jnp.where(condition, 1.0, 0.0).astype(jnp.bfloat16)


def over(value, size):
    return value >> (size.bit_length() - 1) if size & (size - 1) == 0 else value // size


def rest(value, size):
    return value & (size - 1) if size & (size - 1) == 0 else value % size


def mixed(lane):
    return rest(lane, HI) * COPIES + over(lane, HI)


def group_of(lane):
    return over(lane, 2 * NO) * 2 + rest(over(lane, HI), 2)


def orbital_of(lane):
    return rest(lane, HI) * COPIES + rest(over(lane, 2 * HI), COPIES)


def fold_matrix():
    shape = (LANES, COPIES * LANES)
    row, col = iota(shape, 0), iota(shape, 1)
    return ones_where(row == over(col, LANES) * NO + orbital_of(rest(col, LANES)))


def row_matrix(tiles, natoms):
    size = tiles * natoms
    row, col = iota((size, size), 0), iota((size, size), 1)
    return ones_where(col == rest(row, tiles) * natoms + over(row, tiles))


def stack_tiles(flat):
    return jnp.concatenate(
        [flat[:, t : t + LANES] for t in range(0, flat.shape[1], LANES)], axis=0
    )


def dot(left, right):
    return jnp.dot(left, right, preferred_element_type=jnp.float32)


def make_planes(block, planes, at, order, factor=None):
    count = block.shape[0]
    ordered = dot(order, jnp.concatenate([stack_tiles(block[e]) for e in range(count)], axis=1))
    if factor is not None:
        ordered = ordered * factor
    ordered = ordered.astype(jnp.bfloat16)
    for e in range(count):
        planes[at + e] = ordered[:, e * LANES : (e + 1) * LANES]


def tables_kernel(
    natoms, local_hbm, gradient_hbm, coupling_hbm, kernel_out, derivs_out, planes_out,
    local, gradient, coupling, rows, sems,
):
    copies = [
        pltpu.make_async_copy(coupling_hbm.at[:, 0, :], coupling, sems.at[0]),
        pltpu.make_async_copy(gradient_hbm, gradient, sems.at[1]),
        pltpu.make_async_copy(local_hbm, local, sems.at[2]),
    ]
    for copy in copies:
        copy.start()

    tiles = NO * NO // LANES
    block = natoms * tiles
    cells = ND * ND * NB
    depth = rows.shape[2]
    width = -(-NS * cells // LANES) * LANES
    fold = fold_matrix()
    order = row_matrix(tiles, natoms)
    lane = iota((width, 2 * LANES), 1)
    branch = over(lane, LANES) * COPIES + group_of(rest(lane, LANES))
    lane = iota((width, 2 * LANES), 0) - branch * cells
    widen = ones_where((lane >= 0) & (lane < cells) & (branch < NS))
    line, lane = iota((NB * depth, width), 0), iota((NB * depth, width), 1)
    lane = lane - (rest(line, depth) * NB + over(line, depth))
    chosen = lane == 0
    for s in range(1, NS):
        chosen = chosen | (lane == s * cells)

    copies[0].wait()
    table = jnp.transpose(coupling[...])
    table = jnp.concatenate(
        [table, jnp.zeros((natoms, width - NS * cells), jnp.float32)], axis=1
    )
    lefts = [
        jnp.where(chosen, table[atom : atom + 1, :], 0.0).astype(jnp.bfloat16)
        for atom in range(natoms)
    ]
    wide = dot(jnp.concatenate(lefts, axis=0), widen)
    for at in range(natoms * NB):
        for half in range(2):
            rows[at, half] = wide[
                at * depth : (at + 1) * depth, half * LANES : (half + 1) * LANES
            ]

    copies[1].wait()
    flats = [stack_tiles(gradient[slot, j]) for slot in range(NB) for j in range(ND)]
    ordered = dot(order, jnp.concatenate(flats, axis=1)).astype(jnp.bfloat16)
    stacked = [ordered[:, at : at + LANES] for at in range(0, NB * ND * LANES, LANES)]
    wide = dot(jnp.concatenate(stacked, axis=0), fold)
    for slot in range(NB):
        for j in range(ND):
            for atom in range(natoms):
                at = (slot * ND + j) * block + atom * tiles
                derivs_out[atom * NB + slot, j * NO : (j + 1) * NO, :] = jnp.concatenate(
                    [
                        wide[at : at + tiles, q * LANES : (q + 1) * LANES]
                        for q in range(COPIES)
                    ],
                    axis=0,
                ).astype(jnp.bfloat16)

    copies[2].wait()
    make_planes(local, planes_out, 0, row_matrix(2 * tiles, natoms))

    def one_cell(at, carry):
        derivs = [derivs_out[at, j * NO : (j + 1) * NO, :] for j in range(ND)]
        for i in range(ND):
            for half in range(2):
                total = None
                for j in range(ND):
                    row = rows[at, half, ND * i + j : ND * i + j + 1, :]
                    weight = jnp.broadcast_to(row, (NO, LANES)).astype(jnp.bfloat16)
                    term = derivs[j] * weight
                    total = term if total is None else total + term
                kernel_out[at, i * NO : (i + 1) * NO, half * LANES : (half + 1) * LANES] = total
        return carry

    lax.fori_loop(0, natoms * NB, one_cell, 0, unroll=4)


def tables(local, gradient, coupling):
    energies, natoms, size = local.shape
    count = NB * natoms
    return pl.pallas_call(
        functools.partial(tables_kernel, natoms),
        out_shape=(
            jax.ShapeDtypeStruct((count, ND * NO, 2 * LANES), jnp.bfloat16),
            jax.ShapeDtypeStruct((count, ND * NO, LANES), jnp.bfloat16),
            jax.ShapeDtypeStruct((energies, natoms * size // LANES, LANES), jnp.bfloat16),
        ),
        in_specs=[pl.BlockSpec(memory_space=pltpu.HBM)] * 3,
        out_specs=[pl.BlockSpec(memory_space=pltpu.VMEM)] * 3,
        scratch_shapes=[
            pltpu.VMEM(local.shape, local.dtype),
            pltpu.VMEM(gradient.shape, gradient.dtype),
            pltpu.VMEM((coupling.shape[0], natoms), jnp.float32),
            pltpu.VMEM((count, 2, 2 * HI, LANES), jnp.float32),
            pltpu.SemaphoreType.DMA((3,)),
        ],
        compiler_params=pltpu.CompilerParams(vmem_limit_bytes=VMEM_LIMIT),
        cost_estimate=pl.CostEstimate(
            flops=200_000_000, bytes_accessed=6_000_000, transcendentals=0
        ),
        name="tables",
    )(in_hbm(local), in_hbm(gradient), in_hbm(coupling))


def partner(index, step, size):
    return index ^ step if size & (size - 1) == 0 else (index + step) % size


def share_terms(atoms, groups, block_of, kernel, derivs):
    tiles = groups * HI // 2
    lane_group = group_of(iota((NO, LANES), 1))
    masks = [ones_where(lane_group == g) for g in range(COPIES)]
    group = over(iota((NO, LANES), 1), NO)
    row_group = over(iota((HI, LANES), 1), NO)
    spans = -(-NB * ND // COPIES)

    def middles(k):
        blocked = []
        for slot in range(NB):
            wide = lax.dot_general(
                block_of(k, slot), kernel[atoms[k] * NB + slot], NT,
                preferred_element_type=jnp.float32,
            )
            wide = jnp.concatenate(
                [wide, jnp.zeros((groups * NO, LANES - ND * NO), jnp.float32)], axis=1
            )
            rows = []
            for g in range(groups):
                starts = [((g // 2) * COPIES + q) * tiles + (g % 2) * HI for q in range(COPIES)]
                rows.append(jnp.concatenate([wide[at : at + HI] for at in starts], axis=0))
            turned = []
            for d in range(COPIES):
                total = rows[-d % COPIES]
                for lane in range(1, COPIES):
                    total = jnp.where(group == lane, rows[(lane - d) % COPIES], total)
                turned.append(pltpu.roll(total, (COPIES - d) * NO, axis=1) if d else total)
            for i in range(ND):
                total = turned[i]
                for g in range(1, groups):
                    total = jnp.where(group == g, turned[(i - g) % COPIES], total)
                blocked.append(total)
        blocked.extend([jnp.zeros((NO, LANES), jnp.float32)] * (spans * COPIES - len(blocked)))
        pieces = []
        for span in range(spans):
            for u in range(COPIES // 2):
                for q in range(COPIES):
                    for v in range(2):
                        pieces.append(
                            blocked[span * COPIES + 2 * u + v][q * HI : (q + 1) * HI]
                        )
        return jnp.concatenate(pieces, axis=0).astype(jnp.bfloat16)

    def sigmas(k, right):
        left = []
        for span in range(spans):
            total = None
            for g in range(COPIES):
                pair = span * COPIES + g
                if pair < NB * ND:
                    at = (pair % ND) * NO
                    part = derivs[atoms[k] * NB + pair // ND, at : at + NO, :] * masks[g]
                    total = part if total is None else total + part
            left.append(total)
        own = dot(jnp.concatenate(left, axis=1), right)
        rows = [own[q * HI : (q + 1) * HI, :] for q in range(COPIES)]
        placed = []
        for g in range(groups):
            total = None
            for q in range(COPIES):
                shift = (q - g) % COPIES * NO
                part = pltpu.roll(rows[q], shift, axis=1) if shift else rows[q]
                total = part if total is None else jnp.where(row_group == q, part, total)
            placed.append(total)
        return placed

    rights = [middles(k) for k in range(len(atoms))]
    placed = []
    for k, right in enumerate(rights):
        placed.extend(sigmas(k, right))
    row, col = iota((LANES, LANES), 0), iota((LANES, LANES), 1)
    unmix = ones_where(col == (row - rest(row, NO)) + mixed(rest(row, NO)))
    return dot(jnp.concatenate(placed, axis=0).astype(jnp.bfloat16), unmix)


def sandwich_kernel(
    count, natoms, shares, neighbours_hbm, offsets_hbm, middle_planes,
    near_odd, far_odd, far_even, near_even, kernel, derivs, *refs,
):
    outs, own_blocks = refs[: shares - 1], refs[shares - 1]
    neighbours, offsets, planes, blocks, results, sems = refs[shares:]
    copies = [
        pltpu.make_async_copy(neighbours_hbm, neighbours, sems.at[0]),
        pltpu.make_async_copy(offsets_hbm, offsets, sems.at[1]),
    ]
    for copy in copies:
        copy.start()

    tiles = 2 * NO * NO // LANES
    groups = 2 * count
    order = row_matrix(tiles, natoms)
    place, length = lax.axis_index("energy"), lax.axis_size("energy")
    for ref, reach, odd in (
        (near_odd, 1, 1), (far_odd, 2, 1), (far_even, 2, 0), (near_even, 1, 0)
    ):
        other = neighbour(place, reach, odd)
        exists = ((other >= 0) & (other < length)).astype(jnp.float32)
        make_planes(ref, planes, (2 + other - place) * count, order, exists)
    planes[2 * count : 3 * count] = middle_planes[...]

    fold = fold_matrix()
    group = group_of(rest(iota(fold.shape, 1), LANES))
    places = [fold * ones_where(group == g) for g in range(COPIES)]
    for copy in copies:
        copy.wait()
    for half in range(2):
        branches = range(half * COPIES, min(NS, (half + 1) * COPIES))
        shifted_planes = [
            jnp.concatenate(
                [
                    planes[2 * count + e - (1 - 2 * (s % 2)) * offsets[s // 2]]
                    for e in range(count)
                ],
                axis=0,
            )
            for s in branches
        ]
        wide = dot(
            jnp.concatenate(shifted_planes, axis=1),
            jnp.concatenate(places[: len(branches)], axis=0),
        ).astype(jnp.bfloat16)
        for e in range(count):
            for atom in range(natoms):
                for q in range(COPIES):
                    at = (e * COPIES + q) * tiles
                    start = (e * natoms + atom) * tiles
                    blocks[atom, at : at + tiles, half * LANES : (half + 1) * LANES] = wide[
                        start : start + tiles, q * LANES : (q + 1) * LANES
                    ]

    me = lax.axis_index("mom")
    share = natoms // shares
    for k in range(share):
        for slot in range(NB):
            own_blocks[k * NB + slot] = blocks[neighbours[slot, me * share + k]]

    def one_share(step, carry):
        first = partner(me, step, shares) * share
        atoms = [first + k for k in range(share)]
        results[step] = share_terms(
            atoms, groups, lambda k, slot: blocks[neighbours[slot, atoms[k]]], kernel, derivs
        ).astype(jnp.bfloat16)
        return carry

    lax.fori_loop(1, shares, one_share, 0)
    for step in range(1, shares):
        outs[step - 1][...] = results[step]


def sandwich(window, middle_planes, kernel, derivs, neighbours, offsets, shares):
    count, natoms, size = window[0].shape
    groups = 2 * count
    share = natoms // shares
    rows = share * groups * HI
    return pl.pallas_call(
        functools.partial(sandwich_kernel, count, natoms, shares),
        out_shape=(jax.ShapeDtypeStruct((rows, LANES), jnp.bfloat16),) * (shares - 1)
        + (jax.ShapeDtypeStruct((share * NB, groups * NO, 2 * LANES), jnp.bfloat16),),
        in_specs=[pl.BlockSpec(memory_space=pltpu.HBM)] * 2
        + [pl.BlockSpec(memory_space=pltpu.VMEM)] * 7,
        out_specs=[pl.BlockSpec(memory_space=pltpu.VMEM)] * shares,
        scratch_shapes=[
            pltpu.SMEM(neighbours.shape, jnp.int32),
            pltpu.SMEM(offsets.shape, jnp.int32),
            pltpu.VMEM((5 * count, natoms * size // LANES, LANES), jnp.bfloat16),
            pltpu.VMEM((natoms, groups * NO, 2 * LANES), jnp.bfloat16),
            pltpu.VMEM((shares, rows, LANES), jnp.bfloat16),
            pltpu.SemaphoreType.DMA((2,)),
        ],
        compiler_params=pltpu.CompilerParams(vmem_limit_bytes=VMEM_LIMIT),
        cost_estimate=pl.CostEstimate(
            flops=800_000_000, bytes_accessed=7_000_000, transcendentals=0
        ),
        name="sandwich",
    )(
        in_hbm(neighbours), in_hbm(offsets),
        middle_planes, *window, kernel, derivs,
    )


def own_kernel(groups, blocks, kernel, derivs, out):
    share = blocks.shape[0] // NB
    first = lax.axis_index("mom") * share
    out[...] = share_terms(
        [first + k for k in range(share)], groups,
        lambda k, slot: blocks[k * NB + slot], kernel, derivs,
    )


def own_share(blocks, kernel, derivs):
    share = blocks.shape[0] // NB
    groups = blocks.shape[1] // NO
    return pl.pallas_call(
        functools.partial(own_kernel, groups),
        out_shape=jax.ShapeDtypeStruct((share * groups * HI, LANES), jnp.float32),
        in_specs=[pl.BlockSpec(memory_space=pltpu.VMEM)] * 3,
        out_specs=pl.BlockSpec(memory_space=pltpu.VMEM),
        compiler_params=pltpu.CompilerParams(vmem_limit_bytes=VMEM_LIMIT),
        cost_estimate=pl.CostEstimate(
            flops=200_000_000, bytes_accessed=2_000_000, transcendentals=0
        ),
        name="own_share",
    )(blocks, kernel, derivs)


def combine_kernel(own, *refs):
    parts, out, total = refs[:-2], refs[-2], refs[-1]
    count, share, width = out.shape
    tiles = width // LANES
    summed = own[...]
    for part in parts:
        summed = summed + part[...].astype(jnp.float32)
    total[...] = summed
    for e in range(count):
        for t in range(tiles):
            out[e, :, t * LANES : (t + 1) * LANES] = total[
                pl.ds(e * tiles + t, share, stride=count * tiles), :
            ]


def combine(own, parts, count, share):
    return pl.pallas_call(
        combine_kernel,
        out_shape=jax.ShapeDtypeStruct((count, share, 2 * NO * NO), jnp.float32),
        in_specs=[pl.BlockSpec(memory_space=pltpu.VMEM)] * (1 + len(parts)),
        out_specs=pl.BlockSpec(memory_space=pltpu.VMEM),
        scratch_shapes=[pltpu.VMEM(own.shape, jnp.float32)],
        compiler_params=pltpu.CompilerParams(vmem_limit_bytes=VMEM_LIMIT),
        name="combine",
    )(own, *parts)


def neighbour(index, reach, odd):
    return ((index + odd * reach) ^ reach) - odd * reach


def exchanged(array, axis, reach, odd):
    length = lax.axis_size(axis)
    others = [neighbour(i, reach, odd) for i in range(length)]
    pairs = [(i, other if 0 <= other < length else i) for i, other in enumerate(others)]
    return lax.ppermute(array, axis, pairs)


def body(green, coupling, gradient, neighbours, offsets):
    local = green[0]
    count, natoms, _ = local.shape
    shares = lax.axis_size("mom")
    remote = (
        exchanged(local, "energy", 1, 1),
        exchanged(local, "energy", 2, 1),
        exchanged(local, "energy", 2, 0),
        exchanged(local, "energy", 1, 0),
    )
    kernel, derivs, planes = tables(local, gradient, coupling.reshape(-1, 1, coupling.shape[-1]))
    *terms, own_blocks = sandwich(remote, planes, kernel, derivs, neighbours.T, offsets, shares)
    parts = [
        lax.ppermute(term, "mom", [(i, partner(i, step, shares)) for i in range(shares)])
        for step, term in enumerate(terms, 1)
    ]
    own = own_share(own_blocks, kernel, derivs)
    return combine(own, parts, count, natoms // shares)


def solution(mesh):
    in_specs = (P("mom", "energy", None, None), P("mom", None, None, None, None), P(), P(), P())
    out_specs = P("energy", "mom", None)
    return jax.shard_map(body, mesh=mesh, in_specs=in_specs, out_specs=out_specs, check_vma=False)
```

```python
import functools

import jax
import jax.numpy as jnp
from jax import lax
from jax.experimental import pallas as pl
from jax.experimental.pallas import tpu as pltpu
from jax.sharding import PartitionSpec as P

NO = 32
NB = 5
NW = 3
NS = 2 * NW
ND = 3
LANES = 128
COPIES = LANES // NO
HI = NO // COPIES
VMEM_LIMIT = 40 * 1024 * 1024

NT = (((1,), (1,)), ((), ()))


def in_hbm(array):
    return pltpu.with_memory_space_constraint(array, pltpu.HBM)


def iota(shape, dim):
    return lax.broadcasted_iota(jnp.int32, shape, dim)


def ones_where(condition):
    return jnp.where(condition, 1.0, 0.0).astype(jnp.bfloat16)


def over(value, size):
    return value >> (size.bit_length() - 1) if size & (size - 1) == 0 else value // size


def rest(value, size):
    return value & (size - 1) if size & (size - 1) == 0 else value % size


def mixed(lane):
    return rest(lane, HI) * COPIES + over(lane, HI)


def group_of(lane):
    return over(lane, 2 * NO) * 2 + rest(over(lane, HI), 2)


def orbital_of(lane):
    return rest(lane, HI) * COPIES + rest(over(lane, 2 * HI), COPIES)


def fold_matrix():
    shape = (LANES, COPIES * LANES)
    row, col = iota(shape, 0), iota(shape, 1)
    return ones_where(row == over(col, LANES) * NO + orbital_of(rest(col, LANES)))


def row_matrix(tiles, natoms):
    size = tiles * natoms
    row, col = iota((size, size), 0), iota((size, size), 1)
    return ones_where(col == rest(row, tiles) * natoms + over(row, tiles))


def stack_tiles(flat):
    return jnp.concatenate(
        [flat[:, t : t + LANES] for t in range(0, flat.shape[1], LANES)], axis=0
    )


def dot(left, right):
    return jnp.dot(left, right, preferred_element_type=jnp.float32)


def make_planes(block, planes, at, order, factor=None):
    count = block.shape[0]
    ordered = dot(order, jnp.concatenate([stack_tiles(block[e]) for e in range(count)], axis=1))
    if factor is not None:
        ordered = ordered * factor
    ordered = ordered.astype(jnp.bfloat16)
    for e in range(count):
        planes[at + e] = ordered[:, e * LANES : (e + 1) * LANES]


def tables_kernel(
    natoms, local_hbm, gradient_hbm, coupling_hbm, kernel_out, derivs_out, planes_out,
    local, gradient, coupling, rows, sems,
):
    copies = [
        pltpu.make_async_copy(coupling_hbm.at[:, 0, :], coupling, sems.at[0]),
        pltpu.make_async_copy(gradient_hbm, gradient, sems.at[1]),
        pltpu.make_async_copy(local_hbm, local, sems.at[2]),
    ]
    for copy in copies:
        copy.start()

    tiles = NO * NO // LANES
    block = natoms * tiles
    cells = ND * ND * NB
    depth = rows.shape[2]
    width = -(-NS * cells // LANES) * LANES
    fold = fold_matrix()
    order = row_matrix(tiles, natoms)
    lane = iota((width, 2 * LANES), 1)
    branch = over(lane, LANES) * COPIES + group_of(rest(lane, LANES))
    lane = iota((width, 2 * LANES), 0) - branch * cells
    widen = ones_where((lane >= 0) & (lane < cells) & (branch < NS))
    line, lane = iota((NB * depth, width), 0), iota((NB * depth, width), 1)
    lane = lane - (rest(line, depth) * NB + over(line, depth))
    chosen = lane == 0
    for s in range(1, NS):
        chosen = chosen | (lane == s * cells)

    copies[0].wait()
    table = jnp.transpose(coupling[...])
    table = jnp.concatenate(
        [table, jnp.zeros((natoms, width - NS * cells), jnp.float32)], axis=1
    )
    lefts = [
        jnp.where(chosen, table[atom : atom + 1, :], 0.0).astype(jnp.bfloat16)
        for atom in range(natoms)
    ]
    wide = dot(jnp.concatenate(lefts, axis=0), widen)
    for at in range(natoms * NB):
        for half in range(2):
            rows[at, half] = wide[
                at * depth : (at + 1) * depth, half * LANES : (half + 1) * LANES
            ]

    copies[1].wait()
    flats = [stack_tiles(gradient[slot, j]) for slot in range(NB) for j in range(ND)]
    ordered = dot(order, jnp.concatenate(flats, axis=1)).astype(jnp.bfloat16)
    stacked = [ordered[:, at : at + LANES] for at in range(0, NB * ND * LANES, LANES)]
    wide = dot(jnp.concatenate(stacked, axis=0), fold)
    for slot in range(NB):
        for j in range(ND):
            for atom in range(natoms):
                at = (slot * ND + j) * block + atom * tiles
                derivs_out[atom * NB + slot, j * NO : (j + 1) * NO, :] = jnp.concatenate(
                    [
                        wide[at : at + tiles, q * LANES : (q + 1) * LANES]
                        for q in range(COPIES)
                    ],
                    axis=0,
                ).astype(jnp.bfloat16)

    copies[2].wait()
    make_planes(local, planes_out, 0, row_matrix(2 * tiles, natoms))

    def one_cell(at, carry):
        derivs = [derivs_out[at, j * NO : (j + 1) * NO, :] for j in range(ND)]
        for i in range(ND):
            for half in range(2):
                total = None
                for j in range(ND):
                    row = rows[at, half, ND * i + j : ND * i + j + 1, :]
                    weight = jnp.broadcast_to(row, (NO, LANES)).astype(jnp.bfloat16)
                    term = derivs[j] * weight
                    total = term if total is None else total + term
                kernel_out[at, i * NO : (i + 1) * NO, half * LANES : (half + 1) * LANES] = total
        return carry

    lax.fori_loop(0, natoms * NB, one_cell, 0, unroll=4)


def tables(local, gradient, coupling):
    energies, natoms, size = local.shape
    count = NB * natoms
    return pl.pallas_call(
        functools.partial(tables_kernel, natoms),
        out_shape=(
            jax.ShapeDtypeStruct((count, ND * NO, 2 * LANES), jnp.bfloat16),
            jax.ShapeDtypeStruct((count, ND * NO, LANES), jnp.bfloat16),
            jax.ShapeDtypeStruct((energies, natoms * size // LANES, LANES), jnp.bfloat16),
        ),
        in_specs=[pl.BlockSpec(memory_space=pltpu.HBM)] * 3,
        out_specs=[pl.BlockSpec(memory_space=pltpu.VMEM)] * 3,
        scratch_shapes=[
            pltpu.VMEM(local.shape, local.dtype),
            pltpu.VMEM(gradient.shape, gradient.dtype),
            pltpu.VMEM((coupling.shape[0], natoms), jnp.float32),
            pltpu.VMEM((count, 2, 2 * HI, LANES), jnp.float32),
            pltpu.SemaphoreType.DMA((3,)),
        ],
        compiler_params=pltpu.CompilerParams(vmem_limit_bytes=VMEM_LIMIT),
        cost_estimate=pl.CostEstimate(
            flops=200_000_000, bytes_accessed=6_000_000, transcendentals=0
        ),
        name="tables",
    )(in_hbm(local), in_hbm(gradient), in_hbm(coupling))


def partner(index, step, size):
    return index ^ step if size & (size - 1) == 0 else (index + step) % size


def share_terms(atoms, groups, block_of, kernel, derivs):
    tiles = groups * HI // 2
    lane_group = group_of(iota((NO, LANES), 1))
    masks = [ones_where(lane_group == g) for g in range(COPIES)]
    group = over(iota((NO, LANES), 1), NO)
    row_group = over(iota((HI, LANES), 1), NO)
    spans = -(-NB * ND // COPIES)

    def middles(k):
        blocked = []
        for slot in range(NB):
            wide = lax.dot_general(
                block_of(k, slot), kernel[atoms[k] * NB + slot], NT,
                preferred_element_type=jnp.float32,
            )
            wide = jnp.concatenate(
                [wide, jnp.zeros((groups * NO, LANES - ND * NO), jnp.float32)], axis=1
            )
            rows = []
            for g in range(groups):
                starts = [((g // 2) * COPIES + q) * tiles + (g % 2) * HI for q in range(COPIES)]
                rows.append(jnp.concatenate([wide[at : at + HI] for at in starts], axis=0))
            turned = []
            for d in range(COPIES):
                total = rows[-d % COPIES]
                for lane in range(1, COPIES):
                    total = jnp.where(group == lane, rows[(lane - d) % COPIES], total)
                turned.append(pltpu.roll(total, (COPIES - d) * NO, axis=1) if d else total)
            for i in range(ND):
                total = turned[i]
                for g in range(1, groups):
                    total = jnp.where(group == g, turned[(i - g) % COPIES], total)
                blocked.append(total)
        blocked.extend([jnp.zeros((NO, LANES), jnp.float32)] * (spans * COPIES - len(blocked)))
        pieces = []
        for span in range(spans):
            for u in range(COPIES // 2):
                for q in range(COPIES):
                    for v in range(2):
                        pieces.append(
                            blocked[span * COPIES + 2 * u + v][q * HI : (q + 1) * HI]
                        )
        return jnp.concatenate(pieces, axis=0).astype(jnp.bfloat16)

    def sigmas(k, right):
        left = []
        for span in range(spans):
            total = None
            for g in range(COPIES):
                pair = span * COPIES + g
                if pair < NB * ND:
                    at = (pair % ND) * NO
                    part = derivs[atoms[k] * NB + pair // ND, at : at + NO, :] * masks[g]
                    total = part if total is None else total + part
            left.append(total)
        own = dot(jnp.concatenate(left, axis=1), right)
        rows = [own[q * HI : (q + 1) * HI, :] for q in range(COPIES)]
        placed = []
        for g in range(groups):
            total = None
            for q in range(COPIES):
                shift = (q - g) % COPIES * NO
                part = pltpu.roll(rows[q], shift, axis=1) if shift else rows[q]
                total = part if total is None else jnp.where(row_group == q, part, total)
            placed.append(total)
        return placed

    rights = [middles(k) for k in range(len(atoms))]
    placed = []
    for k, right in enumerate(rights):
        placed.extend(sigmas(k, right))
    row, col = iota((LANES, LANES), 0), iota((LANES, LANES), 1)
    unmix = ones_where(col == (row - rest(row, NO)) + mixed(rest(row, NO)))
    return dot(jnp.concatenate(placed, axis=0).astype(jnp.bfloat16), unmix)


def sandwich_kernel(
    count, natoms, shares, neighbours_hbm, offsets_hbm, middle_planes,
    near_even, far_odd, far_even, near_odd, kernel, derivs, *refs,
):
    outs, own_blocks = refs[: shares - 1], refs[shares - 1]
    neighbours, offsets, planes, blocks, results, sems = refs[shares:]
    copies = [
        pltpu.make_async_copy(neighbours_hbm, neighbours, sems.at[0]),
        pltpu.make_async_copy(offsets_hbm, offsets, sems.at[1]),
    ]
    for copy in copies:
        copy.start()

    tiles = 2 * NO * NO // LANES
    groups = 2 * count
    order = row_matrix(tiles, natoms)
    place, length = lax.axis_index("energy"), lax.axis_size("energy")
    for ref, reach, odd in (
        (near_even, 1, 0), (far_odd, 2, 1), (far_even, 2, 0), (near_odd, 1, 1)
    ):
        other = neighbour(place, reach, odd)
        exists = ((other >= 0) & (other < length)).astype(jnp.float32)
        make_planes(ref, planes, (2 + other - place) * count, order, exists)
    planes[2 * count : 3 * count] = middle_planes[...]

    fold = fold_matrix()
    group = group_of(rest(iota(fold.shape, 1), LANES))
    places = [fold * ones_where(group == g) for g in range(COPIES)]
    for copy in copies:
        copy.wait()
    for half in range(2):
        branches = range(half * COPIES, min(NS, (half + 1) * COPIES))
        shifted_planes = [
            jnp.concatenate(
                [
                    planes[2 * count + e - (1 - 2 * (s % 2)) * offsets[s // 2]]
                    for e in range(count)
                ],
                axis=0,
            )
            for s in branches
        ]
        wide = dot(
            jnp.concatenate(shifted_planes, axis=1),
            jnp.concatenate(places[: len(branches)], axis=0),
        ).astype(jnp.bfloat16)
        for e in range(count):
            for atom in range(natoms):
                for q in range(COPIES):
                    at = (e * COPIES + q) * tiles
                    start = (e * natoms + atom) * tiles
                    blocks[atom, at : at + tiles, half * LANES : (half + 1) * LANES] = wide[
                        start : start + tiles, q * LANES : (q + 1) * LANES
                    ]

    me = lax.axis_index("mom")
    share = natoms // shares
    for k in range(share):
        for slot in range(NB):
            own_blocks[k * NB + slot] = blocks[neighbours[slot, me * share + k]]

    def one_share(step, carry):
        first = partner(me, step, shares) * share
        atoms = [first + k for k in range(share)]
        results[step] = share_terms(
            atoms, groups, lambda k, slot: blocks[neighbours[slot, atoms[k]]], kernel, derivs
        ).astype(jnp.bfloat16)
        return carry

    lax.fori_loop(1, shares, one_share, 0)
    for step in range(1, shares):
        outs[step - 1][...] = results[step]


def sandwich(window, middle_planes, kernel, derivs, neighbours, offsets, shares):
    count, natoms, size = window[0].shape
    groups = 2 * count
    share = natoms // shares
    rows = share * groups * HI
    return pl.pallas_call(
        functools.partial(sandwich_kernel, count, natoms, shares),
        out_shape=(jax.ShapeDtypeStruct((rows, LANES), jnp.bfloat16),) * (shares - 1)
        + (jax.ShapeDtypeStruct((share * NB, groups * NO, 2 * LANES), jnp.bfloat16),),
        in_specs=[pl.BlockSpec(memory_space=pltpu.HBM)] * 2
        + [pl.BlockSpec(memory_space=pltpu.VMEM)] * 7,
        out_specs=[pl.BlockSpec(memory_space=pltpu.VMEM)] * shares,
        scratch_shapes=[
            pltpu.SMEM(neighbours.shape, jnp.int32),
            pltpu.SMEM(offsets.shape, jnp.int32),
            pltpu.VMEM((5 * count, natoms * size // LANES, LANES), jnp.bfloat16),
            pltpu.VMEM((natoms, groups * NO, 2 * LANES), jnp.bfloat16),
            pltpu.VMEM((shares, rows, LANES), jnp.bfloat16),
            pltpu.SemaphoreType.DMA((2,)),
        ],
        compiler_params=pltpu.CompilerParams(vmem_limit_bytes=VMEM_LIMIT),
        cost_estimate=pl.CostEstimate(
            flops=800_000_000, bytes_accessed=7_000_000, transcendentals=0
        ),
        name="sandwich",
    )(
        in_hbm(neighbours), in_hbm(offsets),
        middle_planes, *window, kernel, derivs,
    )


def own_kernel(groups, blocks, kernel, derivs, out):
    share = blocks.shape[0] // NB
    first = lax.axis_index("mom") * share
    out[...] = share_terms(
        [first + k for k in range(share)], groups,
        lambda k, slot: blocks[k * NB + slot], kernel, derivs,
    )


def own_share(blocks, kernel, derivs):
    share = blocks.shape[0] // NB
    groups = blocks.shape[1] // NO
    return pl.pallas_call(
        functools.partial(own_kernel, groups),
        out_shape=jax.ShapeDtypeStruct((share * groups * HI, LANES), jnp.float32),
        in_specs=[pl.BlockSpec(memory_space=pltpu.VMEM)] * 3,
        out_specs=pl.BlockSpec(memory_space=pltpu.VMEM),
        compiler_params=pltpu.CompilerParams(vmem_limit_bytes=VMEM_LIMIT),
        cost_estimate=pl.CostEstimate(
            flops=200_000_000, bytes_accessed=2_000_000, transcendentals=0
        ),
        name="own_share",
    )(blocks, kernel, derivs)


def combine_kernel(own, *refs):
    parts, out, total = refs[:-2], refs[-2], refs[-1]
    count, share, width = out.shape
    tiles = width // LANES
    summed = own[...]
    for part in parts:
        summed = summed + part[...].astype(jnp.float32)
    total[...] = summed
    for e in range(count):
        for t in range(tiles):
            out[e, :, t * LANES : (t + 1) * LANES] = total[
                pl.ds(e * tiles + t, share, stride=count * tiles), :
            ]


def combine(own, parts, count, share):
    return pl.pallas_call(
        combine_kernel,
        out_shape=jax.ShapeDtypeStruct((count, share, 2 * NO * NO), jnp.float32),
        in_specs=[pl.BlockSpec(memory_space=pltpu.VMEM)] * (1 + len(parts)),
        out_specs=pl.BlockSpec(memory_space=pltpu.VMEM),
        scratch_shapes=[pltpu.VMEM(own.shape, jnp.float32)],
        compiler_params=pltpu.CompilerParams(vmem_limit_bytes=VMEM_LIMIT),
        name="combine",
    )(own, *parts)


def neighbour(index, reach, odd):
    return ((index + odd * reach) ^ reach) - odd * reach


def exchanged(array, axis, reach, odd):
    length = lax.axis_size(axis)
    others = [neighbour(i, reach, odd) for i in range(length)]
    pairs = [(i, other if 0 <= other < length else i) for i, other in enumerate(others)]
    return lax.ppermute(array, axis, pairs)


def body(green, coupling, gradient, neighbours, offsets):
    local = green[0]
    count, natoms, _ = local.shape
    shares = lax.axis_size("mom")
    remote = (
        exchanged(local, "energy", 1, 0),
        exchanged(local, "energy", 2, 1),
        exchanged(local, "energy", 2, 0),
        exchanged(local, "energy", 1, 1),
    )
    kernel, derivs, planes = tables(local, gradient, coupling.reshape(-1, 1, coupling.shape[-1]))
    *terms, own_blocks = sandwich(remote, planes, kernel, derivs, neighbours.T, offsets, shares)
    parts = [
        lax.ppermute(term, "mom", [(i, partner(i, step, shares)) for i in range(shares)])
        for step, term in enumerate(terms, 1)
    ]
    own = own_share(own_blocks, kernel, derivs)
    return combine(own, parts, count, natoms // shares)


def solution(mesh):
    in_specs = (P("mom", "energy", None, None), P("mom", None, None, None, None), P(), P(), P())
    out_specs = P("energy", "mom", None)
    return jax.shard_map(body, mesh=mesh, in_specs=in_specs, out_specs=out_specs, check_vma=False)
```

```python
import functools

import jax
import jax.numpy as jnp
from jax import lax
from jax.experimental import pallas as pl
from jax.experimental.pallas import tpu as pltpu
from jax.sharding import PartitionSpec as P

NO = 32
NB = 5
NW = 3
NS = 2 * NW
ND = 3
LANES = 128
COPIES = LANES // NO
HI = NO // COPIES
VMEM_LIMIT = 40 * 1024 * 1024

NT = (((1,), (1,)), ((), ()))


def in_hbm(array):
    return pltpu.with_memory_space_constraint(array, pltpu.HBM)


def iota(shape, dim):
    return lax.broadcasted_iota(jnp.int32, shape, dim)


def ones_where(condition):
    return jnp.where(condition, 1.0, 0.0).astype(jnp.bfloat16)


def over(value, size):
    return value >> (size.bit_length() - 1) if size & (size - 1) == 0 else value // size


def rest(value, size):
    return value & (size - 1) if size & (size - 1) == 0 else value % size


def mixed(lane):
    return rest(lane, HI) * COPIES + over(lane, HI)


def group_of(lane):
    return over(lane, 2 * NO) * 2 + rest(over(lane, HI), 2)


def orbital_of(lane):
    return rest(lane, HI) * COPIES + rest(over(lane, 2 * HI), COPIES)


def fold_matrix():
    shape = (LANES, COPIES * LANES)
    row, col = iota(shape, 0), iota(shape, 1)
    return ones_where(row == over(col, LANES) * NO + orbital_of(rest(col, LANES)))


def row_matrix(tiles, natoms):
    size = tiles * natoms
    row, col = iota((size, size), 0), iota((size, size), 1)
    return ones_where(col == rest(row, tiles) * natoms + over(row, tiles))


def stack_tiles(flat):
    return jnp.concatenate(
        [flat[:, t : t + LANES] for t in range(0, flat.shape[1], LANES)], axis=0
    )


def dot(left, right):
    return jnp.dot(left, right, preferred_element_type=jnp.float32)


def make_planes(block, planes, at, order, factor=None):
    count = block.shape[0]
    ordered = dot(order, jnp.concatenate([stack_tiles(block[e]) for e in range(count)], axis=1))
    if factor is not None:
        ordered = ordered * factor
    ordered = ordered.astype(jnp.bfloat16)
    for e in range(count):
        planes[at + e] = ordered[:, e * LANES : (e + 1) * LANES]


def tables_kernel(
    natoms, local_hbm, gradient_hbm, coupling_hbm, kernel_out, derivs_out, planes_out,
    local, gradient, coupling, rows, sems,
):
    copies = [
        pltpu.make_async_copy(coupling_hbm.at[:, 0, :], coupling, sems.at[0]),
        pltpu.make_async_copy(gradient_hbm, gradient, sems.at[1]),
        pltpu.make_async_copy(local_hbm, local, sems.at[2]),
    ]
    for copy in copies:
        copy.start()

    tiles = NO * NO // LANES
    block = natoms * tiles
    cells = ND * ND * NB
    depth = rows.shape[2]
    width = -(-NS * cells // LANES) * LANES
    fold = fold_matrix()
    order = row_matrix(tiles, natoms)
    lane = iota((width, 2 * LANES), 1)
    branch = over(lane, LANES) * COPIES + group_of(rest(lane, LANES))
    lane = iota((width, 2 * LANES), 0) - branch * cells
    widen = ones_where((lane >= 0) & (lane < cells) & (branch < NS))
    line, lane = iota((NB * depth, width), 0), iota((NB * depth, width), 1)
    lane = lane - (rest(line, depth) * NB + over(line, depth))
    chosen = lane == 0
    for s in range(1, NS):
        chosen = chosen | (lane == s * cells)

    copies[0].wait()
    table = jnp.transpose(coupling[...])
    table = jnp.concatenate(
        [table, jnp.zeros((natoms, width - NS * cells), jnp.float32)], axis=1
    )
    lefts = [
        jnp.where(chosen, table[atom : atom + 1, :], 0.0).astype(jnp.bfloat16)
        for atom in range(natoms)
    ]
    wide = dot(jnp.concatenate(lefts, axis=0), widen)
    for at in range(natoms * NB):
        for half in range(2):
            rows[at, half] = wide[
                at * depth : (at + 1) * depth, half * LANES : (half + 1) * LANES
            ]

    copies[1].wait()
    flats = [stack_tiles(gradient[slot, j]) for slot in range(NB) for j in range(ND)]
    ordered = dot(order, jnp.concatenate(flats, axis=1)).astype(jnp.bfloat16)
    stacked = [ordered[:, at : at + LANES] for at in range(0, NB * ND * LANES, LANES)]
    wide = dot(jnp.concatenate(stacked, axis=0), fold)
    for slot in range(NB):
        for j in range(ND):
            for atom in range(natoms):
                at = (slot * ND + j) * block + atom * tiles
                derivs_out[atom * NB + slot, j * NO : (j + 1) * NO, :] = jnp.concatenate(
                    [
                        wide[at : at + tiles, q * LANES : (q + 1) * LANES]
                        for q in range(COPIES)
                    ],
                    axis=0,
                ).astype(jnp.bfloat16)

    copies[2].wait()
    make_planes(local, planes_out, 0, row_matrix(2 * tiles, natoms))

    def one_cell(at, carry):
        derivs = [derivs_out[at, j * NO : (j + 1) * NO, :] for j in range(ND)]
        for i in range(ND):
            for half in range(2):
                total = None
                for j in range(ND):
                    row = rows[at, half, ND * i + j : ND * i + j + 1, :]
                    weight = jnp.broadcast_to(row, (NO, LANES)).astype(jnp.bfloat16)
                    term = derivs[j] * weight
                    total = term if total is None else total + term
                kernel_out[at, i * NO : (i + 1) * NO, half * LANES : (half + 1) * LANES] = total
        return carry

    lax.fori_loop(0, natoms * NB, one_cell, 0, unroll=4)


def tables(local, gradient, coupling):
    energies, natoms, size = local.shape
    count = NB * natoms
    return pl.pallas_call(
        functools.partial(tables_kernel, natoms),
        out_shape=(
            jax.ShapeDtypeStruct((count, ND * NO, 2 * LANES), jnp.bfloat16),
            jax.ShapeDtypeStruct((count, ND * NO, LANES), jnp.bfloat16),
            jax.ShapeDtypeStruct((energies, natoms * size // LANES, LANES), jnp.bfloat16),
        ),
        in_specs=[pl.BlockSpec(memory_space=pltpu.HBM)] * 3,
        out_specs=[pl.BlockSpec(memory_space=pltpu.VMEM)] * 3,
        scratch_shapes=[
            pltpu.VMEM(local.shape, local.dtype),
            pltpu.VMEM(gradient.shape, gradient.dtype),
            pltpu.VMEM((coupling.shape[0], natoms), jnp.float32),
            pltpu.VMEM((count, 2, 2 * HI, LANES), jnp.float32),
            pltpu.SemaphoreType.DMA((3,)),
        ],
        compiler_params=pltpu.CompilerParams(vmem_limit_bytes=VMEM_LIMIT),
        cost_estimate=pl.CostEstimate(
            flops=200_000_000, bytes_accessed=6_000_000, transcendentals=0
        ),
        name="tables",
    )(in_hbm(local), in_hbm(gradient), in_hbm(coupling))


def partner(index, step, size):
    return index ^ step if size & (size - 1) == 0 else (index + step) % size


def share_terms(atoms, groups, block_of, kernel, derivs):
    tiles = groups * HI // 2
    lane_group = group_of(iota((NO, LANES), 1))
    masks = [ones_where(lane_group == g) for g in range(COPIES)]
    group = over(iota((NO, LANES), 1), NO)
    row_group = over(iota((HI, LANES), 1), NO)
    spans = -(-NB * ND // COPIES)

    def middles(k):
        blocked = []
        for slot in range(NB):
            wide = lax.dot_general(
                block_of(k, slot), kernel[atoms[k] * NB + slot], NT,
                preferred_element_type=jnp.float32,
            )
            wide = jnp.concatenate(
                [wide, jnp.zeros((groups * NO, LANES - ND * NO), jnp.float32)], axis=1
            )
            rows = []
            for g in range(groups):
                starts = [((g // 2) * COPIES + q) * tiles + (g % 2) * HI for q in range(COPIES)]
                rows.append(jnp.concatenate([wide[at : at + HI] for at in starts], axis=0))
            turned = []
            for d in range(COPIES):
                total = rows[-d % COPIES]
                for lane in range(1, COPIES):
                    total = jnp.where(group == lane, rows[(lane - d) % COPIES], total)
                turned.append(pltpu.roll(total, (COPIES - d) * NO, axis=1) if d else total)
            for i in range(ND):
                total = turned[i]
                for g in range(1, groups):
                    total = jnp.where(group == g, turned[(i - g) % COPIES], total)
                blocked.append(total)
        blocked.extend([jnp.zeros((NO, LANES), jnp.float32)] * (spans * COPIES - len(blocked)))
        pieces = []
        for span in range(spans):
            for u in range(COPIES // 2):
                for q in range(COPIES):
                    for v in range(2):
                        pieces.append(
                            blocked[span * COPIES + 2 * u + v][q * HI : (q + 1) * HI]
                        )
        return jnp.concatenate(pieces, axis=0).astype(jnp.bfloat16)

    def sigmas(k, right):
        left = []
        for span in range(spans):
            total = None
            for g in range(COPIES):
                pair = span * COPIES + g
                if pair < NB * ND:
                    at = (pair % ND) * NO
                    part = derivs[atoms[k] * NB + pair // ND, at : at + NO, :] * masks[g]
                    total = part if total is None else total + part
            left.append(total)
        own = dot(jnp.concatenate(left, axis=1), right)
        rows = [own[q * HI : (q + 1) * HI, :] for q in range(COPIES)]
        placed = []
        for g in range(groups):
            total = None
            for q in range(COPIES):
                shift = (q - g) % COPIES * NO
                part = pltpu.roll(rows[q], shift, axis=1) if shift else rows[q]
                total = part if total is None else jnp.where(row_group == q, part, total)
            placed.append(total)
        return placed

    rights = [middles(k) for k in range(len(atoms))]
    placed = []
    for k, right in enumerate(rights):
        placed.extend(sigmas(k, right))
    row, col = iota((LANES, LANES), 0), iota((LANES, LANES), 1)
    unmix = ones_where(col == (row - rest(row, NO)) + mixed(rest(row, NO)))
    return dot(jnp.concatenate(placed, axis=0).astype(jnp.bfloat16), unmix)


def sandwich_kernel(
    count, natoms, shares, neighbours_hbm, offsets_hbm, middle_planes,
    near_even, far_odd, far_even, near_odd, kernel, derivs, *refs,
):
    early = 1
    late = shares - early
    outs, late_blocks = refs[:late], refs[late]
    neighbours, offsets, planes, blocks, results, sems = refs[late + 1 :]
    copies = [
        pltpu.make_async_copy(neighbours_hbm, neighbours, sems.at[0]),
        pltpu.make_async_copy(offsets_hbm, offsets, sems.at[1]),
    ]
    for copy in copies:
        copy.start()

    tiles = 2 * NO * NO // LANES
    groups = 2 * count
    order = row_matrix(tiles, natoms)
    place, length = lax.axis_index("energy"), lax.axis_size("energy")
    for ref, reach, odd in (
        (near_even, 1, 0), (far_odd, 2, 1), (far_even, 2, 0), (near_odd, 1, 1)
    ):
        other = neighbour(place, reach, odd)
        exists = ((other >= 0) & (other < length)).astype(jnp.float32)
        make_planes(ref, planes, (2 + other - place) * count, order, exists)
    planes[2 * count : 3 * count] = middle_planes[...]

    fold = fold_matrix()
    group = group_of(rest(iota(fold.shape, 1), LANES))
    places = [fold * ones_where(group == g) for g in range(COPIES)]
    for copy in copies:
        copy.wait()
    for half in range(2):
        branches = range(half * COPIES, min(NS, (half + 1) * COPIES))
        shifted_planes = [
            jnp.concatenate(
                [
                    planes[2 * count + e - (1 - 2 * (s % 2)) * offsets[s // 2]]
                    for e in range(count)
                ],
                axis=0,
            )
            for s in branches
        ]
        wide = dot(
            jnp.concatenate(shifted_planes, axis=1),
            jnp.concatenate(places[: len(branches)], axis=0),
        ).astype(jnp.bfloat16)
        for e in range(count):
            for atom in range(natoms):
                for q in range(COPIES):
                    at = (e * COPIES + q) * tiles
                    start = (e * natoms + atom) * tiles
                    blocks[atom, at : at + tiles, half * LANES : (half + 1) * LANES] = wide[
                        start : start + tiles, q * LANES : (q + 1) * LANES
                    ]

    me = lax.axis_index("mom")
    share = natoms // shares
    for step in range(early):
        first = partner(me, step, shares) * share
        for k in range(share):
            for slot in range(NB):
                late_blocks[(step * share + k) * NB + slot] = blocks[neighbours[slot, first + k]]

    def one_share(step, carry):
        first = partner(me, step, shares) * share
        atoms = [first + k for k in range(share)]
        results[step] = share_terms(
            atoms, groups, lambda k, slot: blocks[neighbours[slot, atoms[k]]], kernel, derivs
        ).astype(jnp.bfloat16)
        return carry

    lax.fori_loop(early, shares, one_share, 0)
    for step in range(early, shares):
        outs[step - early][...] = results[step]


def sandwich(window, middle_planes, kernel, derivs, neighbours, offsets, shares):
    count, natoms, size = window[0].shape
    groups = 2 * count
    share = natoms // shares
    rows = share * groups * HI
    early = 1
    late = shares - early
    return pl.pallas_call(
        functools.partial(sandwich_kernel, count, natoms, shares),
        out_shape=(jax.ShapeDtypeStruct((rows, LANES), jnp.bfloat16),) * late
        + (jax.ShapeDtypeStruct((early * share * NB, groups * NO, 2 * LANES), jnp.bfloat16),),
        in_specs=[pl.BlockSpec(memory_space=pltpu.HBM)] * 2
        + [pl.BlockSpec(memory_space=pltpu.VMEM)] * 7,
        out_specs=[pl.BlockSpec(memory_space=pltpu.VMEM)] * (late + 1),
        scratch_shapes=[
            pltpu.SMEM(neighbours.shape, jnp.int32),
            pltpu.SMEM(offsets.shape, jnp.int32),
            pltpu.VMEM((5 * count, natoms * size // LANES, LANES), jnp.bfloat16),
            pltpu.VMEM((natoms, groups * NO, 2 * LANES), jnp.bfloat16),
            pltpu.VMEM((shares, rows, LANES), jnp.bfloat16),
            pltpu.SemaphoreType.DMA((2,)),
        ],
        compiler_params=pltpu.CompilerParams(vmem_limit_bytes=VMEM_LIMIT),
        cost_estimate=pl.CostEstimate(
            flops=800_000_000, bytes_accessed=7_000_000, transcendentals=0
        ),
        name="sandwich",
    )(
        in_hbm(neighbours), in_hbm(offsets),
        middle_planes, *window, kernel, derivs,
    )


def chip_kernel(groups, shares, blocks, kernel, derivs, own, *outs):
    me = lax.axis_index("mom")
    share = blocks.shape[0] // (NB * (1 + len(outs)))
    for step, out in enumerate((own, *outs)):
        first = partner(me, step, shares) * share
        out[...] = share_terms(
            [first + k for k in range(share)], groups,
            lambda k, slot: blocks[(step * share + k) * NB + slot], kernel, derivs,
        ).astype(out.dtype)


def chip_shares(blocks, kernel, derivs, shares):
    early = 1
    groups = blocks.shape[1] // NO
    rows = blocks.shape[0] // (NB * early) * groups * HI
    return pl.pallas_call(
        functools.partial(chip_kernel, groups, shares),
        out_shape=(jax.ShapeDtypeStruct((rows, LANES), jnp.float32),)
        + (jax.ShapeDtypeStruct((rows, LANES), jnp.bfloat16),) * (early - 1),
        in_specs=[pl.BlockSpec(memory_space=pltpu.VMEM)] * 3,
        out_specs=[pl.BlockSpec(memory_space=pltpu.VMEM)] * early,
        compiler_params=pltpu.CompilerParams(vmem_limit_bytes=VMEM_LIMIT),
        cost_estimate=pl.CostEstimate(
            flops=400_000_000, bytes_accessed=4_000_000, transcendentals=0
        ),
        name="chip_shares",
    )(blocks, kernel, derivs)


def combine_kernel(own, *refs):
    parts, out, total = refs[:-2], refs[-2], refs[-1]
    count, share, width = out.shape
    tiles = width // LANES
    summed = own[...]
    for part in parts:
        summed = summed + part[...].astype(jnp.float32)
    total[...] = summed
    for e in range(count):
        for t in range(tiles):
            out[e, :, t * LANES : (t + 1) * LANES] = total[
                pl.ds(e * tiles + t, share, stride=count * tiles), :
            ]


def combine(own, parts, count, share):
    return pl.pallas_call(
        combine_kernel,
        out_shape=jax.ShapeDtypeStruct((count, share, 2 * NO * NO), jnp.float32),
        in_specs=[pl.BlockSpec(memory_space=pltpu.VMEM)] * (1 + len(parts)),
        out_specs=pl.BlockSpec(memory_space=pltpu.VMEM),
        scratch_shapes=[pltpu.VMEM(own.shape, jnp.float32)],
        compiler_params=pltpu.CompilerParams(vmem_limit_bytes=VMEM_LIMIT),
        name="combine",
    )(own, *parts)


def neighbour(index, reach, odd):
    return ((index + odd * reach) ^ reach) - odd * reach


def exchanged(array, reach, odd):
    energies, momenta = lax.axis_size("energy"), lax.axis_size("mom")
    pairs = []
    for i in range(energies):
        other = neighbour(i, reach, odd)
        for k in range(momenta):
            if 0 <= other < energies:
                target = other * momenta + k
            else:
                target = i * momenta + (k ^ 1 if momenta & 1 == 0 else k)
            pairs.append((i * momenta + k, target))
    return lax.ppermute(array, ("energy", "mom"), pairs)


def body(green, coupling, gradient, neighbours, offsets):
    local = green[0]
    count, natoms, _ = local.shape
    shares = lax.axis_size("mom")
    remote = (
        exchanged(local, 1, 0),
        exchanged(local, 2, 1),
        exchanged(local, 2, 0),
        exchanged(local, 1, 1),
    )
    kernel, derivs, planes = tables(local, gradient, coupling.reshape(-1, 1, coupling.shape[-1]))
    *late, blocks = sandwich(remote, planes, kernel, derivs, neighbours.T, offsets, shares)

    def sent(term, step):
        pairs = [(i, partner(i, step, shares)) for i in range(shares)]
        return lax.ppermute(term, "mom", pairs)

    steps = [*range(shares // 2, shares), *range(1, shares // 2)]
    parts = [sent(late[step - 1], step) for step in steps]
    (own,) = chip_shares(blocks, kernel, derivs, shares)
    return combine(own, parts, count, natoms // shares)


def solution(mesh):
    in_specs = (P("mom", "energy", None, None), P("mom", None, None, None, None), P(), P(), P())
    out_specs = P("energy", "mom", None)
    return jax.shard_map(body, mesh=mesh, in_specs=in_specs, out_specs=out_specs, check_vma=False)
```

```python
import functools

import jax
import jax.numpy as jnp
from jax import lax
from jax.experimental import pallas as pl
from jax.experimental.pallas import tpu as pltpu
from jax.sharding import PartitionSpec as P

NO = 32
NB = 5
NW = 3
NS = 2 * NW
ND = 3
LANES = 128
COPIES = LANES // NO
HI = NO // COPIES
VMEM_LIMIT = 40 * 1024 * 1024

NT = (((1,), (1,)), ((), ()))


def in_hbm(array):
    return pltpu.with_memory_space_constraint(array, pltpu.HBM)


def iota(shape, dim):
    return lax.broadcasted_iota(jnp.int32, shape, dim)


def ones_where(condition):
    return jnp.where(condition, 1.0, 0.0).astype(jnp.bfloat16)


def over(value, size):
    return value >> (size.bit_length() - 1) if size & (size - 1) == 0 else value // size


def rest(value, size):
    return value & (size - 1) if size & (size - 1) == 0 else value % size


def mixed(lane):
    return rest(lane, HI) * COPIES + over(lane, HI)


def group_of(lane):
    return over(lane, 2 * NO) * 2 + rest(over(lane, HI), 2)


def orbital_of(lane):
    return rest(lane, HI) * COPIES + rest(over(lane, 2 * HI), COPIES)


def fold_matrix():
    shape = (LANES, COPIES * LANES)
    row, col = iota(shape, 0), iota(shape, 1)
    return ones_where(row == over(col, LANES) * NO + orbital_of(rest(col, LANES)))


def row_matrix(tiles, natoms):
    size = tiles * natoms
    row, col = iota((size, size), 0), iota((size, size), 1)
    return ones_where(col == rest(row, tiles) * natoms + over(row, tiles))


def stack_tiles(flat):
    return jnp.concatenate(
        [flat[:, t : t + LANES] for t in range(0, flat.shape[1], LANES)], axis=0
    )


def dot(left, right):
    return jnp.dot(left, right, preferred_element_type=jnp.float32)


def make_planes(block, planes, at, order, factor=None):
    count = block.shape[0]
    ordered = dot(order, jnp.concatenate([stack_tiles(block[e]) for e in range(count)], axis=1))
    if factor is not None:
        ordered = ordered * factor
    ordered = ordered.astype(jnp.bfloat16)
    for e in range(count):
        planes[at + e] = ordered[:, e * LANES : (e + 1) * LANES]


def tables_kernel(
    natoms, local_hbm, gradient_hbm, coupling_hbm, kernel_out, derivs_out, planes_out,
    local, gradient, coupling, rows, sems,
):
    copies = [
        pltpu.make_async_copy(coupling_hbm.at[:, 0, :], coupling, sems.at[0]),
        pltpu.make_async_copy(gradient_hbm, gradient, sems.at[1]),
        pltpu.make_async_copy(local_hbm, local, sems.at[2]),
    ]
    for copy in copies:
        copy.start()

    tiles = NO * NO // LANES
    block = natoms * tiles
    cells = ND * ND * NB
    depth = rows.shape[2]
    width = -(-NS * cells // LANES) * LANES
    fold = fold_matrix()
    order = row_matrix(tiles, natoms)
    lane = iota((width, 2 * LANES), 1)
    branch = over(lane, LANES) * COPIES + group_of(rest(lane, LANES))
    lane = iota((width, 2 * LANES), 0) - branch * cells
    widen = ones_where((lane >= 0) & (lane < cells) & (branch < NS))
    line, lane = iota((NB * depth, width), 0), iota((NB * depth, width), 1)
    lane = lane - (rest(line, depth) * NB + over(line, depth))
    chosen = lane == 0
    for s in range(1, NS):
        chosen = chosen | (lane == s * cells)

    copies[0].wait()
    table = jnp.transpose(coupling[...])
    table = jnp.concatenate(
        [table, jnp.zeros((natoms, width - NS * cells), jnp.float32)], axis=1
    )
    lefts = [
        jnp.where(chosen, table[atom : atom + 1, :], 0.0).astype(jnp.bfloat16)
        for atom in range(natoms)
    ]
    wide = dot(jnp.concatenate(lefts, axis=0), widen)
    for at in range(natoms * NB):
        for half in range(2):
            rows[at, half] = wide[
                at * depth : (at + 1) * depth, half * LANES : (half + 1) * LANES
            ]

    copies[1].wait()
    flats = [stack_tiles(gradient[slot, j]) for slot in range(NB) for j in range(ND)]
    ordered = dot(order, jnp.concatenate(flats, axis=1)).astype(jnp.bfloat16)
    stacked = [ordered[:, at : at + LANES] for at in range(0, NB * ND * LANES, LANES)]
    wide = dot(jnp.concatenate(stacked, axis=0), fold)
    for slot in range(NB):
        for j in range(ND):
            for atom in range(natoms):
                at = (slot * ND + j) * block + atom * tiles
                derivs_out[atom * NB + slot, j * NO : (j + 1) * NO, :] = jnp.concatenate(
                    [
                        wide[at : at + tiles, q * LANES : (q + 1) * LANES]
                        for q in range(COPIES)
                    ],
                    axis=0,
                ).astype(jnp.bfloat16)

    copies[2].wait()
    make_planes(local, planes_out, 0, row_matrix(2 * tiles, natoms))

    def one_cell(at, carry):
        derivs = [derivs_out[at, j * NO : (j + 1) * NO, :] for j in range(ND)]
        for i in range(ND):
            for half in range(2):
                total = None
                for j in range(ND):
                    row = rows[at, half, ND * i + j : ND * i + j + 1, :]
                    weight = jnp.broadcast_to(row, (NO, LANES)).astype(jnp.bfloat16)
                    term = derivs[j] * weight
                    total = term if total is None else total + term
                kernel_out[at, i * NO : (i + 1) * NO, half * LANES : (half + 1) * LANES] = total
        return carry

    lax.fori_loop(0, natoms * NB, one_cell, 0, unroll=4)


def tables(local, gradient, coupling):
    energies, natoms, size = local.shape
    count = NB * natoms
    return pl.pallas_call(
        functools.partial(tables_kernel, natoms),
        out_shape=(
            jax.ShapeDtypeStruct((count, ND * NO, 2 * LANES), jnp.bfloat16),
            jax.ShapeDtypeStruct((count, ND * NO, LANES), jnp.bfloat16),
            jax.ShapeDtypeStruct((energies, natoms * size // LANES, LANES), jnp.bfloat16),
        ),
        in_specs=[pl.BlockSpec(memory_space=pltpu.HBM)] * 3,
        out_specs=[pl.BlockSpec(memory_space=pltpu.VMEM)] * 3,
        scratch_shapes=[
            pltpu.VMEM(local.shape, local.dtype),
            pltpu.VMEM(gradient.shape, gradient.dtype),
            pltpu.VMEM((coupling.shape[0], natoms), jnp.float32),
            pltpu.VMEM((count, 2, 2 * HI, LANES), jnp.float32),
            pltpu.SemaphoreType.DMA((3,)),
        ],
        compiler_params=pltpu.CompilerParams(vmem_limit_bytes=VMEM_LIMIT),
        cost_estimate=pl.CostEstimate(
            flops=200_000_000, bytes_accessed=6_000_000, transcendentals=0
        ),
        name="tables",
    )(in_hbm(local), in_hbm(gradient), in_hbm(coupling))


def partner(index, step, size):
    return index ^ step if size & (size - 1) == 0 else (index + step) % size


def share_terms(atoms, groups, block_of, kernel, derivs):
    tiles = groups * HI // 2
    lane_group = group_of(iota((NO, LANES), 1))
    masks = [ones_where(lane_group == g) for g in range(COPIES)]
    group = over(iota((NO, LANES), 1), NO)
    row_group = over(iota((HI, LANES), 1), NO)
    spans = -(-NB * ND // COPIES)

    def middles(k):
        blocked = []
        for slot in range(NB):
            wide = lax.dot_general(
                block_of(k, slot), kernel[atoms[k] * NB + slot], NT,
                preferred_element_type=jnp.float32,
            )
            wide = jnp.concatenate(
                [wide, jnp.zeros((groups * NO, LANES - ND * NO), jnp.float32)], axis=1
            )
            rows = []
            for g in range(groups):
                starts = [((g // 2) * COPIES + q) * tiles + (g % 2) * HI for q in range(COPIES)]
                rows.append(jnp.concatenate([wide[at : at + HI] for at in starts], axis=0))
            turned = []
            for d in range(COPIES):
                total = rows[-d % COPIES]
                for lane in range(1, COPIES):
                    total = jnp.where(group == lane, rows[(lane - d) % COPIES], total)
                turned.append(pltpu.roll(total, (COPIES - d) * NO, axis=1) if d else total)
            for i in range(ND):
                total = turned[i]
                for g in range(1, groups):
                    total = jnp.where(group == g, turned[(i - g) % COPIES], total)
                blocked.append(total)
        blocked.extend([jnp.zeros((NO, LANES), jnp.float32)] * (spans * COPIES - len(blocked)))
        pieces = []
        for span in range(spans):
            for u in range(COPIES // 2):
                for q in range(COPIES):
                    for v in range(2):
                        pieces.append(
                            blocked[span * COPIES + 2 * u + v][q * HI : (q + 1) * HI]
                        )
        return jnp.concatenate(pieces, axis=0).astype(jnp.bfloat16)

    def sigmas(k, right):
        left = []
        for span in range(spans):
            total = None
            for g in range(COPIES):
                pair = span * COPIES + g
                if pair < NB * ND:
                    at = (pair % ND) * NO
                    part = derivs[atoms[k] * NB + pair // ND, at : at + NO, :] * masks[g]
                    total = part if total is None else total + part
            left.append(total)
        own = dot(jnp.concatenate(left, axis=1), right)
        rows = [own[q * HI : (q + 1) * HI, :] for q in range(COPIES)]
        placed = []
        for g in range(groups):
            total = None
            for q in range(COPIES):
                shift = (q - g) % COPIES * NO
                part = pltpu.roll(rows[q], shift, axis=1) if shift else rows[q]
                total = part if total is None else jnp.where(row_group == q, part, total)
            placed.append(total)
        return placed

    rights = [middles(k) for k in range(len(atoms))]
    placed = []
    for k, right in enumerate(rights):
        placed.extend(sigmas(k, right))
    row, col = iota((LANES, LANES), 0), iota((LANES, LANES), 1)
    unmix = ones_where(col == (row - rest(row, NO)) + mixed(rest(row, NO)))
    return dot(jnp.concatenate(placed, axis=0).astype(jnp.bfloat16), unmix)


def sandwich_kernel(
    count, natoms, shares, neighbours_hbm, offsets_hbm, middle_planes,
    far_odd, far_even, near_even, near_odd, kernel, derivs, *refs,
):
    early = 1
    late = shares - early
    outs, late_blocks = refs[:late], refs[late]
    neighbours, offsets, planes, blocks, results, sems = refs[late + 1 :]
    copies = [
        pltpu.make_async_copy(neighbours_hbm, neighbours, sems.at[0]),
        pltpu.make_async_copy(offsets_hbm, offsets, sems.at[1]),
    ]
    for copy in copies:
        copy.start()

    tiles = 2 * NO * NO // LANES
    groups = 2 * count
    order = row_matrix(tiles, natoms)
    place, length = lax.axis_index("energy"), lax.axis_size("energy")
    for ref, reach, odd in (
        (far_odd, 2, 1), (far_even, 2, 0), (near_even, 1, 0), (near_odd, 1, 1)
    ):
        other = neighbour(place, reach, odd)
        exists = ((other >= 0) & (other < length)).astype(jnp.float32)
        make_planes(ref, planes, (2 + other - place) * count, order, exists)
    planes[2 * count : 3 * count] = middle_planes[...]

    fold = fold_matrix()
    group = group_of(rest(iota(fold.shape, 1), LANES))
    places = [fold * ones_where(group == g) for g in range(COPIES)]
    for copy in copies:
        copy.wait()
    for half in range(2):
        branches = range(half * COPIES, min(NS, (half + 1) * COPIES))
        shifted_planes = [
            jnp.concatenate(
                [
                    planes[2 * count + e - (1 - 2 * (s % 2)) * offsets[s // 2]]
                    for e in range(count)
                ],
                axis=0,
            )
            for s in branches
        ]
        wide = dot(
            jnp.concatenate(shifted_planes, axis=1),
            jnp.concatenate(places[: len(branches)], axis=0),
        ).astype(jnp.bfloat16)
        for e in range(count):
            for atom in range(natoms):
                for q in range(COPIES):
                    at = (e * COPIES + q) * tiles
                    start = (e * natoms + atom) * tiles
                    blocks[atom, at : at + tiles, half * LANES : (half + 1) * LANES] = wide[
                        start : start + tiles, q * LANES : (q + 1) * LANES
                    ]

    me = lax.axis_index("mom")
    share = natoms // shares
    for step in range(early):
        first = partner(me, step, shares) * share
        for k in range(share):
            for slot in range(NB):
                late_blocks[(step * share + k) * NB + slot] = blocks[neighbours[slot, first + k]]

    def one_share(step, carry):
        first = partner(me, step, shares) * share
        atoms = [first + k for k in range(share)]
        results[step] = share_terms(
            atoms, groups, lambda k, slot: blocks[neighbours[slot, atoms[k]]], kernel, derivs
        ).astype(jnp.bfloat16)
        return carry

    lax.fori_loop(early, shares, one_share, 0)
    for step in range(early, shares):
        outs[step - early][...] = results[step]


def sandwich(window, middle_planes, kernel, derivs, neighbours, offsets, shares):
    count, natoms, size = window[0].shape
    groups = 2 * count
    share = natoms // shares
    rows = share * groups * HI
    early = 1
    late = shares - early
    return pl.pallas_call(
        functools.partial(sandwich_kernel, count, natoms, shares),
        out_shape=(jax.ShapeDtypeStruct((rows, LANES), jnp.bfloat16),) * late
        + (jax.ShapeDtypeStruct((early * share * NB, groups * NO, 2 * LANES), jnp.bfloat16),),
        in_specs=[pl.BlockSpec(memory_space=pltpu.HBM)] * 2
        + [pl.BlockSpec(memory_space=pltpu.VMEM)] * 7,
        out_specs=[pl.BlockSpec(memory_space=pltpu.VMEM)] * (late + 1),
        scratch_shapes=[
            pltpu.SMEM(neighbours.shape, jnp.int32),
            pltpu.SMEM(offsets.shape, jnp.int32),
            pltpu.VMEM((5 * count, natoms * size // LANES, LANES), jnp.bfloat16),
            pltpu.VMEM((natoms, groups * NO, 2 * LANES), jnp.bfloat16),
            pltpu.VMEM((shares, rows, LANES), jnp.bfloat16),
            pltpu.SemaphoreType.DMA((2,)),
        ],
        compiler_params=pltpu.CompilerParams(vmem_limit_bytes=VMEM_LIMIT),
        cost_estimate=pl.CostEstimate(
            flops=800_000_000, bytes_accessed=7_000_000, transcendentals=0
        ),
        name="sandwich",
    )(
        in_hbm(neighbours), in_hbm(offsets),
        middle_planes, *window, kernel, derivs,
    )


def chip_kernel(groups, shares, blocks, kernel, derivs, own, *outs):
    me = lax.axis_index("mom")
    share = blocks.shape[0] // (NB * (1 + len(outs)))
    for step, out in enumerate((own, *outs)):
        first = partner(me, step, shares) * share
        out[...] = share_terms(
            [first + k for k in range(share)], groups,
            lambda k, slot: blocks[(step * share + k) * NB + slot], kernel, derivs,
        ).astype(out.dtype)


def chip_shares(blocks, kernel, derivs, shares):
    early = 1
    groups = blocks.shape[1] // NO
    rows = blocks.shape[0] // (NB * early) * groups * HI
    return pl.pallas_call(
        functools.partial(chip_kernel, groups, shares),
        out_shape=(jax.ShapeDtypeStruct((rows, LANES), jnp.float32),)
        + (jax.ShapeDtypeStruct((rows, LANES), jnp.bfloat16),) * (early - 1),
        in_specs=[pl.BlockSpec(memory_space=pltpu.VMEM)] * 3,
        out_specs=[pl.BlockSpec(memory_space=pltpu.VMEM)] * early,
        compiler_params=pltpu.CompilerParams(vmem_limit_bytes=VMEM_LIMIT),
        cost_estimate=pl.CostEstimate(
            flops=400_000_000, bytes_accessed=4_000_000, transcendentals=0
        ),
        name="chip_shares",
    )(blocks, kernel, derivs)


def combine_kernel(own, *refs):
    parts, out, total = refs[:-2], refs[-2], refs[-1]
    count, share, width = out.shape
    tiles = width // LANES
    summed = own[...]
    for part in parts:
        summed = summed + part[...].astype(jnp.float32)
    total[...] = summed
    for e in range(count):
        for t in range(tiles):
            out[e, :, t * LANES : (t + 1) * LANES] = total[
                pl.ds(e * tiles + t, share, stride=count * tiles), :
            ]


def combine(own, parts, count, share):
    return pl.pallas_call(
        combine_kernel,
        out_shape=jax.ShapeDtypeStruct((count, share, 2 * NO * NO), jnp.float32),
        in_specs=[pl.BlockSpec(memory_space=pltpu.VMEM)] * (1 + len(parts)),
        out_specs=pl.BlockSpec(memory_space=pltpu.VMEM),
        scratch_shapes=[pltpu.VMEM(own.shape, jnp.float32)],
        compiler_params=pltpu.CompilerParams(vmem_limit_bytes=VMEM_LIMIT),
        name="combine",
    )(own, *parts)


def neighbour(index, reach, odd):
    return ((index + odd * reach) ^ reach) - odd * reach


def exchanged(array, reach, odd):
    energies, momenta = lax.axis_size("energy"), lax.axis_size("mom")
    pairs = []
    for i in range(energies):
        other = neighbour(i, reach, odd)
        for k in range(momenta):
            if 0 <= other < energies:
                target = other * momenta + k
            else:
                target = i * momenta + (k ^ 1 if momenta & 1 == 0 else k)
            pairs.append((i * momenta + k, target))
    return lax.ppermute(array, ("energy", "mom"), pairs)


def body(green, coupling, gradient, neighbours, offsets):
    local = green[0]
    count, natoms, _ = local.shape
    shares = lax.axis_size("mom")
    remote = (
        exchanged(local, 2, 1),
        exchanged(local, 2, 0),
        exchanged(local, 1, 0),
        exchanged(local, 1, 1),
    )
    kernel, derivs, planes = tables(local, gradient, coupling.reshape(-1, 1, coupling.shape[-1]))
    *late, blocks = sandwich(remote, planes, kernel, derivs, neighbours.T, offsets, shares)

    def sent(term, step):
        pairs = [(i, partner(i, step, shares)) for i in range(shares)]
        return lax.ppermute(term, "mom", pairs)

    parts = [sent(term, step) for step, term in enumerate(late, 1)]
    (own,) = chip_shares(blocks, kernel, derivs, shares)
    return combine(own, parts, count, natoms // shares)


def solution(mesh):
    in_specs = (P("mom", "energy", None, None), P("mom", None, None, None, None), P(), P(), P())
    out_specs = P("energy", "mom", None)
    return jax.shard_map(body, mesh=mesh, in_specs=in_specs, out_specs=out_specs, check_vma=False)
```

```python
import functools

import jax
import jax.numpy as jnp
from jax import lax
from jax.experimental import pallas as pl
from jax.experimental.pallas import tpu as pltpu
from jax.sharding import PartitionSpec as P

NO = 32
NB = 5
NW = 3
NS = 2 * NW
ND = 3
LANES = 128
COPIES = LANES // NO
HI = NO // COPIES
VMEM_LIMIT = 40 * 1024 * 1024

NT = (((1,), (1,)), ((), ()))


def in_hbm(array):
    return pltpu.with_memory_space_constraint(array, pltpu.HBM)


def iota(shape, dim):
    return lax.broadcasted_iota(jnp.int32, shape, dim)


def ones_where(condition):
    return jnp.where(condition, 1.0, 0.0).astype(jnp.bfloat16)


def over(value, size):
    return value >> (size.bit_length() - 1) if size & (size - 1) == 0 else value // size


def rest(value, size):
    return value & (size - 1) if size & (size - 1) == 0 else value % size


def mixed(lane):
    return rest(lane, HI) * COPIES + over(lane, HI)


def group_of(lane):
    return over(lane, 2 * NO) * 2 + rest(over(lane, HI), 2)


def orbital_of(lane):
    return rest(lane, HI) * COPIES + rest(over(lane, 2 * HI), COPIES)


def fold_matrix():
    shape = (LANES, COPIES * LANES)
    row, col = iota(shape, 0), iota(shape, 1)
    return ones_where(row == over(col, LANES) * NO + orbital_of(rest(col, LANES)))


def row_matrix(tiles, natoms):
    size = tiles * natoms
    row, col = iota((size, size), 0), iota((size, size), 1)
    return ones_where(col == rest(row, tiles) * natoms + over(row, tiles))


def stack_tiles(flat):
    return jnp.concatenate(
        [flat[:, t : t + LANES] for t in range(0, flat.shape[1], LANES)], axis=0
    )


def dot(left, right):
    return jnp.dot(left, right, preferred_element_type=jnp.float32)


def make_planes(block, planes, at, order, factor=None):
    count = block.shape[0]
    ordered = dot(order, jnp.concatenate([stack_tiles(block[e]) for e in range(count)], axis=1))
    if factor is not None:
        ordered = ordered * factor
    ordered = ordered.astype(jnp.bfloat16)
    for e in range(count):
        planes[at + e] = ordered[:, e * LANES : (e + 1) * LANES]


def tables_kernel(
    natoms, local_hbm, gradient_hbm, coupling_hbm, kernel_out, derivs_out, planes_out,
    local, gradient, coupling, rows, sems,
):
    copies = [
        pltpu.make_async_copy(coupling_hbm.at[:, 0, :], coupling, sems.at[0]),
        pltpu.make_async_copy(gradient_hbm, gradient, sems.at[1]),
        pltpu.make_async_copy(local_hbm, local, sems.at[2]),
    ]
    for copy in copies:
        copy.start()

    tiles = NO * NO // LANES
    block = natoms * tiles
    cells = ND * ND * NB
    depth = rows.shape[2]
    width = -(-NS * cells // LANES) * LANES
    fold = fold_matrix()
    order = row_matrix(tiles, natoms)
    lane = iota((width, 2 * LANES), 1)
    branch = over(lane, LANES) * COPIES + group_of(rest(lane, LANES))
    lane = iota((width, 2 * LANES), 0) - branch * cells
    widen = ones_where((lane >= 0) & (lane < cells) & (branch < NS))
    line, lane = iota((NB * depth, width), 0), iota((NB * depth, width), 1)
    lane = lane - (rest(line, depth) * NB + over(line, depth))
    chosen = lane == 0
    for s in range(1, NS):
        chosen = chosen | (lane == s * cells)

    copies[0].wait()
    table = jnp.transpose(coupling[...])
    table = jnp.concatenate(
        [table, jnp.zeros((natoms, width - NS * cells), jnp.float32)], axis=1
    )
    lefts = [
        jnp.where(chosen, table[atom : atom + 1, :], 0.0).astype(jnp.bfloat16)
        for atom in range(natoms)
    ]
    wide = dot(jnp.concatenate(lefts, axis=0), widen)
    for at in range(natoms * NB):
        for half in range(2):
            rows[at, half] = wide[
                at * depth : (at + 1) * depth, half * LANES : (half + 1) * LANES
            ]

    copies[1].wait()
    flats = [stack_tiles(gradient[slot, j]) for slot in range(NB) for j in range(ND)]
    ordered = dot(order, jnp.concatenate(flats, axis=1)).astype(jnp.bfloat16)
    stacked = [ordered[:, at : at + LANES] for at in range(0, NB * ND * LANES, LANES)]
    wide = dot(jnp.concatenate(stacked, axis=0), fold)
    for slot in range(NB):
        for j in range(ND):
            for atom in range(natoms):
                at = (slot * ND + j) * block + atom * tiles
                derivs_out[atom * NB + slot, j * NO : (j + 1) * NO, :] = jnp.concatenate(
                    [
                        wide[at : at + tiles, q * LANES : (q + 1) * LANES]
                        for q in range(COPIES)
                    ],
                    axis=0,
                ).astype(jnp.bfloat16)

    copies[2].wait()
    make_planes(local, planes_out, 0, row_matrix(2 * tiles, natoms))

    def one_cell(at, carry):
        derivs = [derivs_out[at, j * NO : (j + 1) * NO, :] for j in range(ND)]
        for i in range(ND):
            for half in range(2):
                total = None
                for j in range(ND):
                    row = rows[at, half, ND * i + j : ND * i + j + 1, :]
                    weight = jnp.broadcast_to(row, (NO, LANES)).astype(jnp.bfloat16)
                    term = derivs[j] * weight
                    total = term if total is None else total + term
                kernel_out[at, i * NO : (i + 1) * NO, half * LANES : (half + 1) * LANES] = total
        return carry

    lax.fori_loop(0, natoms * NB, one_cell, 0, unroll=16)


def tables(local, gradient, coupling):
    energies, natoms, size = local.shape
    count = NB * natoms
    return pl.pallas_call(
        functools.partial(tables_kernel, natoms),
        out_shape=(
            jax.ShapeDtypeStruct((count, ND * NO, 2 * LANES), jnp.bfloat16),
            jax.ShapeDtypeStruct((count, ND * NO, LANES), jnp.bfloat16),
            jax.ShapeDtypeStruct((energies, natoms * size // LANES, LANES), jnp.bfloat16),
        ),
        in_specs=[pl.BlockSpec(memory_space=pltpu.HBM)] * 3,
        out_specs=[pl.BlockSpec(memory_space=pltpu.VMEM)] * 3,
        scratch_shapes=[
            pltpu.VMEM(local.shape, local.dtype),
            pltpu.VMEM(gradient.shape, gradient.dtype),
            pltpu.VMEM((coupling.shape[0], natoms), jnp.float32),
            pltpu.VMEM((count, 2, 2 * HI, LANES), jnp.float32),
            pltpu.SemaphoreType.DMA((3,)),
        ],
        compiler_params=pltpu.CompilerParams(vmem_limit_bytes=VMEM_LIMIT),
        cost_estimate=pl.CostEstimate(
            flops=200_000_000, bytes_accessed=6_000_000, transcendentals=0
        ),
        name="tables",
    )(in_hbm(local), in_hbm(gradient), in_hbm(coupling))


def partner(index, step, size):
    return index ^ step if size & (size - 1) == 0 else (index + step) % size


def share_terms(atoms, groups, block_of, kernel, derivs):
    tiles = groups * HI // 2
    lane_group = group_of(iota((NO, LANES), 1))
    masks = [ones_where(lane_group == g) for g in range(COPIES)]
    group = over(iota((NO, LANES), 1), NO)
    row_group = over(iota((HI, LANES), 1), NO)
    spans = -(-NB * ND // COPIES)

    def middles(k):
        blocked = []
        for slot in range(NB):
            wide = lax.dot_general(
                block_of(k, slot), kernel[atoms[k] * NB + slot], NT,
                preferred_element_type=jnp.float32,
            )
            wide = jnp.concatenate(
                [wide, jnp.zeros((groups * NO, LANES - ND * NO), jnp.float32)], axis=1
            )
            rows = []
            for g in range(groups):
                starts = [((g // 2) * COPIES + q) * tiles + (g % 2) * HI for q in range(COPIES)]
                rows.append(jnp.concatenate([wide[at : at + HI] for at in starts], axis=0))
            turned = []
            for d in range(COPIES):
                total = rows[-d % COPIES]
                for lane in range(1, COPIES):
                    total = jnp.where(group == lane, rows[(lane - d) % COPIES], total)
                turned.append(pltpu.roll(total, (COPIES - d) * NO, axis=1) if d else total)
            for i in range(ND):
                total = turned[i]
                for g in range(1, groups):
                    total = jnp.where(group == g, turned[(i - g) % COPIES], total)
                blocked.append(total)
        blocked.extend([jnp.zeros((NO, LANES), jnp.float32)] * (spans * COPIES - len(blocked)))
        pieces = []
        for span in range(spans):
            for u in range(COPIES // 2):
                for q in range(COPIES):
                    for v in range(2):
                        pieces.append(
                            blocked[span * COPIES + 2 * u + v][q * HI : (q + 1) * HI]
                        )
        return jnp.concatenate(pieces, axis=0).astype(jnp.bfloat16)

    def sigmas(k, right):
        left = []
        for span in range(spans):
            total = None
            for g in range(COPIES):
                pair = span * COPIES + g
                if pair < NB * ND:
                    at = (pair % ND) * NO
                    part = derivs[atoms[k] * NB + pair // ND, at : at + NO, :] * masks[g]
                    total = part if total is None else total + part
            left.append(total)
        own = dot(jnp.concatenate(left, axis=1), right)
        rows = [own[q * HI : (q + 1) * HI, :] for q in range(COPIES)]
        placed = []
        for g in range(groups):
            total = None
            for q in range(COPIES):
                shift = (q - g) % COPIES * NO
                part = pltpu.roll(rows[q], shift, axis=1) if shift else rows[q]
                total = part if total is None else jnp.where(row_group == q, part, total)
            placed.append(total)
        return placed

    rights = [middles(k) for k in range(len(atoms))]
    placed = []
    for k, right in enumerate(rights):
        placed.extend(sigmas(k, right))
    row, col = iota((LANES, LANES), 0), iota((LANES, LANES), 1)
    unmix = ones_where(col == (row - rest(row, NO)) + mixed(rest(row, NO)))
    return dot(jnp.concatenate(placed, axis=0).astype(jnp.bfloat16), unmix)


def sandwich_kernel(
    count, natoms, shares, neighbours_hbm, offsets_hbm, middle_planes,
    near_even, far_odd, far_even, near_odd, kernel, derivs, *refs,
):
    early = 1
    late = shares - early
    outs, late_blocks = refs[:late], refs[late]
    neighbours, offsets, planes, blocks, results, sems = refs[late + 1 :]
    copies = [
        pltpu.make_async_copy(neighbours_hbm, neighbours, sems.at[0]),
        pltpu.make_async_copy(offsets_hbm, offsets, sems.at[1]),
    ]
    for copy in copies:
        copy.start()

    tiles = 2 * NO * NO // LANES
    groups = 2 * count
    order = row_matrix(tiles, natoms)
    place, length = lax.axis_index("energy"), lax.axis_size("energy")
    for ref, reach, odd in (
        (near_even, 1, 0), (far_odd, 2, 1), (far_even, 2, 0), (near_odd, 1, 1)
    ):
        other = neighbour(place, reach, odd)
        exists = ((other >= 0) & (other < length)).astype(jnp.float32)
        make_planes(ref, planes, (2 + other - place) * count, order, exists)
    planes[2 * count : 3 * count] = middle_planes[...]

    fold = fold_matrix()
    group = group_of(rest(iota(fold.shape, 1), LANES))
    places = [fold * ones_where(group == g) for g in range(COPIES)]
    for copy in copies:
        copy.wait()
    for half in range(2):
        branches = range(half * COPIES, min(NS, (half + 1) * COPIES))
        shifted_planes = [
            jnp.concatenate(
                [
                    planes[2 * count + e - (1 - 2 * (s % 2)) * offsets[s // 2]]
                    for e in range(count)
                ],
                axis=0,
            )
            for s in branches
        ]
        wide = dot(
            jnp.concatenate(shifted_planes, axis=1),
            jnp.concatenate(places[: len(branches)], axis=0),
        ).astype(jnp.bfloat16)
        for e in range(count):
            for atom in range(natoms):
                for q in range(COPIES):
                    at = (e * COPIES + q) * tiles
                    start = (e * natoms + atom) * tiles
                    blocks[atom, at : at + tiles, half * LANES : (half + 1) * LANES] = wide[
                        start : start + tiles, q * LANES : (q + 1) * LANES
                    ]

    me = lax.axis_index("mom")
    share = natoms // shares
    for step in range(early):
        first = partner(me, step, shares) * share
        for k in range(share):
            for slot in range(NB):
                late_blocks[(step * share + k) * NB + slot] = blocks[neighbours[slot, first + k]]

    def one_share(step, carry):
        first = partner(me, step, shares) * share
        atoms = [first + k for k in range(share)]
        results[step] = share_terms(
            atoms, groups, lambda k, slot: blocks[neighbours[slot, atoms[k]]], kernel, derivs
        ).astype(jnp.bfloat16)
        return carry

    lax.fori_loop(early, shares, one_share, 0)
    for step in range(early, shares):
        outs[step - early][...] = results[step]


def sandwich(window, middle_planes, kernel, derivs, neighbours, offsets, shares):
    count, natoms, size = window[0].shape
    groups = 2 * count
    share = natoms // shares
    rows = share * groups * HI
    early = 1
    late = shares - early
    return pl.pallas_call(
        functools.partial(sandwich_kernel, count, natoms, shares),
        out_shape=(jax.ShapeDtypeStruct((rows, LANES), jnp.bfloat16),) * late
        + (jax.ShapeDtypeStruct((early * share * NB, groups * NO, 2 * LANES), jnp.bfloat16),),
        in_specs=[pl.BlockSpec(memory_space=pltpu.HBM)] * 2
        + [pl.BlockSpec(memory_space=pltpu.VMEM)] * 7,
        out_specs=[pl.BlockSpec(memory_space=pltpu.VMEM)] * (late + 1),
        scratch_shapes=[
            pltpu.SMEM(neighbours.shape, jnp.int32),
            pltpu.SMEM(offsets.shape, jnp.int32),
            pltpu.VMEM((5 * count, natoms * size // LANES, LANES), jnp.bfloat16),
            pltpu.VMEM((natoms, groups * NO, 2 * LANES), jnp.bfloat16),
            pltpu.VMEM((shares, rows, LANES), jnp.bfloat16),
            pltpu.SemaphoreType.DMA((2,)),
        ],
        compiler_params=pltpu.CompilerParams(vmem_limit_bytes=VMEM_LIMIT),
        cost_estimate=pl.CostEstimate(
            flops=800_000_000, bytes_accessed=7_000_000, transcendentals=0
        ),
        name="sandwich",
    )(
        in_hbm(neighbours), in_hbm(offsets),
        middle_planes, *window, kernel, derivs,
    )


def chip_kernel(groups, shares, blocks, kernel, derivs, own, *outs):
    me = lax.axis_index("mom")
    share = blocks.shape[0] // (NB * (1 + len(outs)))
    for step, out in enumerate((own, *outs)):
        first = partner(me, step, shares) * share
        out[...] = share_terms(
            [first + k for k in range(share)], groups,
            lambda k, slot: blocks[(step * share + k) * NB + slot], kernel, derivs,
        ).astype(out.dtype)


def chip_shares(blocks, kernel, derivs, shares):
    early = 1
    groups = blocks.shape[1] // NO
    rows = blocks.shape[0] // (NB * early) * groups * HI
    return pl.pallas_call(
        functools.partial(chip_kernel, groups, shares),
        out_shape=(jax.ShapeDtypeStruct((rows, LANES), jnp.float32),)
        + (jax.ShapeDtypeStruct((rows, LANES), jnp.bfloat16),) * (early - 1),
        in_specs=[pl.BlockSpec(memory_space=pltpu.VMEM)] * 3,
        out_specs=[pl.BlockSpec(memory_space=pltpu.VMEM)] * early,
        compiler_params=pltpu.CompilerParams(vmem_limit_bytes=VMEM_LIMIT),
        cost_estimate=pl.CostEstimate(
            flops=400_000_000, bytes_accessed=4_000_000, transcendentals=0
        ),
        name="chip_shares",
    )(blocks, kernel, derivs)


def combine_kernel(own, *refs):
    parts, out, total = refs[:-2], refs[-2], refs[-1]
    count, share, width = out.shape
    tiles = width // LANES
    summed = own[...]
    for part in parts:
        summed = summed + part[...].astype(jnp.float32)
    total[...] = summed
    for e in range(count):
        for t in range(tiles):
            out[e, :, t * LANES : (t + 1) * LANES] = total[
                pl.ds(e * tiles + t, share, stride=count * tiles), :
            ]


def combine(own, parts, count, share):
    return pl.pallas_call(
        combine_kernel,
        out_shape=jax.ShapeDtypeStruct((count, share, 2 * NO * NO), jnp.float32),
        in_specs=[pl.BlockSpec(memory_space=pltpu.VMEM)] * (1 + len(parts)),
        out_specs=pl.BlockSpec(memory_space=pltpu.VMEM),
        scratch_shapes=[pltpu.VMEM(own.shape, jnp.float32)],
        compiler_params=pltpu.CompilerParams(vmem_limit_bytes=VMEM_LIMIT),
        name="combine",
    )(own, *parts)


def neighbour(index, reach, odd):
    return ((index + odd * reach) ^ reach) - odd * reach


def exchanged(array, reach, odd):
    energies, momenta = lax.axis_size("energy"), lax.axis_size("mom")
    pairs = []
    for i in range(energies):
        other = neighbour(i, reach, odd)
        for k in range(momenta):
            if 0 <= other < energies:
                target = other * momenta + k
            else:
                target = i * momenta + (k ^ 1 if momenta & 1 == 0 else k)
            pairs.append((i * momenta + k, target))
    return lax.ppermute(array, ("energy", "mom"), pairs)


def body(green, coupling, gradient, neighbours, offsets):
    local = green[0]
    count, natoms, _ = local.shape
    shares = lax.axis_size("mom")
    remote = (
        exchanged(local, 1, 0),
        exchanged(local, 2, 1),
        exchanged(local, 2, 0),
        exchanged(local, 1, 1),
    )
    kernel, derivs, planes = tables(local, gradient, coupling.reshape(-1, 1, coupling.shape[-1]))
    *late, blocks = sandwich(remote, planes, kernel, derivs, neighbours.T, offsets, shares)

    def sent(term, step):
        pairs = [(i, partner(i, step, shares)) for i in range(shares)]
        return lax.ppermute(term, "mom", pairs)

    steps = [*range(shares // 2, shares), *range(1, shares // 2)]
    parts = [sent(late[step - 1], step) for step in steps]
    (own,) = chip_shares(blocks, kernel, derivs, shares)
    return combine(own, parts, count, natoms // shares)


def solution(mesh):
    in_specs = (P("mom", "energy", None, None), P("mom", None, None, None, None), P(), P(), P())
    out_specs = P("energy", "mom", None)
    return jax.shard_map(body, mesh=mesh, in_specs=in_specs, out_specs=out_specs, check_vma=False)
```

```python
import functools

import jax
import jax.numpy as jnp
from jax import lax
from jax.experimental import pallas as pl
from jax.experimental.pallas import tpu as pltpu
from jax.sharding import PartitionSpec as P

NO = 32
NB = 5
NW = 3
NS = 2 * NW
ND = 3
LANES = 128
COPIES = LANES // NO
HI = NO // COPIES
VMEM_LIMIT = 40 * 1024 * 1024

NT = (((1,), (1,)), ((), ()))


def in_hbm(array):
    return pltpu.with_memory_space_constraint(array, pltpu.HBM)


def iota(shape, dim):
    return lax.broadcasted_iota(jnp.int32, shape, dim)


def ones_where(condition):
    return jnp.where(condition, 1.0, 0.0).astype(jnp.bfloat16)


def over(value, size):
    return value >> (size.bit_length() - 1) if size & (size - 1) == 0 else value // size


def rest(value, size):
    return value & (size - 1) if size & (size - 1) == 0 else value % size


def mixed(lane):
    return rest(lane, HI) * COPIES + over(lane, HI)


def group_of(lane):
    return over(lane, 2 * NO) * 2 + rest(over(lane, HI), 2)


def orbital_of(lane):
    return rest(lane, HI) * COPIES + rest(over(lane, 2 * HI), COPIES)


def fold_matrix():
    shape = (LANES, COPIES * LANES)
    row, col = iota(shape, 0), iota(shape, 1)
    return ones_where(row == over(col, LANES) * NO + orbital_of(rest(col, LANES)))


def row_matrix(tiles, natoms):
    size = tiles * natoms
    row, col = iota((size, size), 0), iota((size, size), 1)
    return ones_where(col == rest(row, tiles) * natoms + over(row, tiles))


def stack_tiles(flat):
    return jnp.concatenate(
        [flat[:, t : t + LANES] for t in range(0, flat.shape[1], LANES)], axis=0
    )


def dot(left, right):
    return jnp.dot(left, right, preferred_element_type=jnp.float32)


def make_planes(block, planes, at, order, factor=None):
    count = block.shape[0]
    ordered = dot(order, jnp.concatenate([stack_tiles(block[e]) for e in range(count)], axis=1))
    if factor is not None:
        ordered = ordered * factor
    ordered = ordered.astype(jnp.bfloat16)
    for e in range(count):
        planes[at + e] = ordered[:, e * LANES : (e + 1) * LANES]


def tables_kernel(
    natoms, local_hbm, gradient_hbm, coupling_hbm, kernel_out, derivs_out, planes_out,
    local, gradient, coupling, rows, sems,
):
    copies = [
        pltpu.make_async_copy(coupling_hbm.at[:, 0, :], coupling, sems.at[0]),
        pltpu.make_async_copy(gradient_hbm, gradient, sems.at[1]),
        pltpu.make_async_copy(local_hbm, local, sems.at[2]),
    ]
    for copy in copies:
        copy.start()

    tiles = NO * NO // LANES
    block = natoms * tiles
    cells = ND * ND * NB
    depth = rows.shape[2]
    width = -(-NS * cells // LANES) * LANES
    fold = fold_matrix()
    order = row_matrix(tiles, natoms)
    lane = iota((width, 2 * LANES), 1)
    branch = over(lane, LANES) * COPIES + group_of(rest(lane, LANES))
    lane = iota((width, 2 * LANES), 0) - branch * cells
    widen = ones_where((lane >= 0) & (lane < cells) & (branch < NS))
    line, lane = iota((NB * depth, width), 0), iota((NB * depth, width), 1)
    lane = lane - (rest(line, depth) * NB + over(line, depth))
    chosen = lane == 0
    for s in range(1, NS):
        chosen = chosen | (lane == s * cells)

    for copy in copies:
        copy.wait()
    table = jnp.transpose(coupling[...])
    table = jnp.concatenate(
        [table, jnp.zeros((natoms, width - NS * cells), jnp.float32)], axis=1
    )
    lefts = [
        jnp.where(chosen, table[atom : atom + 1, :], 0.0).astype(jnp.bfloat16)
        for atom in range(natoms)
    ]
    wide = dot(jnp.concatenate(lefts, axis=0), widen)
    for at in range(natoms * NB):
        for half in range(2):
            rows[at, half] = wide[
                at * depth : (at + 1) * depth, half * LANES : (half + 1) * LANES
            ]

    flats = [stack_tiles(gradient[slot, j]) for slot in range(NB) for j in range(ND)]
    ordered = dot(order, jnp.concatenate(flats, axis=1)).astype(jnp.bfloat16)
    stacked = [ordered[:, at : at + LANES] for at in range(0, NB * ND * LANES, LANES)]
    wide = dot(jnp.concatenate(stacked, axis=0), fold)
    for slot in range(NB):
        for j in range(ND):
            for atom in range(natoms):
                at = (slot * ND + j) * block + atom * tiles
                derivs_out[atom * NB + slot, j * NO : (j + 1) * NO, :] = jnp.concatenate(
                    [
                        wide[at : at + tiles, q * LANES : (q + 1) * LANES]
                        for q in range(COPIES)
                    ],
                    axis=0,
                ).astype(jnp.bfloat16)

    make_planes(local, planes_out, 0, row_matrix(2 * tiles, natoms))

    def one_cell(at, carry):
        derivs = [derivs_out[at, j * NO : (j + 1) * NO, :] for j in range(ND)]
        for i in range(ND):
            for half in range(2):
                total = None
                for j in range(ND):
                    row = rows[at, half, ND * i + j : ND * i + j + 1, :]
                    weight = jnp.broadcast_to(row, (NO, LANES)).astype(jnp.bfloat16)
                    term = derivs[j] * weight
                    total = term if total is None else total + term
                kernel_out[at, i * NO : (i + 1) * NO, half * LANES : (half + 1) * LANES] = total
        return carry

    lax.fori_loop(0, natoms * NB, one_cell, 0, unroll=4)


def tables(local, gradient, coupling):
    energies, natoms, size = local.shape
    count = NB * natoms
    return pl.pallas_call(
        functools.partial(tables_kernel, natoms),
        out_shape=(
            jax.ShapeDtypeStruct((count, ND * NO, 2 * LANES), jnp.bfloat16),
            jax.ShapeDtypeStruct((count, ND * NO, LANES), jnp.bfloat16),
            jax.ShapeDtypeStruct((energies, natoms * size // LANES, LANES), jnp.bfloat16),
        ),
        in_specs=[pl.BlockSpec(memory_space=pltpu.HBM)] * 3,
        out_specs=[pl.BlockSpec(memory_space=pltpu.VMEM)] * 3,
        scratch_shapes=[
            pltpu.VMEM(local.shape, local.dtype),
            pltpu.VMEM(gradient.shape, gradient.dtype),
            pltpu.VMEM((coupling.shape[0], natoms), jnp.float32),
            pltpu.VMEM((count, 2, 2 * HI, LANES), jnp.float32),
            pltpu.SemaphoreType.DMA((3,)),
        ],
        compiler_params=pltpu.CompilerParams(vmem_limit_bytes=VMEM_LIMIT),
        cost_estimate=pl.CostEstimate(
            flops=200_000_000, bytes_accessed=6_000_000, transcendentals=0
        ),
        name="tables",
    )(in_hbm(local), in_hbm(gradient), in_hbm(coupling))


def partner(index, step, size):
    return index ^ step if size & (size - 1) == 0 else (index + step) % size


def share_terms(atoms, groups, block_of, kernel, derivs):
    tiles = groups * HI // 2
    lane_group = group_of(iota((NO, LANES), 1))
    masks = [ones_where(lane_group == g) for g in range(COPIES)]
    group = over(iota((NO, LANES), 1), NO)
    row_group = over(iota((HI, LANES), 1), NO)
    spans = -(-NB * ND // COPIES)

    def middles(k):
        blocked = []
        for slot in range(NB):
            wide = lax.dot_general(
                block_of(k, slot), kernel[atoms[k] * NB + slot], NT,
                preferred_element_type=jnp.float32,
            )
            wide = jnp.concatenate(
                [wide, jnp.zeros((groups * NO, LANES - ND * NO), jnp.float32)], axis=1
            )
            rows = []
            for g in range(groups):
                starts = [((g // 2) * COPIES + q) * tiles + (g % 2) * HI for q in range(COPIES)]
                rows.append(jnp.concatenate([wide[at : at + HI] for at in starts], axis=0))
            turned = []
            for d in range(COPIES):
                total = rows[-d % COPIES]
                for lane in range(1, COPIES):
                    total = jnp.where(group == lane, rows[(lane - d) % COPIES], total)
                turned.append(pltpu.roll(total, (COPIES - d) * NO, axis=1) if d else total)
            for i in range(ND):
                total = turned[i]
                for g in range(1, groups):
                    total = jnp.where(group == g, turned[(i - g) % COPIES], total)
                blocked.append(total)
        blocked.extend([jnp.zeros((NO, LANES), jnp.float32)] * (spans * COPIES - len(blocked)))
        pieces = []
        for span in range(spans):
            for u in range(COPIES // 2):
                for q in range(COPIES):
                    for v in range(2):
                        pieces.append(
                            blocked[span * COPIES + 2 * u + v][q * HI : (q + 1) * HI]
                        )
        return jnp.concatenate(pieces, axis=0).astype(jnp.bfloat16)

    def sigmas(k, right):
        left = []
        for span in range(spans):
            total = None
            for g in range(COPIES):
                pair = span * COPIES + g
                if pair < NB * ND:
                    at = (pair % ND) * NO
                    part = derivs[atoms[k] * NB + pair // ND, at : at + NO, :] * masks[g]
                    total = part if total is None else total + part
            left.append(total)
        own = dot(jnp.concatenate(left, axis=1), right)
        rows = [own[q * HI : (q + 1) * HI, :] for q in range(COPIES)]
        placed = []
        for g in range(groups):
            total = None
            for q in range(COPIES):
                shift = (q - g) % COPIES * NO
                part = pltpu.roll(rows[q], shift, axis=1) if shift else rows[q]
                total = part if total is None else jnp.where(row_group == q, part, total)
            placed.append(total)
        return placed

    rights = [middles(k) for k in range(len(atoms))]
    placed = []
    for k, right in enumerate(rights):
        placed.extend(sigmas(k, right))
    row, col = iota((LANES, LANES), 0), iota((LANES, LANES), 1)
    unmix = ones_where(col == (row - rest(row, NO)) + mixed(rest(row, NO)))
    return dot(jnp.concatenate(placed, axis=0).astype(jnp.bfloat16), unmix)


def sandwich_kernel(
    count, natoms, shares, neighbours_hbm, offsets_hbm, middle_planes,
    near_even, far_odd, far_even, near_odd, kernel, derivs, *refs,
):
    early = 1
    late = shares - early
    outs, late_blocks = refs[:late], refs[late]
    neighbours, offsets, planes, blocks, results, sems = refs[late + 1 :]
    copies = [
        pltpu.make_async_copy(neighbours_hbm, neighbours, sems.at[0]),
        pltpu.make_async_copy(offsets_hbm, offsets, sems.at[1]),
    ]
    for copy in copies:
        copy.start()

    tiles = 2 * NO * NO // LANES
    groups = 2 * count
    order = row_matrix(tiles, natoms)
    place, length = lax.axis_index("energy"), lax.axis_size("energy")
    for ref, reach, odd in (
        (near_even, 1, 0), (far_odd, 2, 1), (far_even, 2, 0), (near_odd, 1, 1)
    ):
        other = neighbour(place, reach, odd)
        exists = ((other >= 0) & (other < length)).astype(jnp.float32)
        make_planes(ref, planes, (2 + other - place) * count, order, exists)
    planes[2 * count : 3 * count] = middle_planes[...]

    fold = fold_matrix()
    group = group_of(rest(iota(fold.shape, 1), LANES))
    places = [fold * ones_where(group == g) for g in range(COPIES)]
    for copy in copies:
        copy.wait()
    for half in range(2):
        branches = range(half * COPIES, min(NS, (half + 1) * COPIES))
        shifted_planes = [
            jnp.concatenate(
                [
                    planes[2 * count + e - (1 - 2 * (s % 2)) * offsets[s // 2]]
                    for e in range(count)
                ],
                axis=0,
            )
            for s in branches
        ]
        wide = dot(
            jnp.concatenate(shifted_planes, axis=1),
            jnp.concatenate(places[: len(branches)], axis=0),
        ).astype(jnp.bfloat16)
        for e in range(count):
            for atom in range(natoms):
                for q in range(COPIES):
                    at = (e * COPIES + q) * tiles
                    start = (e * natoms + atom) * tiles
                    blocks[atom, at : at + tiles, half * LANES : (half + 1) * LANES] = wide[
                        start : start + tiles, q * LANES : (q + 1) * LANES
                    ]

    me = lax.axis_index("mom")
    share = natoms // shares
    for step in range(early):
        first = partner(me, step, shares) * share
        for k in range(share):
            for slot in range(NB):
                late_blocks[(step * share + k) * NB + slot] = blocks[neighbours[slot, first + k]]

    def one_share(step, carry):
        first = partner(me, step, shares) * share
        atoms = [first + k for k in range(share)]
        results[step] = share_terms(
            atoms, groups, lambda k, slot: blocks[neighbours[slot, atoms[k]]], kernel, derivs
        ).astype(jnp.bfloat16)
        return carry

    lax.fori_loop(early, shares, one_share, 0)
    for step in range(early, shares):
        outs[step - early][...] = results[step]


def sandwich(window, middle_planes, kernel, derivs, neighbours, offsets, shares):
    count, natoms, size = window[0].shape
    groups = 2 * count
    share = natoms // shares
    rows = share * groups * HI
    early = 1
    late = shares - early
    return pl.pallas_call(
        functools.partial(sandwich_kernel, count, natoms, shares),
        out_shape=(jax.ShapeDtypeStruct((rows, LANES), jnp.bfloat16),) * late
        + (jax.ShapeDtypeStruct((early * share * NB, groups * NO, 2 * LANES), jnp.bfloat16),),
        in_specs=[pl.BlockSpec(memory_space=pltpu.HBM)] * 2
        + [pl.BlockSpec(memory_space=pltpu.VMEM)] * 7,
        out_specs=[pl.BlockSpec(memory_space=pltpu.VMEM)] * (late + 1),
        scratch_shapes=[
            pltpu.SMEM(neighbours.shape, jnp.int32),
            pltpu.SMEM(offsets.shape, jnp.int32),
            pltpu.VMEM((5 * count, natoms * size // LANES, LANES), jnp.bfloat16),
            pltpu.VMEM((natoms, groups * NO, 2 * LANES), jnp.bfloat16),
            pltpu.VMEM((shares, rows, LANES), jnp.bfloat16),
            pltpu.SemaphoreType.DMA((2,)),
        ],
        compiler_params=pltpu.CompilerParams(vmem_limit_bytes=VMEM_LIMIT),
        cost_estimate=pl.CostEstimate(
            flops=800_000_000, bytes_accessed=7_000_000, transcendentals=0
        ),
        name="sandwich",
    )(
        in_hbm(neighbours), in_hbm(offsets),
        middle_planes, *window, kernel, derivs,
    )


def chip_kernel(groups, shares, blocks, kernel, derivs, own, *outs):
    me = lax.axis_index("mom")
    share = blocks.shape[0] // (NB * (1 + len(outs)))
    for step, out in enumerate((own, *outs)):
        first = partner(me, step, shares) * share
        out[...] = share_terms(
            [first + k for k in range(share)], groups,
            lambda k, slot: blocks[(step * share + k) * NB + slot], kernel, derivs,
        ).astype(out.dtype)


def chip_shares(blocks, kernel, derivs, shares):
    early = 1
    groups = blocks.shape[1] // NO
    rows = blocks.shape[0] // (NB * early) * groups * HI
    return pl.pallas_call(
        functools.partial(chip_kernel, groups, shares),
        out_shape=(jax.ShapeDtypeStruct((rows, LANES), jnp.float32),)
        + (jax.ShapeDtypeStruct((rows, LANES), jnp.bfloat16),) * (early - 1),
        in_specs=[pl.BlockSpec(memory_space=pltpu.VMEM)] * 3,
        out_specs=[pl.BlockSpec(memory_space=pltpu.VMEM)] * early,
        compiler_params=pltpu.CompilerParams(vmem_limit_bytes=VMEM_LIMIT),
        cost_estimate=pl.CostEstimate(
            flops=400_000_000, bytes_accessed=4_000_000, transcendentals=0
        ),
        name="chip_shares",
    )(blocks, kernel, derivs)


def combine_kernel(own, *refs):
    parts, out, total = refs[:-2], refs[-2], refs[-1]
    count, share, width = out.shape
    tiles = width // LANES
    summed = own[...]
    for part in parts:
        summed = summed + part[...].astype(jnp.float32)
    total[...] = summed
    for e in range(count):
        for t in range(tiles):
            out[e, :, t * LANES : (t + 1) * LANES] = total[
                pl.ds(e * tiles + t, share, stride=count * tiles), :
            ]


def combine(own, parts, count, share):
    return pl.pallas_call(
        combine_kernel,
        out_shape=jax.ShapeDtypeStruct((count, share, 2 * NO * NO), jnp.float32),
        in_specs=[pl.BlockSpec(memory_space=pltpu.VMEM)] * (1 + len(parts)),
        out_specs=pl.BlockSpec(memory_space=pltpu.VMEM),
        scratch_shapes=[pltpu.VMEM(own.shape, jnp.float32)],
        compiler_params=pltpu.CompilerParams(vmem_limit_bytes=VMEM_LIMIT),
        name="combine",
    )(own, *parts)


def neighbour(index, reach, odd):
    return ((index + odd * reach) ^ reach) - odd * reach


def exchanged(array, reach, odd):
    energies, momenta = lax.axis_size("energy"), lax.axis_size("mom")
    pairs = []
    for i in range(energies):
        other = neighbour(i, reach, odd)
        for k in range(momenta):
            if 0 <= other < energies:
                target = other * momenta + k
            else:
                target = i * momenta + (k ^ 1 if momenta & 1 == 0 else k)
            pairs.append((i * momenta + k, target))
    return lax.ppermute(array, ("energy", "mom"), pairs)


def body(green, coupling, gradient, neighbours, offsets):
    local = green[0]
    count, natoms, _ = local.shape
    shares = lax.axis_size("mom")
    remote = (
        exchanged(local, 1, 0),
        exchanged(local, 2, 1),
        exchanged(local, 2, 0),
        exchanged(local, 1, 1),
    )
    kernel, derivs, planes = tables(local, gradient, coupling.reshape(-1, 1, coupling.shape[-1]))
    *late, blocks = sandwich(remote, planes, kernel, derivs, neighbours.T, offsets, shares)

    def sent(term, step):
        pairs = [(i, partner(i, step, shares)) for i in range(shares)]
        return lax.ppermute(term, "mom", pairs)

    steps = [*range(shares // 2, shares), *range(1, shares // 2)]
    parts = [sent(late[step - 1], step) for step in steps]
    (own,) = chip_shares(blocks, kernel, derivs, shares)
    return combine(own, parts, count, natoms // shares)


def solution(mesh):
    in_specs = (P("mom", "energy", None, None), P("mom", None, None, None, None), P(), P(), P())
    out_specs = P("energy", "mom", None)
    return jax.shard_map(body, mesh=mesh, in_specs=in_specs, out_specs=out_specs, check_vma=False)
```
